512 devices in a mesh: row: 16 (over y, x), col: 32 (over z, core).
Axes of the slice: x: 4, y: 4, z: 16, core: 2. Of those that a mesh axis runs over, the one named last changes fastest.
Arguments:
- tokens: bfloat16 [192, 12288], P('col', 'row'), may hold values from -6 to 6
- w_in: bfloat16 [12288, 49152], P('row', 'col'), may hold values from -0.0546875 to 0.0546875
- w_out: bfloat16 [49152, 12288], P('col', 'row'), may hold values from -0.02734375 to 0.02734375
- grad_out: bfloat16 [192, 12288], P('col', 'row'), may hold values from -6 to 6
Outputs:
- mixed: bfloat16 [192, 12288], P('col', 'row')
- grad_in: bfloat16 [192, 12288], P('col', 'row')
The draws below stay inside these ranges and needn't reach their ends.
All inputs are finite; a program needn't handle non-finite values.
Results may differ from the reference program's by a relative error of at most 0.0049.
Values may be sent and summed in bfloat16 or wider, within the bound.
A program may use at most 64 MiB of HBM per device.

```python
import jax
import jax.numpy as jnp
from jax import lax

D = 12288
FF = 49152
TOKENS = 192


def block_scale(key, extent, cuts, least, high):
    gain, own = 1.0, jax.random.fold_in(key, 6)
    for axis_at, parts in cuts:
        draws = jnp.exp(jax.random.uniform(jax.random.fold_in(own, axis_at), (parts,), jnp.float32, least / len(cuts), high / len(cuts)))
        gain = gain * jnp.repeat(draws, extent[axis_at] // parts).reshape([-1 if axis == axis_at else 1 for axis in range(len(extent))])
    return gain


def noise(stream_key, shape, spread, reach, cuts=(), held_as=jnp.bfloat16):
    factor_of = block_scale(stream_key, shape, cuts, -0.22, 0.18) if cuts else 1.0
    drawn = jax.random.normal(stream_key, shape, jnp.float32) * spread * factor_of
    return jnp.minimum(jnp.maximum(drawn, -reach), reach).astype(held_as)


def setup_inputs(seed: int = 0) -> dict:
    keys = jax.random.split(jax.random.key(seed), 5)
    tokens = noise(keys[0], (TOKENS, D), 1.0, 6.0, ((0, 32), (1, 16)))
    w_in = noise(keys[1], (D, FF), D ** -0.5, 0.0546875, ((0, 16), (1, 32)))
    w_out = noise(keys[2], (FF, D), FF ** -0.5, 0.02734375, ((0, 32), (1, 16)))
    grad_out = noise(keys[3], (TOKENS, D), 1.0, 6.0, ((0, 32), (1, 16)))
    return {"tokens": tokens, "w_in": w_in, "w_out": w_out, "grad_out": grad_out}


gelu_scale = 0.7978845608028654
cubic_coef = 0.044715


def gelu_tanh(values):
    inner = gelu_scale * (values + cubic_coef * values * values * values)
    return 0.5 * values * (1.0 + jnp.tanh(inner))


def gelu_slope(values):
    squared = values * values
    bent = jnp.tanh(gelu_scale * (values + cubic_coef * squared * values))
    return 0.5 * (1.0 + bent) + 0.5 * values * (1.0 - bent * bent) * gelu_scale * (1.0 + 3.0 * cubic_coef * squared)


def reference(tokens, w_in, w_out, grad_out):
    hidden = jnp.dot(tokens, w_in, preferred_element_type=jnp.float32)
    activated = gelu_tanh(hidden).astype(jnp.bfloat16)
    mixed = jnp.dot(activated, w_out, preferred_element_type=jnp.float32).astype(jnp.bfloat16)
    grad_act = lax.dot_general(grad_out, w_out, (((1,), (1,)), ((), ())), preferred_element_type=jnp.float32)
    grad_hidden = (grad_act * gelu_slope(hidden)).astype(jnp.bfloat16)
    grad_in = lax.dot_general(grad_hidden, w_in, (((1,), (1,)), ((), ())), preferred_element_type=jnp.float32)
    return mixed, grad_in.astype(jnp.bfloat16)
```

```python
import jax
import jax.numpy as jnp
from jax import lax
from jax.experimental import pallas as pl
from jax.experimental.pallas import tpu as pltpu
from jax.sharding import PartitionSpec as P

gelu_scale = 0.7978845608028654
cubic_coef = 0.044715

F32, BF16 = jnp.float32, jnp.bfloat16
MESH = pl.DeviceIdType.MESH
NEAR, FAR = (1, -1, 2, -2), (2, -2, 6, -6)


def gelu_and_slope(values):
    squared = values * values
    bent = jnp.tanh(gelu_scale * (values + cubic_coef * squared * values))
    act = 0.5 * values * (1.0 + bent)
    slope = 0.5 * (1.0 + bent) + 0.5 * values * (1.0 - bent * bent) * gelu_scale * (
        1.0 + 3.0 * cubic_coef * squared
    )
    return act, slope


def against(left, right):
    return lax.dot_general(left, right, (((1,), (1,)), ((), ())), preferred_element_type=F32)


class Chain:
    def __init__(self, refs):
        (self.own, self.gathered, self.x, self.part, self.send1, self.relay, self.near1,
         self.total, self.send2, self.recv2, self.all, self.acc, self.blocks, self.sendz,
         self.nearz, self.nearz2, self.sendf, self.recvf) = refs


def chain_scratch(half, width):
    block = (48, half)
    return [
        pltpu.VMEM((16, half), BF16),
        pltpu.VMEM((16, 16, half), BF16),
        pltpu.VMEM((96, width), BF16),
        pltpu.VMEM((4, 4) + block, F32),
        pltpu.VMEM((4, 4) + block, BF16),
        pltpu.VMEM((2, 2) + block, BF16),
        pltpu.VMEM((2, 4) + block, BF16),
        pltpu.VMEM((4,) + block, F32),
        pltpu.VMEM((4,) + block, BF16),
        pltpu.VMEM((3,) + block, BF16),
        pltpu.VMEM((4, 4) + block, BF16),
        pltpu.VMEM((128, width), F32),
        pltpu.VMEM((16, 16, half), F32),
        pltpu.VMEM((16, 16, half), BF16),
        pltpu.VMEM((2, 4, 16, half), BF16),
        pltpu.VMEM((4, 16, half), BF16),
        pltpu.VMEM((4, 16, half), BF16),
        pltpu.VMEM((4, 16, half), BF16),
    ]


CHAIN_REFS = 18
COPIES = 96


def kernel(tok_ref, win_ref, wout_ref, gout_ref, mixed_ref, gin_ref, *scratch):
    win, wout, padded, slope_ref = scratch[:4]
    h = Chain(scratch[4:4 + CHAIN_REFS])
    g = Chain(scratch[4 + CHAIN_REFS:4 + 2 * CHAIN_REFS])
    local_sem, send_sem, recv_sem = scratch[4 + 2 * CHAIN_REFS:]
    width = tok_ref.shape[1]
    half = width // 2

    row, col = lax.axis_index("row"), lax.axis_index("col")
    y, x = lax.div(row, 4), lax.rem(row, 4)
    z, core = lax.div(col, 2), lax.rem(col, 2)

    def at_x(step):
        return (y * 4 + lax.rem(x + step + 4, 4), col)

    def at_y(step):
        return (lax.rem(y + step + 4, 4) * 4 + x, col)

    def at_z(step):
        return (row, lax.rem(z + step + 16, 16) * 2 + core)

    other_core = (row, z * 2 + 1 - core)

    local = []
    for part in range(2):
        cut = pl.ds(part * width, width)
        for src, dst in ((win_ref.at[:, cut], win), (wout_ref.at[cut, :], wout)):
            copy = pltpu.make_async_copy(src, dst.at[2 * core + part], local_sem.at[len(local)])
            copy.start()
            local.append(copy)

    partners = [other_core]
    partners += [at_x(step) for step in (1, -1, 2)]
    partners += [at_y(step) for step in (1, -1, 2)]
    partners += [at_z(step) for step in (1, -1, 2, -2, 6, -6)]
    barrier = pltpu.get_barrier_semaphore()
    for partner in partners:
        pl.semaphore_signal(barrier, inc=1, device_id=partner, device_id_type=MESH)

    def pack(ref, own):
        padded[...] = jnp.zeros_like(padded)
        padded[0:6, :] = ref[...].astype(F32)
        whole = padded[...]
        own[...] = jnp.concatenate([whole[:, :half], whole[:, half:]], axis=0).astype(BF16)

    pack(tok_ref, h.own)
    pack(gout_ref, g.own)

    pl.semaphore_wait(barrier, len(partners))

    started = []

    def send(src, dst, device):
        n = len(started)
        copy = pltpu.make_async_remote_copy(
            src_ref=src, dst_ref=dst, send_sem=send_sem.at[n], recv_sem=recv_sem.at[n],
            device_id=device, device_id_type=MESH,
        )
        copy.start()
        started.append(copy)
        return copy

    def arrived(copies):
        for copy in copies:
            copy.wait_recv()

    slot = lax.rem(z, 4) * 4 + lax.div(z, 4)
    held = lax.rem(z + 2, 4) * 4

    def gather_far(c):
        return [send(c.own, c.gathered.at[slot], at_z(step)) for step in FAR]

    def gather_near(c):
        out = []
        for step, first, count in ((1, 0, 4), (-1, 0, 4), (2, 0, 2), (-2, 2, 2)):
            piece = c.gathered.at[pl.ds(held + first, count)]
            out.append(send(piece, piece, at_z(step)))
        return out

    far_h = gather_far(h)
    far_g = gather_far(g)
    pushed = []
    for src_ref, dst in ((win_ref, win), (wout_ref, wout)):
        for part in range(2):
            cut = pl.ds(part * width, width)
            src = src_ref.at[:, cut] if dst is win else src_ref.at[cut, :]
            pushed.append(send(src, dst.at[2 * core + part], other_core))
    arrived(far_h)
    near_h = gather_near(h)
    arrived(far_g)
    near_g = gather_near(g)

    def squeeze(c):
        blocks = c.gathered[...].astype(F32)
        left = blocks[:, :8, :].reshape(128, half)
        right = blocks[:, 8:, :].reshape(128, half)
        spread = jnp.concatenate([left, right], axis=1).astype(BF16)
        at = lax.broadcasted_iota(jnp.int32, (96, 128), 0)
        come = lax.broadcasted_iota(jnp.int32, (96, 128), 1)
        within = come & 7
        pick = jnp.where((within < 6) & (at == 6 * (come >> 3) + within), 1.0, 0.0).astype(BF16)
        c.x[...] = jnp.dot(pick, spread, preferred_element_type=F32).astype(BF16)

    def expander():
        at = lax.broadcasted_iota(jnp.int32, (128, 96), 0)
        come = lax.broadcasted_iota(jnp.int32, (128, 96), 1)
        within = at & 7
        return jnp.where((within < 6) & (come == 6 * (at >> 3) + within), 1.0, 0.0).astype(BF16)

    def quarters(value):
        return [
            value[48 * up:48 * up + 48, half * side:half * side + half]
            for up in range(2) for side in range(2)
        ]

    def relays(c, ahead):
        c.send1[2] = c.part[2].astype(BF16)
        return [
            send(c.send1.at[2, pl.ds(0, 2)], c.relay.at[0], ahead(1)),
            send(c.send1.at[2, pl.ds(2, 2)], c.relay.at[1], ahead(-1)),
        ]

    def direct_up(c, ahead):
        c.send1[1, 2:4] = c.part[1, 2:4].astype(BF16)
        return [send(c.send1.at[1, pl.ds(2, 2)], c.near1.at[0, pl.ds(2, 2)], ahead(1))]

    def direct_down(c, ahead):
        c.send1[3, 0:2] = c.part[3, 0:2].astype(BF16)
        return [send(c.send1.at[3, pl.ds(0, 2)], c.near1.at[1, pl.ds(0, 2)], ahead(-1))]

    def passed_on(c, got, ahead):
        arrived(got[:1])
        c.send1[1, 0:2] = (c.part[1, 0:2] + c.relay[0].astype(F32)).astype(BF16)
        out = [send(c.send1.at[1, pl.ds(0, 2)], c.near1.at[0, pl.ds(0, 2)], ahead(1))]
        arrived(got[1:])
        c.send1[3, 2:4] = (c.part[3, 2:4] + c.relay[1].astype(F32)).astype(BF16)
        out.append(send(c.send1.at[3, pl.ds(2, 2)], c.near1.at[1, pl.ds(2, 2)], ahead(-1)))
        return out

    def second_sum(c, got, ahead, place):
        arrived(got)
        c.total[...] = c.part[0] + c.near1[0].astype(F32) + c.near1[1].astype(F32)
        c.send2[...] = c.total[...].astype(BF16)
        out = []
        for n, step in enumerate((2, 1, -1)):
            there = lax.rem(place + step + 4, 4)
            out.append(send(c.send2.at[there], c.recv2.at[n], ahead(step)))
        return out

    def summed(c, got, place):
        arrived(got)
        return (
            c.total[place] + c.recv2[0].astype(F32) + c.recv2[1].astype(F32) + c.recv2[2].astype(F32)
        )

    arrived(near_h)
    squeeze(h)
    for copy in (local[0], local[2]):
        copy.wait()
    arrived(pushed[:2])

    def hidden_part(rel):
        got = jnp.dot(h.x[...], win[lax.rem(x + rel, 4)], preferred_element_type=F32)
        for v, piece in enumerate(quarters(got)):
            h.part[rel, v] = piece

    hidden_part(2)
    relay_h = relays(h, at_x)
    hidden_part(1)
    direct_h = direct_up(h, at_x)
    hidden_part(3)
    direct_h += direct_down(h, at_x)
    hidden_part(0)

    arrived(near_g)
    squeeze(g)
    for copy in (local[1], local[3]):
        copy.wait()
    arrived(pushed[2:])

    direct_h += passed_on(h, relay_h, at_x)

    def grad_part(u, carry):
        got = against(g.x[...], wout[u])
        for v, piece in enumerate(quarters(got)):
            g.part[lax.rem(v - y + 4, 4), u] = piece
        return carry

    lax.fori_loop(0, 4, grad_part, 0)
    relay_g = relays(g, at_y)
    direct_g = direct_up(g, at_y) + direct_down(g, at_y)

    second_h = second_sum(h, direct_h, at_y, y)
    direct_g += passed_on(g, relay_g, at_y)
    hidden = summed(h, second_h, y)
    act, slope = gelu_and_slope(hidden)
    slope_ref[...] = slope
    h.all[x, y] = act.astype(BF16)

    def spread_first(c, chunk, place, ahead):
        piece = c.all.at[chunk, place]
        return [send(piece, piece, ahead(step)) for step in (2, 1, -1)]

    def spread_second(c, got, chunk, ahead):
        arrived(got)
        low, high = c.all.at[chunk, pl.ds(0, 2)], c.all.at[chunk, pl.ds(2, 2)]
        return [
            send(low, low, ahead(1)),
            send(high, high, ahead(-1)),
            send(high, high, ahead(1)),
            send(low, low, ahead(-1)),
        ]

    def spread_third(c, got, place, ahead):
        arrived(got[:1])
        piece = c.all.at[lax.rem(place + 3, 4), pl.ds(0, 2)]
        out = [send(piece, piece, ahead(1))]
        arrived(got[1:2])
        piece = c.all.at[lax.rem(place + 1, 4), pl.ds(2, 2)]
        out.append(send(piece, piece, ahead(-1)))
        return out

    first_h = spread_first(h, x, y, at_y)
    second_g = second_sum(g, direct_g, at_x, x)
    spread_h = spread_second(h, first_h, x, at_x)
    grad_act = summed(g, second_g, x)
    g.all[y, x] = (grad_act * slope_ref[...]).astype(BF16)
    first_g = spread_first(g, y, x, at_x)

    expand = expander()

    def widened(blocks):
        rows = [jnp.concatenate([blocks[2 * up], blocks[2 * up + 1]], axis=1) for up in range(2)]
        return jnp.dot(
            expand, jnp.concatenate(rows, axis=0), preferred_element_type=F32
        ).astype(BF16)

    def mixed_part(rel):
        u = lax.rem(x + rel, 4)
        return jnp.dot(widened(h.all[u]), wout[u], preferred_element_type=F32)

    h.acc[...] = mixed_part(0)
    spread_h2 = spread_third(h, spread_h, x, at_x)
    spread_g = spread_second(g, first_g, y, at_y)
    arrived(spread_h[2:])
    h.acc[...] += mixed_part(1)
    h.acc[...] += mixed_part(3)
    spread_g2 = spread_third(g, spread_g, y, at_y)
    arrived(spread_h2)
    h.acc[...] += mixed_part(2)

    def to_near(c):
        acc = c.acc[...]
        left = acc[:, :half].reshape(16, 8, half)
        right = acc[:, half:].reshape(16, 8, half)
        blocks = jnp.concatenate([left, right], axis=1)
        c.blocks[...] = blocks
        c.sendz[...] = blocks.astype(BF16)
        up = c.sendz.at[pl.ds(lax.rem(z + 3, 4) * 4, 4)]
        down = c.sendz.at[pl.ds(lax.rem(z + 1, 4) * 4, 4)]
        here = lax.rem(z, 4) * 4
        return [
            send(c.sendz.at[pl.ds(here, 2)], c.nearz2.at[pl.ds(0, 2)], at_z(2)),
            send(c.sendz.at[pl.ds(here + 2, 2)], c.nearz2.at[pl.ds(2, 2)], at_z(-2)),
            send(up, c.nearz.at[0], at_z(1)),
            send(down, c.nearz.at[1], at_z(-1)),
        ]

    def to_far(c, got):
        arrived(got)
        total = c.blocks[pl.ds(held, 4)] + c.nearz[0].astype(F32)
        total = total + c.nearz[1].astype(F32) + c.nearz2[...].astype(F32)
        c.sendf[...] = total.astype(BF16)
        out = []
        for n, step in enumerate(FAR):
            there = lax.div(lax.rem(z + step + 16, 16), 4)
            out.append(send(c.sendf.at[there], c.recvf.at[n], at_z(step)))
        return out

    def finish(c, got, out_ref):
        arrived(got)
        total = c.recvf[0].astype(F32) + c.recvf[1].astype(F32)
        total = total + c.recvf[2].astype(F32) + c.recvf[3].astype(F32)
        whole = jnp.concatenate([total[:8], total[8:]], axis=1)
        out_ref[...] = whole[:6].astype(BF16)

    near_h = to_near(h)

    arrived(spread_g[2:])
    arrived(spread_g2)
    g.acc[...] = jnp.zeros_like(g.acc)

    def grad_in_part(u, carry):
        blocks = [g.all[v, u] for v in range(4)]
        g.acc[...] += against(widened(blocks), win[u])
        return carry

    lax.fori_loop(0, 4, grad_in_part, 0)
    near_g = to_near(g)
    far_h = to_far(h, near_h)
    far_g = to_far(g, near_g)
    finish(h, far_h, mixed_ref)
    finish(g, far_g, gin_ref)

    for copy in started:
        copy.wait_send()


def shards(tokens, w_in, w_out, grad_out):
    rows, width = tokens.shape
    half = width // 2
    out = jax.ShapeDtypeStruct((rows, width), BF16)
    vmem = pl.BlockSpec(memory_space=pltpu.VMEM)
    hbm = pl.BlockSpec(memory_space=pl.ANY)
    return pl.pallas_call(
        kernel,
        out_shape=(out, out),
        in_specs=[vmem, hbm, hbm, vmem],
        out_specs=(vmem, vmem),
        scratch_shapes=[
            pltpu.VMEM((4, width, width), BF16),
            pltpu.VMEM((4, width, width), BF16),
            pltpu.VMEM((8, width), F32),
            pltpu.VMEM((48, half), F32),
        ]
        + chain_scratch(half, width)
        + chain_scratch(half, width)
        + [
            pltpu.SemaphoreType.DMA((4,)),
            pltpu.SemaphoreType.DMA((COPIES,)),
            pltpu.SemaphoreType.DMA((COPIES,)),
        ],
        compiler_params=pltpu.CompilerParams(
            collective_id=0, has_side_effects=True, vmem_limit_bytes=48 * 1024 * 1024
        ),
        cost_estimate=pl.CostEstimate(
            flops=8 * 192 * width * w_in.shape[1], bytes_accessed=4 * w_in.size, transcendentals=0
        ),
    )(tokens, w_in, w_out, grad_out)


def solution(mesh):
    placed = (P("col", "row"), P("row", "col"), P("col", "row"), P("col", "row"))
    return jax.shard_map(
        shards,
        mesh=mesh,
        in_specs=placed,
        out_specs=(P("col", "row"), P("col", "row")),
        check_vma=False,
    )
```

```python
import jax
import jax.numpy as jnp
from jax import lax
from jax.experimental import pallas as pl
from jax.experimental.pallas import tpu as pltpu
from jax.sharding import PartitionSpec as P

gelu_scale = 0.7978845608028654
cubic_coef = 0.044715

F32, BF16 = jnp.float32, jnp.bfloat16
MESH = pl.DeviceIdType.MESH
NEAR, FAR = (1, -1, 2, -2), (2, -2, 6, -6)


def gelu_and_slope(values):
    squared = values * values
    bent = jnp.tanh(gelu_scale * (values + cubic_coef * squared * values))
    act = 0.5 * values * (1.0 + bent)
    slope = 0.5 * (1.0 + bent) + 0.5 * values * (1.0 - bent * bent) * gelu_scale * (
        1.0 + 3.0 * cubic_coef * squared
    )
    return act, slope


def against(left, right):
    return lax.dot_general(left, right, (((1,), (1,)), ((), ())), preferred_element_type=F32)


class Chain:
    def __init__(self, refs):
        (self.own, self.gathered, self.x, self.part, self.send1, self.relay, self.near1,
         self.total, self.send2, self.recv2, self.all, self.acc, self.blocks, self.sendz,
         self.nearz, self.nearz2, self.sendf, self.recvf, self.swap, self.raw) = refs


def chain_scratch(half, width):
    block = (48, half)
    return [
        pltpu.VMEM((16, half), BF16),
        pltpu.VMEM((2, 16, 16, half), BF16),
        pltpu.VMEM((192, width), BF16),
        pltpu.VMEM((4, 4) + block, F32),
        pltpu.VMEM((4, 4) + block, BF16),
        pltpu.VMEM((2, 2) + block, BF16),
        pltpu.VMEM((2, 4) + block, BF16),
        pltpu.VMEM((4,) + block, F32),
        pltpu.VMEM((4,) + block, BF16),
        pltpu.VMEM((3,) + block, BF16),
        pltpu.VMEM((4, 4) + block, BF16),
        pltpu.VMEM((2, 128, width), F32),
        pltpu.VMEM((2, 16, 16, half), F32),
        pltpu.VMEM((16, 16, half), BF16),
        pltpu.VMEM((2, 4, 16, half), BF16),
        pltpu.VMEM((4, 16, half), BF16),
        pltpu.VMEM((4, 16, half), BF16),
        pltpu.VMEM((4, 16, half), BF16),
        pltpu.VMEM((16, 16, half), F32),
        pltpu.VMEM((6, width), BF16),
    ]


CHAIN_REFS = 20
COPIES = 96


def kernel(tok_ref, win_ref, wout_ref, gout_ref, mixed_ref, gin_ref, *scratch):
    win, wout, padded, slope_ref = scratch[:4]
    h = Chain(scratch[4:4 + CHAIN_REFS])
    g = Chain(scratch[4 + CHAIN_REFS:4 + 2 * CHAIN_REFS])
    local_sem, send_sem, recv_sem = scratch[4 + 2 * CHAIN_REFS:]
    width = tok_ref.shape[1]
    hid = wout_ref.shape[0] // 4
    half = width // 2

    row, col = lax.axis_index("row"), lax.axis_index("col")
    y, x = lax.div(row, 4), lax.rem(row, 4)
    z, core = lax.div(col, 2), lax.rem(col, 2)

    def at_x(step):
        return (y * 4 + lax.rem(x + step + 4, 4), col)

    def at_y(step):
        return (lax.rem(y + step + 4, 4) * 4 + x, col)

    def at_z(step):
        return (row, lax.rem(z + step + 16, 16) * 2 + core)

    other_core = (row, z * 2 + 1 - core)

    local = [
        pltpu.make_async_copy(src, dst, local_sem.at[n])
        for n, (src, dst) in enumerate(
            ((tok_ref, h.raw), (gout_ref, g.raw), (win_ref, win), (wout_ref, wout))
        )
    ]
    for copy in local:
        copy.start()

    partners = [other_core]
    partners += [at_x(step) for step in (1, -1, 2)]
    partners += [at_y(step) for step in (1, -1, 2)]
    partners += [at_z(step) for step in (1, -1, 2, -2, 6, -6)]
    barrier = pltpu.get_barrier_semaphore()
    for partner in partners:
        pl.semaphore_signal(barrier, inc=1, device_id=partner, device_id_type=MESH)

    def pack(ref, own):
        padded[...] = jnp.zeros_like(padded)
        padded[0:6, :] = ref[...].astype(F32)
        whole = padded[...]
        own[...] = jnp.concatenate([whole[:, :half], whole[:, half:]], axis=0).astype(BF16)

    local[0].wait()
    pack(h.raw, h.own)
    local[1].wait()
    pack(g.raw, g.own)

    pl.semaphore_wait(barrier, len(partners))

    started = []

    def send(src, dst, device):
        n = len(started)
        copy = pltpu.make_async_remote_copy(
            src_ref=src, dst_ref=dst, send_sem=send_sem.at[n], recv_sem=recv_sem.at[n],
            device_id=device, device_id_type=MESH,
        )
        copy.start()
        started.append(copy)
        return copy

    def arrived(copies):
        for copy in copies:
            copy.wait_recv()

    slot = lax.rem(z, 4) * 4 + lax.div(z, 4)
    held = lax.rem(z + 2, 4) * 4

    def gather_far(c):
        return [send(c.own, c.gathered.at[core, slot], at_z(step)) for step in FAR]

    def gather_near(c):
        out = []
        for step, first, count in ((1, 0, 4), (-1, 0, 4), (2, 0, 2), (-2, 2, 2)):
            piece = c.gathered.at[core, pl.ds(held + first, count)]
            out.append(send(piece, piece, at_z(step)))
        return out

    def across(c, first):
        piece = c.gathered.at[core, pl.ds(first, 4)]
        return send(piece, piece, other_core)

    def share(c, got):
        out = []
        for copies, first in ((got[:1], z + 1), (got[1:2], z + 3), (got[2:], z)):
            arrived(copies)
            out.append(across(c, lax.rem(first, 4) * 4))
        return out

    far_h = gather_far(h)
    far_g = gather_far(g)
    arrived(far_h)
    near_h = gather_near(h)
    share_h = [across(h, held)]
    arrived(far_g)
    near_g = gather_near(g)
    share_g = [across(g, held)]
    share_h += share(h, near_h)

    def squeeze(c):
        blocks = c.gathered[...].astype(F32).reshape(32, 16, half)
        left = blocks[:, :8, :].reshape(256, half)
        right = blocks[:, 8:, :].reshape(256, half)
        spread = jnp.concatenate([left, right], axis=1).astype(BF16)
        at = lax.broadcasted_iota(jnp.int32, (192, 256), 0)
        come = lax.broadcasted_iota(jnp.int32, (192, 256), 1)
        within = come & 7
        pick = jnp.where((within < 6) & (at == 6 * (come >> 3) + within), 1.0, 0.0).astype(BF16)
        c.x[...] = jnp.dot(pick, spread, preferred_element_type=F32).astype(BF16)

    def expander():
        at = lax.broadcasted_iota(jnp.int32, (128, 96), 0)
        come = lax.broadcasted_iota(jnp.int32, (128, 96), 1)
        within = at & 7
        return jnp.where((within < 6) & (come == 6 * (at >> 3) + within), 1.0, 0.0).astype(BF16)

    def row_groups(value):
        return [value[48 * up:48 * up + 48] for up in range(4)]

    def relays(c, ahead):
        c.send1[2] = c.part[2].astype(BF16)
        return [
            send(c.send1.at[2, pl.ds(0, 2)], c.relay.at[0], ahead(1)),
            send(c.send1.at[2, pl.ds(2, 2)], c.relay.at[1], ahead(-1)),
        ]

    def direct_up(c, ahead):
        c.send1[1, 2:4] = c.part[1, 2:4].astype(BF16)
        return [send(c.send1.at[1, pl.ds(2, 2)], c.near1.at[0, pl.ds(2, 2)], ahead(1))]

    def direct_down(c, ahead):
        c.send1[3, 0:2] = c.part[3, 0:2].astype(BF16)
        return [send(c.send1.at[3, pl.ds(0, 2)], c.near1.at[1, pl.ds(0, 2)], ahead(-1))]

    def passed_on(c, got, ahead):
        arrived(got[:1])
        c.send1[1, 0:2] = (c.part[1, 0:2] + c.relay[0].astype(F32)).astype(BF16)
        out = [send(c.send1.at[1, pl.ds(0, 2)], c.near1.at[0, pl.ds(0, 2)], ahead(1))]
        arrived(got[1:])
        c.send1[3, 2:4] = (c.part[3, 2:4] + c.relay[1].astype(F32)).astype(BF16)
        out.append(send(c.send1.at[3, pl.ds(2, 2)], c.near1.at[1, pl.ds(2, 2)], ahead(-1)))
        return out

    def second_sum(c, got, ahead, place):
        arrived(got)
        c.total[...] = c.part[0] + c.near1[0].astype(F32) + c.near1[1].astype(F32)
        c.send2[...] = c.total[...].astype(BF16)
        out = []
        for n, step in enumerate((2, 1, -1)):
            there = lax.rem(place + step + 4, 4)
            out.append(send(c.send2.at[there], c.recv2.at[n], ahead(step)))
        return out

    def summed(c, got, place):
        arrived(got)
        return (
            c.total[place] + c.recv2[0].astype(F32) + c.recv2[1].astype(F32) + c.recv2[2].astype(F32)
        )

    local[2].wait()
    arrived(share_h)
    squeeze(h)

    def hidden_part(rel):
        cut = pl.ds(pl.multiple_of(lax.rem(x + rel, 4) * hid, hid), hid)
        got = jnp.dot(h.x[...], win[:, cut], preferred_element_type=F32)
        for v, piece in enumerate(row_groups(got)):
            h.part[rel, v] = piece

    hidden_part(2)
    relay_h = relays(h, at_x)
    hidden_part(1)
    direct_h = direct_up(h, at_x)
    hidden_part(3)
    direct_h += direct_down(h, at_x)
    hidden_part(0)

    share_g += share(g, near_g)
    local[3].wait()
    direct_h += passed_on(h, relay_h, at_x)
    arrived(share_g)
    squeeze(g)

    def grad_part(u, carry):
        got = against(g.x[...], wout[pl.ds(pl.multiple_of(u * hid, hid), hid), :])
        for v, piece in enumerate(row_groups(got)):
            g.part[lax.rem(v - y + 4, 4), u] = piece
        return carry

    lax.fori_loop(0, 4, grad_part, 0)
    relay_g = relays(g, at_y)
    direct_g = direct_up(g, at_y) + direct_down(g, at_y)

    second_h = second_sum(h, direct_h, at_y, y)
    direct_g += passed_on(g, relay_g, at_y)
    hidden = summed(h, second_h, y)
    act, slope = gelu_and_slope(hidden)
    slope_ref[...] = slope
    h.all[x, y] = act.astype(BF16)

    def spread_first(c, chunk, place, ahead):
        piece = c.all.at[chunk, place]
        return [send(piece, piece, ahead(step)) for step in (2, 1, -1)]

    def spread_second(c, got, chunk, ahead):
        arrived(got)
        low, high = c.all.at[chunk, pl.ds(0, 2)], c.all.at[chunk, pl.ds(2, 2)]
        return [
            send(low, low, ahead(1)),
            send(high, high, ahead(-1)),
            send(high, high, ahead(1)),
            send(low, low, ahead(-1)),
        ]

    def spread_third(c, got, place, ahead):
        arrived(got[:1])
        piece = c.all.at[lax.rem(place + 3, 4), pl.ds(0, 2)]
        out = [send(piece, piece, ahead(1))]
        arrived(got[1:2])
        piece = c.all.at[lax.rem(place + 1, 4), pl.ds(2, 2)]
        out.append(send(piece, piece, ahead(-1)))
        return out

    first_h = spread_first(h, x, y, at_y)
    second_g = second_sum(g, direct_g, at_x, x)
    spread_h = spread_second(h, first_h, x, at_x)
    grad_act = summed(g, second_g, x)
    g.all[y, x] = (grad_act * slope_ref[...]).astype(BF16)
    first_g = spread_first(g, y, x, at_x)

    expand = expander()

    def widened(first, second):
        rows = jnp.concatenate([first, second], axis=0)
        return jnp.dot(expand, rows, preferred_element_type=F32).astype(BF16)

    def mixed_part(rel):
        u = lax.rem(x + rel, 4)
        rows = [widened(h.all[u, 2 * side], h.all[u, 2 * side + 1]) for side in range(2)]
        cut = pl.ds(pl.multiple_of(u * hid, hid), hid)
        got = jnp.dot(jnp.concatenate(rows, axis=0), wout[cut, :], preferred_element_type=F32)
        return got.reshape(2, 128, width)

    h.acc[...] = mixed_part(0)
    spread_h2 = spread_third(h, spread_h, x, at_x)
    spread_g = spread_second(g, first_g, y, at_y)
    arrived(spread_h[2:])
    h.acc[...] += mixed_part(1)
    h.acc[...] += mixed_part(3)
    spread_g2 = spread_third(g, spread_g, y, at_y)
    arrived(spread_h2)
    h.acc[...] += mixed_part(2)

    def in_blocks(c, side):
        acc = c.acc[side]
        left = acc[:, :half].reshape(16, 8, half)
        right = acc[:, half:].reshape(16, 8, half)
        c.blocks[side] = jnp.concatenate([left, right], axis=1)

    def to_other_core(c):
        in_blocks(c, 1 - core)
        return [send(c.blocks.at[1 - core], c.swap, other_core)]

    def to_near(c, got):
        arrived(got)
        blocks = c.blocks[core] + c.swap[...]
        c.blocks[core] = blocks
        c.sendz[...] = blocks.astype(BF16)
        up = c.sendz.at[pl.ds(lax.rem(z + 3, 4) * 4, 4)]
        down = c.sendz.at[pl.ds(lax.rem(z + 1, 4) * 4, 4)]
        here = lax.rem(z, 4) * 4
        return [
            send(c.sendz.at[pl.ds(here, 2)], c.nearz2.at[pl.ds(0, 2)], at_z(2)),
            send(c.sendz.at[pl.ds(here + 2, 2)], c.nearz2.at[pl.ds(2, 2)], at_z(-2)),
            send(up, c.nearz.at[0], at_z(1)),
            send(down, c.nearz.at[1], at_z(-1)),
        ]

    def to_far(c, got):
        arrived(got)
        total = c.blocks[core, pl.ds(held, 4)] + c.nearz[0].astype(F32)
        total = total + c.nearz[1].astype(F32) + c.nearz2[...].astype(F32)
        c.sendf[...] = total.astype(BF16)
        out = []
        for n, step in enumerate(FAR):
            there = lax.div(lax.rem(z + step + 16, 16), 4)
            out.append(send(c.sendf.at[there], c.recvf.at[n], at_z(step)))
        return out

    def finish(c, got, out_ref):
        arrived(got)
        total = c.recvf[0].astype(F32) + c.recvf[1].astype(F32)
        total = total + c.recvf[2].astype(F32) + c.recvf[3].astype(F32)
        whole = jnp.concatenate([total[:8], total[8:]], axis=1)
        out_ref[...] = whole[:6].astype(BF16)

    swap_h = to_other_core(h)
    in_blocks(h, core)
    near_h = to_near(h, swap_h)

    arrived(spread_g[2:])
    arrived(spread_g2)

    def grad_in_part(side):
        rows = [widened(g.all[2 * side, u], g.all[2 * side + 1, u]) for u in range(4)]
        g.acc[side] = against(jnp.concatenate(rows, axis=1), win[...])

    grad_in_part(1 - core)
    swap_g = to_other_core(g)
    grad_in_part(core)
    in_blocks(g, core)
    near_g = to_near(g, swap_g)
    far_h = to_far(h, near_h)
    far_g = to_far(g, near_g)
    finish(h, far_h, mixed_ref)
    finish(g, far_g, gin_ref)

    for copy in started:
        copy.wait_send()


def shards(tokens, w_in, w_out, grad_out):
    rows, width = tokens.shape
    half = width // 2
    out = jax.ShapeDtypeStruct((rows, width), BF16)
    vmem = pl.BlockSpec(memory_space=pltpu.VMEM)
    hbm = pl.BlockSpec(memory_space=pltpu.HBM)
    return pl.pallas_call(
        kernel,
        out_shape=(out, out),
        in_specs=[hbm, hbm, hbm, hbm],
        out_specs=(vmem, vmem),
        scratch_shapes=[
            pltpu.VMEM(w_in.shape, BF16),
            pltpu.VMEM(w_out.shape, BF16),
            pltpu.VMEM((8, width), F32),
            pltpu.VMEM((48, half), F32),
        ]
        + chain_scratch(half, width)
        + chain_scratch(half, width)
        + [
            pltpu.SemaphoreType.DMA((4,)),
            pltpu.SemaphoreType.DMA((COPIES,)),
            pltpu.SemaphoreType.DMA((COPIES,)),
        ],
        compiler_params=pltpu.CompilerParams(
            collective_id=0, has_side_effects=True, vmem_limit_bytes=62 * 1024 * 1024
        ),
        cost_estimate=pl.CostEstimate(
            flops=8 * 192 * width * w_in.shape[1], bytes_accessed=4 * w_in.size, transcendentals=0
        ),
    )(tokens, w_in, w_out, grad_out)


def solution(mesh):
    placed = (P("col", "row"), P("row", "col"), P("col", "row"), P("col", "row"))
    return jax.shard_map(
        shards,
        mesh=mesh,
        in_specs=placed,
        out_specs=(P("col", "row"), P("col", "row")),
        check_vma=False,
    )
```

```python
import jax
import jax.numpy as jnp
from jax import lax
from jax.experimental import pallas as pl
from jax.experimental.pallas import tpu as pltpu
from jax.sharding import PartitionSpec as P

gelu_scale = 0.7978845608028654
cubic_coef = 0.044715

F32, BF16 = jnp.float32, jnp.bfloat16
MESH = pl.DeviceIdType.MESH
NEAR, FAR = (1, -1, 2, -2), (2, -2, 6, -6)


def gelu_and_slope(values):
    squared = values * values
    bent = jnp.tanh(gelu_scale * (values + cubic_coef * squared * values))
    act = 0.5 * values * (1.0 + bent)
    slope = 0.5 * (1.0 + bent) + 0.5 * values * (1.0 - bent * bent) * gelu_scale * (
        1.0 + 3.0 * cubic_coef * squared
    )
    return act, slope


def against(left, right):
    return lax.dot_general(left, right, (((1,), (1,)), ((), ())), preferred_element_type=F32)


class Chain:
    def __init__(self, refs):
        (self.own, self.gathered, self.x, self.part, self.send1, self.relay, self.near1,
         self.total, self.send2, self.recv2, self.all, self.acc, self.blocks, self.sendz,
         self.nearz, self.nearz2, self.sendf, self.recvf, self.swap, self.raw) = refs


def chain_scratch(half, width):
    block = (48, half)
    return [
        pltpu.VMEM((16, half), BF16),
        pltpu.VMEM((2, 16, 16, half), BF16),
        pltpu.VMEM((192, width), BF16),
        pltpu.VMEM((4, 4) + block, F32),
        pltpu.VMEM((4, 4) + block, BF16),
        pltpu.VMEM((2, 2) + block, BF16),
        pltpu.VMEM((2, 4) + block, BF16),
        pltpu.VMEM((4,) + block, F32),
        pltpu.VMEM((4,) + block, BF16),
        pltpu.VMEM((3,) + block, BF16),
        pltpu.VMEM((4, 4) + block, BF16),
        pltpu.VMEM((2, 128, width), F32),
        pltpu.VMEM((2, 16, 16, half), F32),
        pltpu.VMEM((16, 16, half), BF16),
        pltpu.VMEM((2, 4, 16, half), BF16),
        pltpu.VMEM((4, 16, half), BF16),
        pltpu.VMEM((4, 16, half), BF16),
        pltpu.VMEM((4, 16, half), BF16),
        pltpu.VMEM((16, 16, half), F32),
        pltpu.VMEM((6, width), BF16),
    ]


CHAIN_REFS = 20
COPIES = 96


def kernel(tok_ref, win_ref, wout_ref, gout_ref, mixed_ref, gin_ref, *scratch):
    win, wout, padded, slope_ref = scratch[:4]
    h = Chain(scratch[4:4 + CHAIN_REFS])
    g = Chain(scratch[4 + CHAIN_REFS:4 + 2 * CHAIN_REFS])
    local_sem, send_sem, recv_sem = scratch[4 + 2 * CHAIN_REFS:]
    width = tok_ref.shape[1]
    hid = wout_ref.shape[0] // 4
    half = width // 2

    row, col = lax.axis_index("row"), lax.axis_index("col")
    y, x = lax.div(row, 4), lax.rem(row, 4)
    z, core = lax.div(col, 2), lax.rem(col, 2)

    def at_x(step):
        return (y * 4 + lax.rem(x + step + 4, 4), col)

    def at_y(step):
        return (lax.rem(y + step + 4, 4) * 4 + x, col)

    def at_z(step):
        return (row, lax.rem(z + step + 16, 16) * 2 + core)

    other_core = (row, z * 2 + 1 - core)

    local = [
        pltpu.make_async_copy(src, dst, local_sem.at[n])
        for n, (src, dst) in enumerate(
            ((tok_ref, h.raw), (gout_ref, g.raw), (win_ref, win), (wout_ref, wout))
        )
    ]
    for copy in local:
        copy.start()

    partners = [other_core]
    partners += [at_x(step) for step in (1, -1, 2)]
    partners += [at_y(step) for step in (1, -1, 2)]
    partners += [at_z(step) for step in (1, -1, 2, -2, 6, -6)]
    barrier = pltpu.get_barrier_semaphore()
    for partner in partners:
        pl.semaphore_signal(barrier, inc=1, device_id=partner, device_id_type=MESH)

    def pack(ref, own):
        padded[...] = jnp.zeros_like(padded)
        padded[0:6, :] = ref[...].astype(F32)
        whole = padded[...]
        own[...] = jnp.concatenate([whole[:, :half], whole[:, half:]], axis=0).astype(BF16)

    local[0].wait()
    pack(h.raw, h.own)
    local[1].wait()
    pack(g.raw, g.own)

    pl.semaphore_wait(barrier, len(partners))

    started = []

    def send(src, dst, device):
        n = len(started)
        copy = pltpu.make_async_remote_copy(
            src_ref=src, dst_ref=dst, send_sem=send_sem.at[n], recv_sem=recv_sem.at[n],
            device_id=device, device_id_type=MESH,
        )
        copy.start()
        started.append(copy)
        return copy

    def arrived(copies):
        for copy in copies:
            copy.wait_recv()

    slot = lax.rem(z, 4) * 4 + lax.div(z, 4)
    held = lax.rem(z + 2, 4) * 4

    def gather_far(c):
        return [send(c.own, c.gathered.at[core, slot], at_z(step)) for step in FAR]

    def gather_near(c):
        out = []
        for step, first, count in ((1, 0, 4), (-1, 0, 4), (2, 0, 2), (-2, 2, 2)):
            piece = c.gathered.at[core, pl.ds(held + first, count)]
            out.append(send(piece, piece, at_z(step)))
        return out

    def across(c, first):
        piece = c.gathered.at[core, pl.ds(first, 4)]
        return send(piece, piece, other_core)

    def share(c, got):
        out = []
        for copies, first in ((got[:1], z + 1), (got[1:2], z + 3), (got[2:], z)):
            arrived(copies)
            out.append(across(c, lax.rem(first, 4) * 4))
        return out

    far_h = gather_far(h)
    far_g = gather_far(g)
    arrived(far_h)
    near_h = gather_near(h)
    share_h = [across(h, held)]
    arrived(far_g)
    near_g = gather_near(g)
    share_g = [across(g, held)]
    share_h += share(h, near_h)

    def squeeze(c):
        blocks = c.gathered[...].astype(F32).reshape(32, 16, half)
        left = blocks[:, :8, :].reshape(256, half)
        right = blocks[:, 8:, :].reshape(256, half)
        spread = jnp.concatenate([left, right], axis=1).astype(BF16)
        at = lax.broadcasted_iota(jnp.int32, (192, 256), 0)
        come = lax.broadcasted_iota(jnp.int32, (192, 256), 1)
        within = come & 7
        pick = jnp.where((within < 6) & (at == 6 * (come >> 3) + within), 1.0, 0.0).astype(BF16)
        c.x[...] = jnp.dot(pick, spread, preferred_element_type=F32).astype(BF16)

    def expander():
        at = lax.broadcasted_iota(jnp.int32, (128, 96), 0)
        come = lax.broadcasted_iota(jnp.int32, (128, 96), 1)
        within = at & 7
        return jnp.where((within < 6) & (come == 6 * (at >> 3) + within), 1.0, 0.0).astype(BF16)

    def row_groups(value):
        return [value[48 * up:48 * up + 48] for up in range(4)]

    def relays(c, ahead):
        c.send1[2] = c.part[2].astype(BF16)
        return [
            send(c.send1.at[2, pl.ds(0, 2)], c.relay.at[0], ahead(1)),
            send(c.send1.at[2, pl.ds(2, 2)], c.relay.at[1], ahead(-1)),
        ]

    def direct_up(c, ahead):
        c.send1[1, 2:4] = c.part[1, 2:4].astype(BF16)
        return [send(c.send1.at[1, pl.ds(2, 2)], c.near1.at[0, pl.ds(2, 2)], ahead(1))]

    def direct_down(c, ahead):
        c.send1[3, 0:2] = c.part[3, 0:2].astype(BF16)
        return [send(c.send1.at[3, pl.ds(0, 2)], c.near1.at[1, pl.ds(0, 2)], ahead(-1))]

    def passed_on(c, got, ahead):
        arrived(got[:1])
        c.send1[1, 0:2] = (c.part[1, 0:2] + c.relay[0].astype(F32)).astype(BF16)
        out = [send(c.send1.at[1, pl.ds(0, 2)], c.near1.at[0, pl.ds(0, 2)], ahead(1))]
        arrived(got[1:])
        c.send1[3, 2:4] = (c.part[3, 2:4] + c.relay[1].astype(F32)).astype(BF16)
        out.append(send(c.send1.at[3, pl.ds(2, 2)], c.near1.at[1, pl.ds(2, 2)], ahead(-1)))
        return out

    def second_sum(c, got, ahead, place):
        arrived(got)
        c.total[...] = c.part[0] + c.near1[0].astype(F32) + c.near1[1].astype(F32)
        c.send2[...] = c.total[...].astype(BF16)
        out = []
        for n, step in enumerate((2, 1, -1)):
            there = lax.rem(place + step + 4, 4)
            out.append(send(c.send2.at[there], c.recv2.at[n], ahead(step)))
        return out

    def summed(c, got, place):
        arrived(got)
        return (
            c.total[place] + c.recv2[0].astype(F32) + c.recv2[1].astype(F32) + c.recv2[2].astype(F32)
        )

    local[2].wait()
    arrived(share_h)
    squeeze(h)

    def hidden_part(u, carry):
        cut = pl.ds(pl.multiple_of(u * hid, hid), hid)
        got = jnp.dot(h.x[...], win[:, cut], preferred_element_type=F32)
        for v, piece in enumerate(row_groups(got)):
            h.part[lax.rem(u - x + 4, 4), v] = piece
        return carry

    lax.fori_loop(0, 4, hidden_part, 0)
    relay_h = relays(h, at_x)
    direct_h = direct_up(h, at_x) + direct_down(h, at_x)

    share_g += share(g, near_g)
    local[3].wait()
    direct_h += passed_on(h, relay_h, at_x)
    arrived(share_g)
    squeeze(g)

    def grad_part(u, carry):
        got = against(g.x[...], wout[pl.ds(pl.multiple_of(u * hid, hid), hid), :])
        for v, piece in enumerate(row_groups(got)):
            g.part[lax.rem(v - y + 4, 4), u] = piece
        return carry

    lax.fori_loop(0, 4, grad_part, 0)
    relay_g = relays(g, at_y)
    direct_g = direct_up(g, at_y) + direct_down(g, at_y)

    second_h = second_sum(h, direct_h, at_y, y)
    direct_g += passed_on(g, relay_g, at_y)
    hidden = summed(h, second_h, y)
    act, slope = gelu_and_slope(hidden)
    slope_ref[...] = slope
    h.all[x, y] = act.astype(BF16)

    def spread_first(c, chunk, place, ahead):
        piece = c.all.at[chunk, place]
        return [send(piece, piece, ahead(step)) for step in (2, 1, -1)]

    def spread_second(c, got, chunk, ahead):
        arrived(got)
        low, high = c.all.at[chunk, pl.ds(0, 2)], c.all.at[chunk, pl.ds(2, 2)]
        return [
            send(low, low, ahead(1)),
            send(high, high, ahead(-1)),
            send(high, high, ahead(1)),
            send(low, low, ahead(-1)),
        ]

    def spread_third(c, got, place, ahead):
        arrived(got[:1])
        piece = c.all.at[lax.rem(place + 3, 4), pl.ds(0, 2)]
        out = [send(piece, piece, ahead(1))]
        arrived(got[1:2])
        piece = c.all.at[lax.rem(place + 1, 4), pl.ds(2, 2)]
        out.append(send(piece, piece, ahead(-1)))
        return out

    first_h = spread_first(h, x, y, at_y)
    second_g = second_sum(g, direct_g, at_x, x)
    spread_h = spread_second(h, first_h, x, at_x)
    grad_act = summed(g, second_g, x)
    g.all[y, x] = (grad_act * slope_ref[...]).astype(BF16)
    first_g = spread_first(g, y, x, at_x)

    expand = expander()

    def widened(first, second):
        rows = jnp.concatenate([first, second], axis=0)
        return jnp.dot(expand, rows, preferred_element_type=F32).astype(BF16)

    def mixed_part(u, carry):
        rows = [widened(h.all[u, 2 * side], h.all[u, 2 * side + 1]) for side in range(2)]
        cut = pl.ds(pl.multiple_of(u * hid, hid), hid)
        got = jnp.dot(jnp.concatenate(rows, axis=0), wout[cut, :], preferred_element_type=F32)
        h.acc[...] += got.reshape(2, 128, width)
        return carry

    spread_h2 = spread_third(h, spread_h, x, at_x)
    spread_g = spread_second(g, first_g, y, at_y)
    arrived(spread_h[2:])
    spread_g2 = spread_third(g, spread_g, y, at_y)
    arrived(spread_h2)
    h.acc[...] = jnp.zeros_like(h.acc)
    lax.fori_loop(0, 4, mixed_part, 0)

    def in_blocks(c, side):
        acc = c.acc[side]
        left = acc[:, :half].reshape(16, 8, half)
        right = acc[:, half:].reshape(16, 8, half)
        c.blocks[side] = jnp.concatenate([left, right], axis=1)

    def to_other_core(c):
        in_blocks(c, 1 - core)
        return [send(c.blocks.at[1 - core], c.swap, other_core)]

    def to_near(c, got):
        arrived(got)
        blocks = c.blocks[core] + c.swap[...]
        c.blocks[core] = blocks
        c.sendz[...] = blocks.astype(BF16)
        up = c.sendz.at[pl.ds(lax.rem(z + 3, 4) * 4, 4)]
        down = c.sendz.at[pl.ds(lax.rem(z + 1, 4) * 4, 4)]
        here = lax.rem(z, 4) * 4
        return [
            send(c.sendz.at[pl.ds(here, 2)], c.nearz2.at[pl.ds(0, 2)], at_z(2)),
            send(c.sendz.at[pl.ds(here + 2, 2)], c.nearz2.at[pl.ds(2, 2)], at_z(-2)),
            send(up, c.nearz.at[0], at_z(1)),
            send(down, c.nearz.at[1], at_z(-1)),
        ]

    def to_far(c, got):
        arrived(got)
        total = c.blocks[core, pl.ds(held, 4)] + c.nearz[0].astype(F32)
        total = total + c.nearz[1].astype(F32) + c.nearz2[...].astype(F32)
        c.sendf[...] = total.astype(BF16)
        out = []
        for n, step in enumerate(FAR):
            there = lax.div(lax.rem(z + step + 16, 16), 4)
            out.append(send(c.sendf.at[there], c.recvf.at[n], at_z(step)))
        return out

    def finish(c, got, out_ref):
        arrived(got)
        total = c.recvf[0].astype(F32) + c.recvf[1].astype(F32)
        total = total + c.recvf[2].astype(F32) + c.recvf[3].astype(F32)
        whole = jnp.concatenate([total[:8], total[8:]], axis=1)
        out_ref[...] = whole[:6].astype(BF16)

    swap_h = to_other_core(h)
    in_blocks(h, core)
    near_h = to_near(h, swap_h)

    arrived(spread_g[2:])
    arrived(spread_g2)

    def grad_in_part(u, carry):
        rows = [widened(g.all[2 * side, u], g.all[2 * side + 1, u]) for side in range(2)]
        cut = pl.ds(pl.multiple_of(u * hid, hid), hid)
        got = against(jnp.concatenate(rows, axis=0), win[:, cut])
        g.acc[...] += got.reshape(2, 128, width)
        return carry

    g.acc[...] = jnp.zeros_like(g.acc)
    lax.fori_loop(0, 4, grad_in_part, 0)
    swap_g = to_other_core(g)
    in_blocks(g, core)
    near_g = to_near(g, swap_g)
    far_h = to_far(h, near_h)
    far_g = to_far(g, near_g)
    finish(h, far_h, mixed_ref)
    finish(g, far_g, gin_ref)

    for copy in started:
        copy.wait_send()


def shards(tokens, w_in, w_out, grad_out):
    rows, width = tokens.shape
    half = width // 2
    out = jax.ShapeDtypeStruct((rows, width), BF16)
    vmem = pl.BlockSpec(memory_space=pltpu.VMEM)
    hbm = pl.BlockSpec(memory_space=pltpu.HBM)
    return pl.pallas_call(
        kernel,
        out_shape=(out, out),
        in_specs=[hbm, hbm, hbm, hbm],
        out_specs=(vmem, vmem),
        scratch_shapes=[
            pltpu.VMEM(w_in.shape, BF16),
            pltpu.VMEM(w_out.shape, BF16),
            pltpu.VMEM((8, width), F32),
            pltpu.VMEM((48, half), F32),
        ]
        + chain_scratch(half, width)
        + chain_scratch(half, width)
        + [
            pltpu.SemaphoreType.DMA((4,)),
            pltpu.SemaphoreType.DMA((COPIES,)),
            pltpu.SemaphoreType.DMA((COPIES,)),
        ],
        compiler_params=pltpu.CompilerParams(
            collective_id=0, has_side_effects=True, vmem_limit_bytes=62 * 1024 * 1024
        ),
        cost_estimate=pl.CostEstimate(
            flops=8 * 192 * width * w_in.shape[1], bytes_accessed=4 * w_in.size, transcendentals=0
        ),
    )(tokens, w_in, w_out, grad_out)


def solution(mesh):
    placed = (P("col", "row"), P("row", "col"), P("col", "row"), P("col", "row"))
    return jax.shard_map(
        shards,
        mesh=mesh,
        in_specs=placed,
        out_specs=(P("col", "row"), P("col", "row")),
        check_vma=False,
    )
```

```python
import jax
import jax.numpy as jnp
from jax import lax
from jax.experimental import pallas as pl
from jax.experimental.pallas import tpu as pltpu
from jax.sharding import PartitionSpec as P

gelu_scale = 0.7978845608028654
cubic_coef = 0.044715

F32, BF16 = jnp.float32, jnp.bfloat16
MESH = pl.DeviceIdType.MESH
NEAR, FAR = (1, -1, 2, -2), (2, -2, 6, -6)


def gelu_and_slope(values):
    squared = values * values
    bent = jnp.tanh(gelu_scale * (values + cubic_coef * squared * values))
    act = 0.5 * values * (1.0 + bent)
    slope = 0.5 * (1.0 + bent) + 0.5 * values * (1.0 - bent * bent) * gelu_scale * (
        1.0 + 3.0 * cubic_coef * squared
    )
    return act, slope


def against(left, right):
    return lax.dot_general(left, right, (((1,), (1,)), ((), ())), preferred_element_type=F32)


class Chain:
    def __init__(self, refs):
        (self.x, self.part, self.send1, self.relay, self.near1,
         self.total, self.send2, self.recv2, self.all, self.acc, self.blocks, self.sendz,
         self.nearz, self.nearz2, self.sendf, self.recvf) = refs


def chain_scratch(half, width):
    block = (48, half)
    return [
        pltpu.VMEM((96, width), BF16),
        pltpu.VMEM((4, 4) + block, F32),
        pltpu.VMEM((4, 4) + block, BF16),
        pltpu.VMEM((2, 2) + block, BF16),
        pltpu.VMEM((2, 4) + block, BF16),
        pltpu.VMEM((4,) + block, F32),
        pltpu.VMEM((4,) + block, BF16),
        pltpu.VMEM((3,) + block, BF16),
        pltpu.VMEM((4, 4) + block, BF16),
        pltpu.VMEM((128, width), F32),
        pltpu.VMEM((16, 16, half), F32),
        pltpu.VMEM((16, 16, half), BF16),
        pltpu.VMEM((2, 4, 16, half), BF16),
        pltpu.VMEM((4, 16, half), BF16),
        pltpu.VMEM((4, 16, half), BF16),
        pltpu.VMEM((4, 16, half), BF16),
    ]


CHAIN_REFS = 16
COPIES = 96


def kernel(tok_ref, win_ref, wout_ref, gout_ref, mixed_ref, gin_ref, *scratch):
    win, wout, raw, gathered, slope_ref = scratch[:5]
    h = Chain(scratch[5:5 + CHAIN_REFS])
    g = Chain(scratch[5 + CHAIN_REFS:5 + 2 * CHAIN_REFS])
    local_sem, send_sem, recv_sem = scratch[5 + 2 * CHAIN_REFS:]
    width = tok_ref.shape[1]
    half = width // 2

    row, col = lax.axis_index("row"), lax.axis_index("col")
    y, x = lax.div(row, 4), lax.rem(row, 4)
    z, core = lax.div(col, 2), lax.rem(col, 2)

    def at_x(step):
        return (y * 4 + lax.rem(x + step + 4, 4), col)

    def at_y(step):
        return (lax.rem(y + step + 4, 4) * 4 + x, col)

    def at_z(step):
        return (row, lax.rem(z + step + 16, 16) * 2 + core)

    other_core = (row, z * 2 + 1 - core)

    moves = [(tok_ref, raw.at[0]), (gout_ref, raw.at[1])]
    for part in range(2):
        cut = pl.ds(part * width, width)
        moves.append((win_ref.at[:, cut], win.at[2 * core + part]))
    for part in range(2):
        cut = pl.ds(part * width, width)
        moves.append((wout_ref.at[cut, :], wout.at[2 * core + part]))
    local = [pltpu.make_async_copy(src, dst, local_sem.at[n]) for n, (src, dst) in enumerate(moves)]
    for copy in local:
        copy.start()

    partners = [other_core]
    partners += [at_x(step) for step in (1, -1, 2)]
    partners += [at_y(step) for step in (1, -1, 2)]
    partners += [at_z(step) for step in (1, -1, 2, -2, 6, -6)]
    barrier = pltpu.get_barrier_semaphore()
    for partner in partners:
        pl.semaphore_signal(barrier, inc=1, device_id=partner, device_id_type=MESH)

    def slot(place):
        return lax.rem(place, 4) * 4 + lax.div(place, 4)

    empty = jnp.zeros((2, width), F32)
    for n in range(2):
        local[n].wait()
        whole = jnp.concatenate([raw[n].astype(F32), empty], axis=0)
        folded = jnp.concatenate([whole[:, :half], whole[:, half:]], axis=0)
        gathered[slot(z), n] = folded.astype(BF16)

    pl.semaphore_wait(barrier, len(partners))

    started = []

    def send(src, dst, device):
        n = len(started)
        copy = pltpu.make_async_remote_copy(
            src_ref=src, dst_ref=dst, send_sem=send_sem.at[n], recv_sem=recv_sem.at[n],
            device_id=device, device_id_type=MESH,
        )
        copy.start()
        started.append(copy)
        return copy

    def arrived(copies):
        for copy in copies:
            copy.wait_recv()

    pieces = []
    for part in range(2):
        for rows in range(2):
            src = win_ref.at[pl.ds(rows * half, half), pl.ds(part * width, width)]
            pieces.append((src, win.at[2 * core + part, pl.ds(rows * half, half)]))
    for part in range(2):
        for rows in range(2):
            src = wout_ref.at[pl.ds(part * width + rows * half, half)]
            pieces.append((src, wout.at[2 * core + part, pl.ds(rows * half, half)]))

    held = lax.rem(z + 2, 4) * 4
    pushed, up, down = [], [], []
    for step in range(8):
        arrived(up[-1:])
        block = gathered.at[slot(lax.rem(z - step + 16, 16))]
        block = block if step < 7 else block.at[0]
        up.append(send(block, block, at_z(1)))
        arrived(down[-1:])
        block = gathered.at[slot(lax.rem(z + step, 16))]
        block = block if step < 7 else block.at[1]
        down.append(send(block, block, at_z(-1)))
        for src, dst in pieces[2 * step:2 * step + 2]:
            pushed.append(send(src, dst, other_core))
    arrived(up[-1:] + down[-1:])

    def squeeze(c, n):
        blocks = gathered[:, n].astype(F32)
        left = blocks[:, :8, :].reshape(128, half)
        right = blocks[:, 8:, :].reshape(128, half)
        spread = jnp.concatenate([left, right], axis=1).astype(BF16)
        at = lax.broadcasted_iota(jnp.int32, (96, 128), 0)
        come = lax.broadcasted_iota(jnp.int32, (96, 128), 1)
        within = come & 7
        pick = jnp.where((within < 6) & (at == 6 * (come >> 3) + within), 1.0, 0.0).astype(BF16)
        c.x[...] = jnp.dot(pick, spread, preferred_element_type=F32).astype(BF16)

    def expander():
        at = lax.broadcasted_iota(jnp.int32, (128, 96), 0)
        come = lax.broadcasted_iota(jnp.int32, (128, 96), 1)
        within = at & 7
        return jnp.where((within < 6) & (come == 6 * (at >> 3) + within), 1.0, 0.0).astype(BF16)

    def quarters(value):
        return [
            value[48 * up:48 * up + 48, half * side:half * side + half]
            for up in range(2) for side in range(2)
        ]

    def relays(c, ahead):
        c.send1[2] = c.part[2].astype(BF16)
        return [
            send(c.send1.at[2, pl.ds(0, 2)], c.relay.at[0], ahead(1)),
            send(c.send1.at[2, pl.ds(2, 2)], c.relay.at[1], ahead(-1)),
        ]

    def direct_up(c, ahead):
        c.send1[1, 2:4] = c.part[1, 2:4].astype(BF16)
        return [send(c.send1.at[1, pl.ds(2, 2)], c.near1.at[0, pl.ds(2, 2)], ahead(1))]

    def direct_down(c, ahead):
        c.send1[3, 0:2] = c.part[3, 0:2].astype(BF16)
        return [send(c.send1.at[3, pl.ds(0, 2)], c.near1.at[1, pl.ds(0, 2)], ahead(-1))]

    def passed_on(c, got, ahead):
        arrived(got[:1])
        c.send1[1, 0:2] = (c.part[1, 0:2] + c.relay[0].astype(F32)).astype(BF16)
        out = [send(c.send1.at[1, pl.ds(0, 2)], c.near1.at[0, pl.ds(0, 2)], ahead(1))]
        arrived(got[1:])
        c.send1[3, 2:4] = (c.part[3, 2:4] + c.relay[1].astype(F32)).astype(BF16)
        out.append(send(c.send1.at[3, pl.ds(2, 2)], c.near1.at[1, pl.ds(2, 2)], ahead(-1)))
        return out

    def second_sum(c, got, ahead, place):
        arrived(got)
        c.total[...] = c.part[0] + c.near1[0].astype(F32) + c.near1[1].astype(F32)
        c.send2[...] = c.total[...].astype(BF16)
        out = []
        for n, step in enumerate((2, 1, -1)):
            there = lax.rem(place + step + 4, 4)
            out.append(send(c.send2.at[there], c.recv2.at[n], ahead(step)))
        return out

    def summed(c, got, place):
        arrived(got)
        return (
            c.total[place] + c.recv2[0].astype(F32) + c.recv2[1].astype(F32) + c.recv2[2].astype(F32)
        )

    squeeze(h, 0)
    for copy in local[2:4]:
        copy.wait()
    arrived(pushed[:4])

    def hidden_part(rel):
        got = jnp.dot(h.x[...], win[lax.rem(x + rel, 4)], preferred_element_type=F32)
        for v, piece in enumerate(quarters(got)):
            h.part[rel, v] = piece

    hidden_part(2)
    relay_h = relays(h, at_x)
    hidden_part(1)
    direct_h = direct_up(h, at_x)
    hidden_part(3)
    direct_h += direct_down(h, at_x)
    hidden_part(0)

    squeeze(g, 1)
    for copy in local[4:]:
        copy.wait()
    arrived(pushed[4:])

    def grad_part(u, carry):
        got = against(g.x[...], wout[u])
        for v, piece in enumerate(quarters(got)):
            g.part[lax.rem(v - y + 4, 4), u] = piece
        return carry

    lax.fori_loop(0, 4, grad_part, 0)
    relay_g = relays(g, at_y)
    direct_h += passed_on(h, relay_h, at_x)
    direct_g = direct_up(g, at_y) + direct_down(g, at_y)

    second_h = second_sum(h, direct_h, at_y, y)
    direct_g += passed_on(g, relay_g, at_y)
    hidden = summed(h, second_h, y)
    act, slope = gelu_and_slope(hidden)
    slope_ref[...] = slope
    h.all[x, y] = act.astype(BF16)

    def spread_first(c, chunk, place, ahead):
        piece = c.all.at[chunk, place]
        return [send(piece, piece, ahead(step)) for step in (2, 1, -1)]

    def spread_second(c, got, chunk, ahead):
        arrived(got)
        low, high = c.all.at[chunk, pl.ds(0, 2)], c.all.at[chunk, pl.ds(2, 2)]
        return [
            send(low, low, ahead(1)),
            send(high, high, ahead(-1)),
            send(high, high, ahead(1)),
            send(low, low, ahead(-1)),
        ]

    def spread_third(c, got, place, ahead):
        arrived(got[:1])
        piece = c.all.at[lax.rem(place + 3, 4), pl.ds(0, 2)]
        out = [send(piece, piece, ahead(1))]
        arrived(got[1:2])
        piece = c.all.at[lax.rem(place + 1, 4), pl.ds(2, 2)]
        out.append(send(piece, piece, ahead(-1)))
        return out

    first_h = spread_first(h, x, y, at_y)
    second_g = second_sum(g, direct_g, at_x, x)
    spread_h = spread_second(h, first_h, x, at_x)
    grad_act = summed(g, second_g, x)
    g.all[y, x] = (grad_act * slope_ref[...]).astype(BF16)
    first_g = spread_first(g, y, x, at_x)

    expand = expander()

    def widened(blocks):
        rows = [jnp.concatenate([blocks[2 * up], blocks[2 * up + 1]], axis=1) for up in range(2)]
        return jnp.dot(
            expand, jnp.concatenate(rows, axis=0), preferred_element_type=F32
        ).astype(BF16)

    def mixed_part(rel):
        u = lax.rem(x + rel, 4)
        return jnp.dot(widened(h.all[u]), wout[u], preferred_element_type=F32)

    h.acc[...] = mixed_part(0)
    spread_h2 = spread_third(h, spread_h, x, at_x)
    spread_g = spread_second(g, first_g, y, at_y)
    arrived(spread_h[2:])
    h.acc[...] += mixed_part(1)
    h.acc[...] += mixed_part(3)
    spread_g2 = spread_third(g, spread_g, y, at_y)
    arrived(spread_h2)
    h.acc[...] += mixed_part(2)

    def to_near(c):
        acc = c.acc[...]
        left = acc[:, :half].reshape(16, 8, half)
        right = acc[:, half:].reshape(16, 8, half)
        blocks = jnp.concatenate([left, right], axis=1)
        c.blocks[...] = blocks
        c.sendz[...] = blocks.astype(BF16)
        up = c.sendz.at[pl.ds(lax.rem(z + 3, 4) * 4, 4)]
        down = c.sendz.at[pl.ds(lax.rem(z + 1, 4) * 4, 4)]
        here = lax.rem(z, 4) * 4
        return [
            send(c.sendz.at[pl.ds(here, 2)], c.nearz2.at[pl.ds(0, 2)], at_z(2)),
            send(c.sendz.at[pl.ds(here + 2, 2)], c.nearz2.at[pl.ds(2, 2)], at_z(-2)),
            send(up, c.nearz.at[0], at_z(1)),
            send(down, c.nearz.at[1], at_z(-1)),
        ]

    def to_far(c, got):
        arrived(got)
        total = c.blocks[pl.ds(held, 4)] + c.nearz[0].astype(F32)
        total = total + c.nearz[1].astype(F32) + c.nearz2[...].astype(F32)
        c.sendf[...] = total.astype(BF16)
        out = []
        for n, step in enumerate(FAR):
            there = lax.div(lax.rem(z + step + 16, 16), 4)
            out.append(send(c.sendf.at[there], c.recvf.at[n], at_z(step)))
        return out

    def finish(c, got, out_ref):
        arrived(got)
        total = c.recvf[0].astype(F32) + c.recvf[1].astype(F32)
        total = total + c.recvf[2].astype(F32) + c.recvf[3].astype(F32)
        whole = jnp.concatenate([total[:8], total[8:]], axis=1)
        out_ref[...] = whole[:6].astype(BF16)

    near_h = to_near(h)

    arrived(spread_g[2:])
    arrived(spread_g2)
    g.acc[...] = jnp.zeros_like(g.acc)

    def grad_in_part(u, carry):
        blocks = [g.all[v, u] for v in range(4)]
        g.acc[...] += against(widened(blocks), win[u])
        return carry

    lax.fori_loop(0, 4, grad_in_part, 0)
    near_g = to_near(g)
    far_h = to_far(h, near_h)
    far_g = to_far(g, near_g)
    late = near_g + far_h + far_g
    for copy in started:
        if not any(copy is other for other in late):
            copy.wait_send()
    finish(h, far_h, mixed_ref)
    finish(g, far_g, gin_ref)

    for copy in late:
        copy.wait_send()


def shards(tokens, w_in, w_out, grad_out):
    rows, width = tokens.shape
    half = width // 2
    out = jax.ShapeDtypeStruct((rows, width), BF16)
    vmem = pl.BlockSpec(memory_space=pltpu.VMEM)
    hbm = pl.BlockSpec(memory_space=pl.ANY)
    return pl.pallas_call(
        kernel,
        out_shape=(out, out),
        in_specs=[hbm, hbm, hbm, hbm],
        out_specs=(vmem, vmem),
        scratch_shapes=[
            pltpu.VMEM((4, width, width), BF16),
            pltpu.VMEM((4, width, width), BF16),
            pltpu.VMEM((2,) + tokens.shape, BF16),
            pltpu.VMEM((16, 2, 16, half), BF16),
            pltpu.VMEM((48, half), F32),
        ]
        + chain_scratch(half, width)
        + chain_scratch(half, width)
        + [
            pltpu.SemaphoreType.DMA((6,)),
            pltpu.SemaphoreType.DMA((COPIES,)),
            pltpu.SemaphoreType.DMA((COPIES,)),
        ],
        compiler_params=pltpu.CompilerParams(
            collective_id=0, has_side_effects=True, vmem_limit_bytes=62 * 1024 * 1024
        ),
        cost_estimate=pl.CostEstimate(
            flops=8 * 192 * width * w_in.shape[1], bytes_accessed=4 * w_in.size, transcendentals=0
        ),
    )(tokens, w_in, w_out, grad_out)


def solution(mesh):
    placed = (P("col", "row"), P("row", "col"), P("col", "row"), P("col", "row"))
    return jax.shard_map(
        shards,
        mesh=mesh,
        in_specs=placed,
        out_specs=(P("col", "row"), P("col", "row")),
        check_vma=False,
    )
```

```python
import jax
import jax.numpy as jnp
from jax import lax
from jax.experimental import pallas as pl
from jax.experimental.pallas import tpu as pltpu
from jax.sharding import PartitionSpec as P

gelu_scale = 0.7978845608028654
cubic_coef = 0.044715

F32, BF16 = jnp.float32, jnp.bfloat16
MESH = pl.DeviceIdType.MESH
FAR = (6, -6, 2, -2)


def gelu_and_slope(values):
    squared = values * values
    bent = jnp.tanh(gelu_scale * (values + cubic_coef * squared * values))
    act = 0.5 * values * (1.0 + bent)
    slope = 0.5 * (1.0 + bent) + 0.5 * values * (1.0 - bent * bent) * gelu_scale * (
        1.0 + 3.0 * cubic_coef * squared
    )
    return act, slope


def against(left, right):
    return lax.dot_general(left, right, (((1,), (1,)), ((), ())), preferred_element_type=F32)


def times(left, right):
    return jnp.dot(left, right, preferred_element_type=F32)


COPIES = 80


def kernel(
    tok_ref, win_ref, wout_ref, gout_ref, mixed_ref, gin_ref,
    win, wout, raw, own, gathered, rows_ref, part, send1, relay, near1, total, send2, recv2,
    spread, slope_out, slope_in, acc, blocks, sendz, nearz, nearz2, sendf, recvf,
    local_sem, send_sem, recv_sem, far_in_sem, far_out_sem,
):
    width = tok_ref.shape[1]
    half = width // 2

    row, col = lax.axis_index("row"), lax.axis_index("col")
    y, x = lax.div(row, 4), lax.rem(row, 4)
    z, core = lax.div(col, 2), lax.rem(col, 2)
    a = core * x + (1 - core) * y
    b = core * y + (1 - core) * x

    def at_a(step):
        there = lax.rem(a + step + 4, 4)
        return (core * (y * 4 + there) + (1 - core) * (there * 4 + x), col)

    def at_b(step):
        there = lax.rem(b + step + 4, 4)
        return (core * (there * 4 + x) + (1 - core) * (y * 4 + there), col)

    def at_z(step, on=core):
        return (row, lax.rem(z + step + 16, 16) * 2 + on)

    other_core = (row, z * 2 + 1 - core)
    turned = (x * 4 + y, z * 2 + 1 - core)

    moves = [(tok_ref, raw.at[1]), (gout_ref, raw.at[0])]
    for p in range(2):
        moves.append((win_ref.at[:, pl.ds(p * width, width)], win.at[2 * core + p]))
    for p in range(2):
        moves.append((wout_ref.at[pl.ds(p * width, width), :], wout.at[2 * core + p]))
    local = [pltpu.make_async_copy(src, dst, local_sem.at[n]) for n, (src, dst) in enumerate(moves)]
    for copy in local:
        copy.start()

    partners = [other_core, turned]
    partners += [at_a(step) for step in (1, -1, 2)]
    partners += [at_b(step) for step in (1, -1, 2)]
    partners += [at_z(step) for step in (1, -1, 2, -2, 6, -6)]
    partners += [at_z(step, 1 - core) for step in (2, -2, 6, -6)]
    barrier = pltpu.get_barrier_semaphore()
    for partner in partners:
        pl.semaphore_signal(barrier, inc=1, device_id=partner, device_id_type=MESH)

    empty = jnp.zeros((2, width), F32)
    for chain, copy in ((1, local[0]), (0, local[1])):
        copy.wait()
        whole = jnp.concatenate([raw[chain].astype(F32), empty], axis=0)
        folded = jnp.concatenate([whole[:, :half], whole[:, half:]], axis=0)
        own[chain] = folded.astype(BF16)

    pl.semaphore_wait(barrier, len(partners))

    count = [0]

    def message(src, dst, device, sem=None):
        n = count[0]
        count[0] += 1
        return pltpu.make_async_remote_copy(
            src_ref=src, dst_ref=dst, send_sem=send_sem.at[n],
            recv_sem=recv_sem.at[n] if sem is None else sem,
            device_id=device, device_id_type=MESH,
        )

    def send(src, dst, device, sem=None):
        copy = message(src, dst, device, sem)
        copy.start()
        return copy

    def arrived(copies):
        for copy in copies:
            copy.wait_recv()

    def sent(copies):
        for copy in copies:
            copy.wait_send()

    slot = lax.rem(z, 4) * 4 + lax.div(z, 4)
    held = lax.rem(z + 2, 4) * 4
    far_in = []
    for n, step in enumerate(FAR):
        for chain in (1, 0):
            far_in.append(
                send(own.at[chain], gathered.at[slot, core], at_z(step, chain), far_in_sem.at[n, core])
            )

    push_in = [
        message(win_ref.at[:, pl.ds(p * width, width)], win.at[2 * core + p], other_core)
        for p in range(2)
    ]
    push_out = [
        message(wout_ref.at[pl.ds(p * width, width), :], wout.at[2 * core + p], other_core)
        for p in range(2)
    ]

    @pl.when(core == 0)
    def _():
        for copy in push_in:
            copy.start()

    @pl.when(core == 1)
    def _():
        for copy in push_out:
            copy.start()

    for n in range(4):
        for source in range(2):
            pltpu.make_async_copy(
                own.at[source], gathered.at[held + n, source], far_in_sem.at[n, source]
            ).wait()

    near_in = []
    for step, first, size in ((1, 0, 4), (-1, 0, 4), (2, 0, 2), (-2, 2, 2)):
        piece = gathered.at[pl.ds(held + first, size)]
        near_in.append(send(piece, piece, at_z(step)))

    @pl.when(core == 0)
    def _():
        for copy in push_out:
            copy.start()

    @pl.when(core == 1)
    def _():
        for copy in push_in:
            copy.start()

    sent(far_in)

    def padding(shape, dim):
        tight = lax.broadcasted_iota(jnp.int32, shape, 1 - dim)
        wide = lax.broadcasted_iota(jnp.int32, shape, dim)
        within = wide & 7
        return jnp.where((within < 6) & (tight == 6 * (wide >> 3) + within), 1.0, 0.0).astype(BF16)

    squeeze, expand = padding((192, 256), 1), padding((256, 192), 0)

    arrived(near_in)
    gained = gathered[...].astype(F32).reshape(32, 16, half)
    left = gained[:, :8, :].reshape(256, half)
    right = gained[:, 8:, :].reshape(256, half)
    rows_ref[...] = times(squeeze, jnp.concatenate([left, right], axis=1).astype(BF16)).astype(BF16)

    def product(rel):
        quarter = lax.rem(a + rel, 4)

        def keep(got):
            for v in range(4):
                part[rel, v] = got[48 * v:48 * v + 48]

        @pl.when(core == 1)
        def _():
            keep(times(rows_ref[...], win[quarter]))

        @pl.when(core == 0)
        def _():
            keep(against(rows_ref[...], wout[quarter]))

    @pl.when(core == 1)
    def _():
        for copy in local[2:4]:
            copy.wait()
        arrived(push_in)

    @pl.when(core == 0)
    def _():
        for copy in local[4:]:
            copy.wait()
        arrived(push_out)

    low, high = pl.ds(0, 2), pl.ds(2, 2)
    product(2)
    send1[2] = part[2].astype(BF16)
    relays = [
        send(send1.at[2, low], relay.at[0], at_a(1)),
        send(send1.at[2, high], relay.at[1], at_a(-1)),
    ]

    def others(n, carry):
        product(lax.rem(n + 3, 4))
        return carry

    lax.fori_loop(0, 3, others, 0)
    send1[1, 2:4] = part[1, 2:4].astype(BF16)
    direct = [send(send1.at[1, high], near1.at[0, high], at_a(1))]
    send1[3, 0:2] = part[3, 0:2].astype(BF16)
    direct.append(send(send1.at[3, low], near1.at[1, low], at_a(-1)))

    arrived(relays[:1])
    send1[1, 0:2] = (part[1, 0:2] + relay[0].astype(F32)).astype(BF16)
    direct.append(send(send1.at[1, low], near1.at[0, low], at_a(1)))
    arrived(relays[1:])
    send1[3, 2:4] = (part[3, 2:4] + relay[1].astype(F32)).astype(BF16)
    direct.append(send(send1.at[3, high], near1.at[1, high], at_a(-1)))

    sent(near_in)
    sent(relays)
    arrived(direct)
    total[...] = part[0] + near1[0].astype(F32) + near1[1].astype(F32)
    send2[...] = total[...].astype(BF16)
    second = []
    for n, step in enumerate((2, 1, -1)):
        second.append(send(send2.at[lax.rem(b + step + 4, 4)], recv2.at[n], at_b(step)))
    sent(direct)
    arrived(second)
    summed = total[b] + recv2[0].astype(F32) + recv2[1].astype(F32) + recv2[2].astype(F32)

    turn = message(slope_out, slope_in, turned)

    @pl.when(core == 1)
    def _():
        act, slope = gelu_and_slope(summed)
        spread[a, b] = act.astype(BF16)
        slope_out[...] = slope

    @pl.when(core == 0)
    def _():
        turn.wait_recv()
        spread[a, b] = (summed * slope_in[...]).astype(BF16)

    piece = spread.at[a, b]
    first = [send(piece, piece, at_b(step)) for step in (2, 1, -1)]

    @pl.when(core == 1)
    def _():
        turn.start()

    sent(second)
    arrived(first)
    low_piece, high_piece = spread.at[a, low], spread.at[a, high]
    back = [
        send(low_piece, low_piece, at_a(1)),
        send(high_piece, high_piece, at_a(-1)),
        send(high_piece, high_piece, at_a(1)),
        send(low_piece, low_piece, at_a(-1)),
    ]

    @pl.when(core == 1)
    def _():
        for copy in local[4:]:
            copy.wait()
        arrived(push_out)

    @pl.when(core == 0)
    def _():
        for copy in local[2:4]:
            copy.wait()
        arrived(push_in)

    def contribute(rel):
        quarter = lax.rem(a + rel, 4)
        tight = jnp.concatenate([spread[quarter, v] for v in range(4)], axis=0)
        padded = times(expand, tight).astype(BF16)

        @pl.when(core == 1)
        def _():
            acc[...] += times(padded, wout[quarter])

        @pl.when(core == 0)
        def _():
            acc[...] += against(padded, win[quarter])

    acc[...] = jnp.zeros_like(acc)
    arrived(back[:1])
    piece = spread.at[lax.rem(a + 3, 4), low]
    onward = [send(piece, piece, at_a(1))]
    arrived(back[1:2])
    piece = spread.at[lax.rem(a + 1, 4), high]
    onward.append(send(piece, piece, at_a(-1)))
    contribute(0)
    arrived(back[2:])

    def sides(n, carry):
        contribute(2 * n + 1)
        return carry

    lax.fori_loop(0, 2, sides, 0)
    sent(first)
    sent(back)
    sent(push_in)
    sent(push_out)
    arrived(onward)
    contribute(2)

    wide = acc[...]
    left = wide[:, :half].reshape(32, 8, half)
    right = wide[:, half:].reshape(32, 8, half)
    folded = jnp.concatenate([left, right], axis=1).reshape(16, 2, 16, half)
    sendz[...] = folded.astype(BF16)
    here = lax.rem(z, 4) * 4
    near_out = [
        send(sendz.at[pl.ds(here, 2)], nearz2.at[low], at_z(2)),
        send(sendz.at[pl.ds(here + 2, 2)], nearz2.at[high], at_z(-2)),
        send(sendz.at[pl.ds(lax.rem(z + 3, 4) * 4, 4)], nearz.at[0], at_z(1)),
        send(sendz.at[pl.ds(lax.rem(z + 1, 4) * 4, 4)], nearz.at[1], at_z(-1)),
    ]
    blocks[...] = folded
    sent(onward)

    @pl.when(core == 1)
    def _():
        turn.wait_send()

    arrived(near_out)
    sums = blocks[pl.ds(held, 4)] + nearz2[...].astype(F32)
    sums = sums + nearz[0].astype(F32) + nearz[1].astype(F32)
    sendf[...] = sums.astype(BF16)
    far_out = []
    for n, step in enumerate(FAR):
        there = lax.div(lax.rem(z + step + 16, 16), 4)
        for target in range(2):
            far_out.append(
                send(
                    sendf.at[there, target], recvf.at[core, n], at_z(step, target),
                    far_out_sem.at[n, core],
                )
            )
    sent(near_out)
    for chain, out_ref in ((1, mixed_ref), (0, gin_ref)):
        for n in range(4):
            pltpu.make_async_copy(own.at[0], recvf.at[chain, n], far_out_sem.at[n, chain]).wait()
        got = recvf[chain, 0].astype(F32) + recvf[chain, 1].astype(F32)
        got = got + recvf[chain, 2].astype(F32) + recvf[chain, 3].astype(F32)
        out_ref[...] = jnp.concatenate([got[:8], got[8:]], axis=1)[:6].astype(BF16)
    sent(far_out)


def shards(tokens, w_in, w_out, grad_out):
    rows, width = tokens.shape
    half = width // 2
    out = jax.ShapeDtypeStruct((rows, width), BF16)
    vmem = pl.BlockSpec(memory_space=pltpu.VMEM)
    hbm = pl.BlockSpec(memory_space=pl.ANY)
    block, piece = (48, width), (16, half)
    return pl.pallas_call(
        kernel,
        out_shape=(out, out),
        in_specs=[hbm, hbm, hbm, hbm],
        out_specs=(vmem, vmem),
        scratch_shapes=[
            pltpu.VMEM((4, width, width), BF16),
            pltpu.VMEM((4, width, width), BF16),
            pltpu.VMEM((2, rows, width), BF16),
            pltpu.VMEM((2,) + piece, BF16),
            pltpu.VMEM((16, 2) + piece, BF16),
            pltpu.VMEM((192, width), BF16),
            pltpu.VMEM((4, 4) + block, F32),
            pltpu.VMEM((4, 4) + block, BF16),
            pltpu.VMEM((2, 2) + block, BF16),
            pltpu.VMEM((2, 4) + block, BF16),
            pltpu.VMEM((4,) + block, F32),
            pltpu.VMEM((4,) + block, BF16),
            pltpu.VMEM((3,) + block, BF16),
            pltpu.VMEM((4, 4) + block, BF16),
            pltpu.VMEM(block, F32),
            pltpu.VMEM(block, F32),
            pltpu.VMEM((256, width), F32),
            pltpu.VMEM((16, 2) + piece, F32),
            pltpu.VMEM((16, 2) + piece, BF16),
            pltpu.VMEM((2, 4, 2) + piece, BF16),
            pltpu.VMEM((4, 2) + piece, BF16),
            pltpu.VMEM((4, 2) + piece, BF16),
            pltpu.VMEM((2, 4) + piece, BF16),
            pltpu.SemaphoreType.DMA((6,)),
            pltpu.SemaphoreType.DMA((COPIES,)),
            pltpu.SemaphoreType.DMA((COPIES,)),
            pltpu.SemaphoreType.DMA((4, 2)),
            pltpu.SemaphoreType.DMA((4, 2)),
        ],
        compiler_params=pltpu.CompilerParams(
            collective_id=0, has_side_effects=True, vmem_limit_bytes=62 * 1024 * 1024
        ),
        cost_estimate=pl.CostEstimate(
            flops=8 * 192 * width * w_in.shape[1], bytes_accessed=4 * w_in.size, transcendentals=0
        ),
    )(tokens, w_in, w_out, grad_out)


def solution(mesh):
    placed = (P("col", "row"), P("row", "col"), P("col", "row"), P("col", "row"))
    return jax.shard_map(
        shards,
        mesh=mesh,
        in_specs=placed,
        out_specs=(P("col", "row"), P("col", "row")),
        check_vma=False,
    )
```

```python
import jax
import jax.numpy as jnp
from jax import lax
from jax.experimental import pallas as pl
from jax.experimental.pallas import tpu as pltpu
from jax.sharding import PartitionSpec as P

gelu_scale = 0.7978845608028654
cubic_coef = 0.044715

F32, BF16 = jnp.float32, jnp.bfloat16
MESH = pl.DeviceIdType.MESH
FAR = (6, -6, 2, -2)


def gelu_and_slope(values):
    squared = values * values
    bent = jnp.tanh(gelu_scale * (values + cubic_coef * squared * values))
    act = 0.5 * values * (1.0 + bent)
    slope = 0.5 * (1.0 + bent) + 0.5 * values * (1.0 - bent * bent) * gelu_scale * (
        1.0 + 3.0 * cubic_coef * squared
    )
    return act, slope


def against(left, right):
    return lax.dot_general(left, right, (((1,), (1,)), ((), ())), preferred_element_type=F32)


class Chain:
    def __init__(self, refs):
        (self.x, self.part, self.send1, self.relay, self.near1,
         self.total, self.send2, self.recv2, self.all, self.acc, self.blocks, self.sendz,
         self.nearz, self.nearz2, self.sendf, self.recvf) = refs


def chain_scratch(half, width):
    block = (48, half)
    return [
        pltpu.VMEM((96, width), BF16),
        pltpu.VMEM((4, 4) + block, F32),
        pltpu.VMEM((4, 4) + block, BF16),
        pltpu.VMEM((2, 2) + block, BF16),
        pltpu.VMEM((2, 4) + block, BF16),
        pltpu.VMEM((4,) + block, F32),
        pltpu.VMEM((4,) + block, BF16),
        pltpu.VMEM((3,) + block, BF16),
        pltpu.VMEM((4, 4) + block, BF16),
        pltpu.VMEM((128, width), F32),
        pltpu.VMEM((16, 16, half), F32),
        pltpu.VMEM((16, 16, half), BF16),
        pltpu.VMEM((2, 4, 16, half), BF16),
        pltpu.VMEM((4, 16, half), BF16),
        pltpu.VMEM((4, 16, half), BF16),
        pltpu.VMEM((4, 16, half), BF16),
    ]


CHAIN_REFS = 16
COPIES = 96


def kernel(tok_ref, win_ref, wout_ref, gout_ref, mixed_ref, gin_ref, *scratch):
    win, wout, raw, own, gathered, slope_ref = scratch[:6]
    h = Chain(scratch[6:6 + CHAIN_REFS])
    g = Chain(scratch[6 + CHAIN_REFS:6 + 2 * CHAIN_REFS])
    local_sem, send_sem, recv_sem = scratch[6 + 2 * CHAIN_REFS:]
    width = tok_ref.shape[1]
    half = width // 2

    row, col = lax.axis_index("row"), lax.axis_index("col")
    y, x = lax.div(row, 4), lax.rem(row, 4)
    z, core = lax.div(col, 2), lax.rem(col, 2)

    def at_x(step):
        return (y * 4 + lax.rem(x + step + 4, 4), col)

    def at_y(step):
        return (lax.rem(y + step + 4, 4) * 4 + x, col)

    def at_z(step):
        return (row, lax.rem(z + step + 16, 16) * 2 + core)

    other_core = (row, z * 2 + 1 - core)

    moves = [(tok_ref, raw.at[0]), (gout_ref, raw.at[1])]
    for part in range(2):
        cut = pl.ds(part * width, width)
        moves.append((win_ref.at[:, cut], win.at[2 * core + part]))
    for part in range(2):
        cut = pl.ds(part * width, width)
        moves.append((wout_ref.at[cut, :], wout.at[2 * core + part]))
    local = [pltpu.make_async_copy(src, dst, local_sem.at[n]) for n, (src, dst) in enumerate(moves)]
    for copy in local:
        copy.start()

    partners = [other_core]
    partners += [at_x(step) for step in (1, -1, 2)]
    partners += [at_y(step) for step in (1, -1, 2)]
    partners += [at_z(step) for step in (1, -1, 2, -2, 6, -6)]
    barrier = pltpu.get_barrier_semaphore()
    for partner in partners:
        pl.semaphore_signal(barrier, inc=1, device_id=partner, device_id_type=MESH)

    empty = jnp.zeros((2, width), F32)
    for n in range(2):
        local[n].wait()
        whole = jnp.concatenate([raw[n].astype(F32), empty], axis=0)
        folded = jnp.concatenate([whole[:, :half], whole[:, half:]], axis=0)
        own[n] = folded.astype(BF16)

    pl.semaphore_wait(barrier, len(partners))

    started = []

    def send(src, dst, device):
        n = len(started)
        copy = pltpu.make_async_remote_copy(
            src_ref=src, dst_ref=dst, send_sem=send_sem.at[n], recv_sem=recv_sem.at[n],
            device_id=device, device_id_type=MESH,
        )
        copy.start()
        started.append(copy)
        return copy

    def arrived(copies):
        for copy in copies:
            copy.wait_recv()

    slot = lax.rem(z, 4) * 4 + lax.div(z, 4)
    held = lax.rem(z + 2, 4) * 4

    def gather_far(n):
        return [send(own.at[n], gathered.at[n, slot], at_z(step)) for step in FAR]

    def gather_near(n):
        out = []
        for step, first, count in ((2, 0, 2), (-2, 2, 2), (1, 0, 4), (-1, 0, 4)):
            piece = gathered.at[n, pl.ds(held + first, count)]
            out.append(send(piece, piece, at_z(step)))
        return out

    far_in = [gather_far(0), gather_far(1)]
    pushed = []
    for part in range(2):
        src = win_ref.at[:, pl.ds(part * width, width)]
        pushed.append(send(src, win.at[2 * core + part], other_core))
    near_in = []
    for n in range(2):
        arrived(far_in[n])
        near_in.append(gather_near(n))
    for part in range(2):
        src = wout_ref.at[pl.ds(part * width, width)]
        pushed.append(send(src, wout.at[2 * core + part], other_core))

    def squeeze(c, n):
        blocks = gathered[n].astype(F32)
        left = blocks[:, :8, :].reshape(128, half)
        right = blocks[:, 8:, :].reshape(128, half)
        spread = jnp.concatenate([left, right], axis=1).astype(BF16)
        at = lax.broadcasted_iota(jnp.int32, (96, 128), 0)
        come = lax.broadcasted_iota(jnp.int32, (96, 128), 1)
        within = come & 7
        pick = jnp.where((within < 6) & (at == 6 * (come >> 3) + within), 1.0, 0.0).astype(BF16)
        c.x[...] = jnp.dot(pick, spread, preferred_element_type=F32).astype(BF16)

    def expander():
        at = lax.broadcasted_iota(jnp.int32, (128, 96), 0)
        come = lax.broadcasted_iota(jnp.int32, (128, 96), 1)
        within = at & 7
        return jnp.where((within < 6) & (come == 6 * (at >> 3) + within), 1.0, 0.0).astype(BF16)

    def quarters(value):
        return [
            value[48 * up:48 * up + 48, half * side:half * side + half]
            for up in range(2) for side in range(2)
        ]

    def relays(c, ahead):
        c.send1[2] = c.part[2].astype(BF16)
        return [
            send(c.send1.at[2, pl.ds(0, 2)], c.relay.at[0], ahead(1)),
            send(c.send1.at[2, pl.ds(2, 2)], c.relay.at[1], ahead(-1)),
        ]

    def direct_up(c, ahead):
        c.send1[1, 2:4] = c.part[1, 2:4].astype(BF16)
        return [send(c.send1.at[1, pl.ds(2, 2)], c.near1.at[0, pl.ds(2, 2)], ahead(1))]

    def direct_down(c, ahead):
        c.send1[3, 0:2] = c.part[3, 0:2].astype(BF16)
        return [send(c.send1.at[3, pl.ds(0, 2)], c.near1.at[1, pl.ds(0, 2)], ahead(-1))]

    def passed_on(c, got, ahead):
        arrived(got[:1])
        c.send1[1, 0:2] = (c.part[1, 0:2] + c.relay[0].astype(F32)).astype(BF16)
        out = [send(c.send1.at[1, pl.ds(0, 2)], c.near1.at[0, pl.ds(0, 2)], ahead(1))]
        arrived(got[1:])
        c.send1[3, 2:4] = (c.part[3, 2:4] + c.relay[1].astype(F32)).astype(BF16)
        out.append(send(c.send1.at[3, pl.ds(2, 2)], c.near1.at[1, pl.ds(2, 2)], ahead(-1)))
        return out

    def second_sum(c, got, ahead, place):
        arrived(got)
        c.total[...] = c.part[0] + c.near1[0].astype(F32) + c.near1[1].astype(F32)
        c.send2[...] = c.total[...].astype(BF16)
        out = []
        for n, step in enumerate((2, 1, -1)):
            there = lax.rem(place + step + 4, 4)
            out.append(send(c.send2.at[there], c.recv2.at[n], ahead(step)))
        return out

    def summed(c, got, place):
        arrived(got)
        return (
            c.total[place] + c.recv2[0].astype(F32) + c.recv2[1].astype(F32) + c.recv2[2].astype(F32)
        )

    arrived(near_in[0])
    squeeze(h, 0)
    for copy in local[2:4]:
        copy.wait()
    arrived(pushed[:2])

    def hidden_part(rel):
        got = jnp.dot(h.x[...], win[lax.rem(x + rel, 4)], preferred_element_type=F32)
        for v, piece in enumerate(quarters(got)):
            h.part[rel, v] = piece

    hidden_part(2)
    relay_h = relays(h, at_x)
    hidden_part(1)
    direct_h = direct_up(h, at_x)
    hidden_part(3)
    direct_h += direct_down(h, at_x)
    hidden_part(0)

    arrived(near_in[1])
    squeeze(g, 1)
    direct_h += passed_on(h, relay_h, at_x)
    for copy in local[4:]:
        copy.wait()
    arrived(pushed[2:])

    def grad_part(u, carry):
        got = against(g.x[...], wout[u])
        for v, piece in enumerate(quarters(got)):
            g.part[lax.rem(v - y + 4, 4), u] = piece
        return carry

    lax.fori_loop(0, 4, grad_part, 0)
    relay_g = relays(g, at_y)
    direct_g = direct_up(g, at_y) + direct_down(g, at_y)

    second_h = second_sum(h, direct_h, at_y, y)
    direct_g += passed_on(g, relay_g, at_y)
    hidden = summed(h, second_h, y)
    act, slope = gelu_and_slope(hidden)
    slope_ref[...] = slope
    h.all[x, y] = act.astype(BF16)

    def spread_first(c, chunk, place, ahead):
        piece = c.all.at[chunk, place]
        return [send(piece, piece, ahead(step)) for step in (2, 1, -1)]

    def spread_second(c, got, chunk, ahead):
        arrived(got)
        low, high = c.all.at[chunk, pl.ds(0, 2)], c.all.at[chunk, pl.ds(2, 2)]
        return [
            send(low, low, ahead(1)),
            send(high, high, ahead(-1)),
            send(high, high, ahead(1)),
            send(low, low, ahead(-1)),
        ]

    def spread_third(c, got, place, ahead):
        arrived(got[:1])
        piece = c.all.at[lax.rem(place + 3, 4), pl.ds(0, 2)]
        out = [send(piece, piece, ahead(1))]
        arrived(got[1:2])
        piece = c.all.at[lax.rem(place + 1, 4), pl.ds(2, 2)]
        out.append(send(piece, piece, ahead(-1)))
        return out

    first_h = spread_first(h, x, y, at_y)
    second_g = second_sum(g, direct_g, at_x, x)
    spread_h = spread_second(h, first_h, x, at_x)
    grad_act = summed(g, second_g, x)
    g.all[y, x] = (grad_act * slope_ref[...]).astype(BF16)
    first_g = spread_first(g, y, x, at_x)

    expand = expander()

    def widened(blocks):
        rows = [jnp.concatenate([blocks[2 * up], blocks[2 * up + 1]], axis=1) for up in range(2)]
        return jnp.dot(
            expand, jnp.concatenate(rows, axis=0), preferred_element_type=F32
        ).astype(BF16)

    def mixed_part(rel):
        u = lax.rem(x + rel, 4)
        return jnp.dot(widened(h.all[u]), wout[u], preferred_element_type=F32)

    h.acc[...] = mixed_part(0)
    spread_h2 = spread_third(h, spread_h, x, at_x)
    spread_g = spread_second(g, first_g, y, at_y)
    arrived(spread_h[2:])
    h.acc[...] += mixed_part(1)
    h.acc[...] += mixed_part(3)
    spread_g2 = spread_third(g, spread_g, y, at_y)
    arrived(spread_h2)
    h.acc[...] += mixed_part(2)

    def to_near(c):
        acc = c.acc[...]
        left = acc[:, :half].reshape(16, 8, half)
        right = acc[:, half:].reshape(16, 8, half)
        blocks = jnp.concatenate([left, right], axis=1)
        c.blocks[...] = blocks
        c.sendz[...] = blocks.astype(BF16)
        up = c.sendz.at[pl.ds(lax.rem(z + 3, 4) * 4, 4)]
        down = c.sendz.at[pl.ds(lax.rem(z + 1, 4) * 4, 4)]
        here = lax.rem(z, 4) * 4
        return [
            send(c.sendz.at[pl.ds(here, 2)], c.nearz2.at[pl.ds(0, 2)], at_z(2)),
            send(c.sendz.at[pl.ds(here + 2, 2)], c.nearz2.at[pl.ds(2, 2)], at_z(-2)),
            send(up, c.nearz.at[0], at_z(1)),
            send(down, c.nearz.at[1], at_z(-1)),
        ]

    def to_far(c, got):
        arrived(got)
        total = c.blocks[pl.ds(held, 4)] + c.nearz[0].astype(F32)
        total = total + c.nearz[1].astype(F32) + c.nearz2[...].astype(F32)
        c.sendf[...] = total.astype(BF16)
        out = []
        for n, step in enumerate(FAR):
            there = lax.div(lax.rem(z + step + 16, 16), 4)
            out.append(send(c.sendf.at[there], c.recvf.at[n], at_z(step)))
        return out

    def finish(c, got, out_ref):
        arrived(got)
        total = c.recvf[0].astype(F32) + c.recvf[1].astype(F32)
        total = total + c.recvf[2].astype(F32) + c.recvf[3].astype(F32)
        whole = jnp.concatenate([total[:8], total[8:]], axis=1)
        out_ref[...] = whole[:6].astype(BF16)

    near_h = to_near(h)

    arrived(spread_g[2:])
    arrived(spread_g2)
    g.acc[...] = jnp.zeros_like(g.acc)

    def grad_in_part(u, carry):
        blocks = [g.all[v, u] for v in range(4)]
        g.acc[...] += against(widened(blocks), win[u])
        return carry

    lax.fori_loop(0, 4, grad_in_part, 0)
    near_g = to_near(g)
    far_h = to_far(h, near_h)
    far_g = to_far(g, near_g)
    late = near_g + far_h + far_g
    for copy in started:
        if not any(copy is other for other in late):
            copy.wait_send()
    finish(h, far_h, mixed_ref)
    finish(g, far_g, gin_ref)

    for copy in late:
        copy.wait_send()


def shards(tokens, w_in, w_out, grad_out):
    rows, width = tokens.shape
    half = width // 2
    out = jax.ShapeDtypeStruct((rows, width), BF16)
    vmem = pl.BlockSpec(memory_space=pltpu.VMEM)
    hbm = pl.BlockSpec(memory_space=pl.ANY)
    return pl.pallas_call(
        kernel,
        out_shape=(out, out),
        in_specs=[hbm, hbm, hbm, hbm],
        out_specs=(vmem, vmem),
        scratch_shapes=[
            pltpu.VMEM((4, width, width), BF16),
            pltpu.VMEM((4, width, width), BF16),
            pltpu.VMEM((2,) + tokens.shape, BF16),
            pltpu.VMEM((2, 16, half), BF16),
            pltpu.VMEM((2, 16, 16, half), BF16),
            pltpu.VMEM((48, half), F32),
        ]
        + chain_scratch(half, width)
        + chain_scratch(half, width)
        + [
            pltpu.SemaphoreType.DMA((6,)),
            pltpu.SemaphoreType.DMA((COPIES,)),
            pltpu.SemaphoreType.DMA((COPIES,)),
        ],
        compiler_params=pltpu.CompilerParams(
            collective_id=0, has_side_effects=True, vmem_limit_bytes=62 * 1024 * 1024
        ),
        cost_estimate=pl.CostEstimate(
            flops=8 * 192 * width * w_in.shape[1], bytes_accessed=4 * w_in.size, transcendentals=0
        ),
    )(tokens, w_in, w_out, grad_out)


def solution(mesh):
    placed = (P("col", "row"), P("row", "col"), P("col", "row"), P("col", "row"))
    return jax.shard_map(
        shards,
        mesh=mesh,
        in_specs=placed,
        out_specs=(P("col", "row"), P("col", "row")),
        check_vma=False,
    )
```

```python
import jax
import jax.numpy as jnp
from jax import lax
from jax.experimental import pallas as pl
from jax.experimental.pallas import tpu as pltpu
from jax.sharding import PartitionSpec as P

gelu_scale = 0.7978845608028654
cubic_coef = 0.044715

F32, BF16 = jnp.float32, jnp.bfloat16
MESH = pl.DeviceIdType.MESH
FAR = (6, -6, 2, -2)


def gelu_and_slope(values):
    squared = values * values
    bent = jnp.tanh(gelu_scale * (values + cubic_coef * squared * values))
    act = 0.5 * values * (1.0 + bent)
    slope = 0.5 * (1.0 + bent) + 0.5 * values * (1.0 - bent * bent) * gelu_scale * (
        1.0 + 3.0 * cubic_coef * squared
    )
    return act, slope


def against(left, right):
    return lax.dot_general(left, right, (((1,), (1,)), ((), ())), preferred_element_type=F32)


class Chain:
    def __init__(self, refs):
        (self.x, self.part, self.send1, self.relay, self.near1,
         self.total, self.send2, self.recv2, self.all, self.acc, self.blocks, self.sendz,
         self.nearz, self.nearz2, self.sendf, self.recvf) = refs


def chain_scratch(half, width):
    block = (48, half)
    return [
        pltpu.VMEM((96, width), BF16),
        pltpu.VMEM((4, 4) + block, F32),
        pltpu.VMEM((4, 4) + block, BF16),
        pltpu.VMEM((2, 2) + block, BF16),
        pltpu.VMEM((2, 4) + block, BF16),
        pltpu.VMEM((4,) + block, F32),
        pltpu.VMEM((4,) + block, BF16),
        pltpu.VMEM((3,) + block, BF16),
        pltpu.VMEM((4, 4) + block, BF16),
        pltpu.VMEM((128, width), F32),
        pltpu.VMEM((16, 16, half), F32),
        pltpu.VMEM((16, 16, half), BF16),
        pltpu.VMEM((2, 4, 16, half), BF16),
        pltpu.VMEM((4, 16, half), BF16),
        pltpu.VMEM((4, 16, half), BF16),
        pltpu.VMEM((4, 16, half), BF16),
    ]


CHAIN_REFS = 16
COPIES = 96


def kernel(tok_ref, win_ref, wout_ref, gout_ref, out_ref, *scratch):
    win, wout, raw, own, gathered, slope_out, slope_in = scratch[:7]
    h = Chain(scratch[7:7 + CHAIN_REFS])
    g = Chain(scratch[7 + CHAIN_REFS:7 + 2 * CHAIN_REFS])
    local_sem, send_sem, recv_sem = scratch[7 + 2 * CHAIN_REFS:]
    width = tok_ref.shape[1]
    half = width // 2

    row, col = lax.axis_index("row"), lax.axis_index("col")
    y, x = lax.div(row, 4), lax.rem(row, 4)
    z, core = lax.div(col, 2), lax.rem(col, 2)

    def at_x(step):
        return (y * 4 + lax.rem(x + step + 4, 4), col)

    def at_y(step):
        return (lax.rem(y + step + 4, 4) * 4 + x, col)

    def at_z(step):
        return (row, lax.rem(z + step + 16, 16) * 2 + core)

    other_core = (row, z * 2 + 1 - core)
    turned = (x * 4 + y, col)
    same = lax.div(3 - lax.max(x - y, y - x), 3)

    moves = [(tok_ref, raw.at[0]), (gout_ref, raw.at[1])]
    for part in range(2):
        cut = pl.ds(part * width, width)
        moves.append((win_ref.at[:, cut], win.at[2 * core + part]))
    for part in range(2):
        cut = pl.ds(part * width, width)
        moves.append((wout_ref.at[cut, :], wout.at[2 * core + part]))
    local = [pltpu.make_async_copy(src, dst, local_sem.at[n]) for n, (src, dst) in enumerate(moves)]
    for copy in local:
        copy.start()

    partners = [other_core, (x * 4 + y, z * 2 + core + same * (1 - 2 * core))]
    partners += [at_x(step) for step in (1, -1, 2)]
    partners += [at_y(step) for step in (1, -1, 2)]
    partners += [at_z(step) for step in (1, -1, 2, -2, 6, -6)]
    barrier = pltpu.get_barrier_semaphore()
    for partner in partners:
        pl.semaphore_signal(barrier, inc=1, device_id=partner, device_id_type=MESH)

    empty = jnp.zeros((2, width), F32)
    for n in range(2):
        local[n].wait()
        whole = jnp.concatenate([raw[n].astype(F32), empty], axis=0)
        folded = jnp.concatenate([whole[:, :half], whole[:, half:]], axis=0)
        own[n] = folded.astype(BF16)

    pl.semaphore_wait(barrier, len(partners))

    started = []

    def send(src, dst, device):
        n = len(started)
        copy = pltpu.make_async_remote_copy(
            src_ref=src, dst_ref=dst, send_sem=send_sem.at[n], recv_sem=recv_sem.at[n],
            device_id=device, device_id_type=MESH,
        )
        copy.start()
        started.append(copy)
        return copy

    def arrived(copies):
        for copy in copies:
            copy.wait_recv()

    slot = lax.rem(z, 4) * 4 + lax.div(z, 4)
    held = lax.rem(z + 2, 4) * 4

    def gather_far(n):
        return [send(own.at[n], gathered.at[n, slot], at_z(step)) for step in FAR]

    def gather_near(n):
        out = []
        for step, first, count in ((2, 0, 2), (-2, 2, 2), (1, 0, 4), (-1, 0, 4)):
            piece = gathered.at[n, pl.ds(held + first, count)]
            out.append(send(piece, piece, at_z(step)))
        return out

    far_in = [gather_far(0), gather_far(1)]
    pushed = []
    for part in range(2):
        src = win_ref.at[:, pl.ds(part * width, width)]
        pushed.append(send(src, win.at[2 * core + part], other_core))
    near_in = []
    for n in range(2):
        arrived(far_in[n])
        near_in.append(gather_near(n))
    for part in range(2):
        src = wout_ref.at[pl.ds(part * width, width)]
        pushed.append(send(src, wout.at[2 * core + part], other_core))

    def squeeze(c, n):
        blocks = gathered[n].astype(F32)
        left = blocks[:, :8, :].reshape(128, half)
        right = blocks[:, 8:, :].reshape(128, half)
        spread = jnp.concatenate([left, right], axis=1).astype(BF16)
        at = lax.broadcasted_iota(jnp.int32, (96, 128), 0)
        come = lax.broadcasted_iota(jnp.int32, (96, 128), 1)
        within = come & 7
        pick = jnp.where((within < 6) & (at == 6 * (come >> 3) + within), 1.0, 0.0).astype(BF16)
        c.x[...] = jnp.dot(pick, spread, preferred_element_type=F32).astype(BF16)

    def expander():
        at = lax.broadcasted_iota(jnp.int32, (128, 96), 0)
        come = lax.broadcasted_iota(jnp.int32, (128, 96), 1)
        within = at & 7
        return jnp.where((within < 6) & (come == 6 * (at >> 3) + within), 1.0, 0.0).astype(BF16)

    def quarters(value):
        return [
            value[48 * up:48 * up + 48, half * side:half * side + half]
            for up in range(2) for side in range(2)
        ]

    def relays(c, ahead):
        c.send1[2] = c.part[2].astype(BF16)
        return [
            send(c.send1.at[2, pl.ds(0, 2)], c.relay.at[0], ahead(1)),
            send(c.send1.at[2, pl.ds(2, 2)], c.relay.at[1], ahead(-1)),
        ]

    def direct_up(c, ahead):
        c.send1[1, 2:4] = c.part[1, 2:4].astype(BF16)
        return [send(c.send1.at[1, pl.ds(2, 2)], c.near1.at[0, pl.ds(2, 2)], ahead(1))]

    def direct_down(c, ahead):
        c.send1[3, 0:2] = c.part[3, 0:2].astype(BF16)
        return [send(c.send1.at[3, pl.ds(0, 2)], c.near1.at[1, pl.ds(0, 2)], ahead(-1))]

    def passed_on(c, got, ahead):
        arrived(got[:1])
        c.send1[1, 0:2] = (c.part[1, 0:2] + c.relay[0].astype(F32)).astype(BF16)
        out = [send(c.send1.at[1, pl.ds(0, 2)], c.near1.at[0, pl.ds(0, 2)], ahead(1))]
        arrived(got[1:])
        c.send1[3, 2:4] = (c.part[3, 2:4] + c.relay[1].astype(F32)).astype(BF16)
        out.append(send(c.send1.at[3, pl.ds(2, 2)], c.near1.at[1, pl.ds(2, 2)], ahead(-1)))
        return out

    def second_sum(c, got, ahead, place):
        arrived(got)
        c.total[...] = c.part[0] + c.near1[0].astype(F32) + c.near1[1].astype(F32)
        c.send2[...] = c.total[...].astype(BF16)
        out = []
        for n, step in enumerate((2, 1, -1)):
            there = lax.rem(place + step + 4, 4)
            out.append(send(c.send2.at[there], c.recv2.at[n], ahead(step)))
        return out

    def summed(c, got, place):
        arrived(got)
        return (
            c.total[place] + c.recv2[0].astype(F32) + c.recv2[1].astype(F32) + c.recv2[2].astype(F32)
        )

    arrived(near_in[0])
    squeeze(h, 0)
    for copy in local[2:4]:
        copy.wait()
    arrived(pushed[:2])

    def keep(c, rel, got):
        for v, piece in enumerate(quarters(got)):
            c.part[rel, v] = piece

    def hidden_part(rel):
        keep(h, rel, jnp.dot(h.x[...], win[lax.rem(x + rel, 4)], preferred_element_type=F32))

    def grad_part(rel):
        keep(g, rel, against(g.x[...], wout[lax.rem(y + rel, 4)]))

    hidden_part(2)
    relay_h = relays(h, at_x)
    hidden_part(1)
    direct_h = direct_up(h, at_x)
    hidden_part(3)
    direct_h += direct_down(h, at_x)
    hidden_part(0)

    arrived(near_in[1])
    squeeze(g, 1)
    direct_h += passed_on(h, relay_h, at_x)
    for copy in local[4:]:
        copy.wait()
    arrived(pushed[2:])

    grad_part(2)
    relay_g = relays(g, at_y)
    grad_part(1)
    direct_g = direct_up(g, at_y)
    grad_part(3)
    direct_g += direct_down(g, at_y)
    second_h = second_sum(h, direct_h, at_y, y)
    grad_part(0)
    direct_g += passed_on(g, relay_g, at_y)
    hidden = summed(h, second_h, y)
    act, slope = gelu_and_slope(hidden)
    h.all[x, y] = act.astype(BF16)

    def spread_first(c, chunk, place, ahead):
        piece = c.all.at[chunk, place]
        return [send(piece, piece, ahead(step)) for step in (2, 1, -1)]

    def spread_second(c, got, chunk, ahead):
        arrived(got)
        low, high = c.all.at[chunk, pl.ds(0, 2)], c.all.at[chunk, pl.ds(2, 2)]
        return [
            send(low, low, ahead(1)),
            send(high, high, ahead(-1)),
            send(high, high, ahead(1)),
            send(low, low, ahead(-1)),
        ]

    def spread_third(c, got, place, ahead):
        arrived(got[:1])
        piece = c.all.at[lax.rem(place + 3, 4), pl.ds(0, 2)]
        out = [send(piece, piece, ahead(1))]
        arrived(got[1:2])
        piece = c.all.at[lax.rem(place + 1, 4), pl.ds(2, 2)]
        out.append(send(piece, piece, ahead(-1)))
        return out

    first_h = spread_first(h, x, y, at_y)
    slope_out[...] = slope
    turn = pltpu.make_async_remote_copy(
        src_ref=slope_out, dst_ref=slope_in, send_sem=send_sem.at[COPIES - 1],
        recv_sem=recv_sem.at[COPIES - 1], device_id=turned, device_id_type=MESH,
    )

    @pl.when(x != y)
    def _():
        turn.start()

    @pl.when(x == y)
    def _():
        slope_in[...] = slope_out[...]

    second_g = second_sum(g, direct_g, at_x, x)
    spread_h = spread_second(h, first_h, x, at_x)
    grad_act = summed(g, second_g, x)

    @pl.when(x != y)
    def _():
        turn.wait_recv()

    g.all[y, x] = (grad_act * slope_in[...]).astype(BF16)
    first_g = spread_first(g, y, x, at_x)

    expand = expander()

    def widened(blocks):
        rows = [jnp.concatenate([blocks[2 * up], blocks[2 * up + 1]], axis=1) for up in range(2)]
        return jnp.dot(
            expand, jnp.concatenate(rows, axis=0), preferred_element_type=F32
        ).astype(BF16)

    def mixed_part(rel):
        u = lax.rem(x + rel, 4)
        return jnp.dot(widened(h.all[u]), wout[u], preferred_element_type=F32)

    def grad_in_part(rel):
        u = lax.rem(y + rel, 4)
        return against(widened(g.all[u]), win[u])

    h.acc[...] = mixed_part(0)
    spread_h2 = spread_third(h, spread_h, x, at_x)
    spread_g = spread_second(g, first_g, y, at_y)
    arrived(spread_h[2:])
    h.acc[...] += mixed_part(1)
    h.acc[...] += mixed_part(3)
    spread_g2 = spread_third(g, spread_g, y, at_y)
    arrived(spread_h2)
    h.acc[...] += mixed_part(2)

    def to_near(c):
        acc = c.acc[...]
        left = acc[:, :half].reshape(16, 8, half)
        right = acc[:, half:].reshape(16, 8, half)
        blocks = jnp.concatenate([left, right], axis=1)
        c.blocks[...] = blocks
        c.sendz[...] = blocks.astype(BF16)
        up = c.sendz.at[pl.ds(lax.rem(z + 3, 4) * 4, 4)]
        down = c.sendz.at[pl.ds(lax.rem(z + 1, 4) * 4, 4)]
        here = lax.rem(z, 4) * 4
        return [
            send(c.sendz.at[pl.ds(here, 2)], c.nearz2.at[pl.ds(0, 2)], at_z(2)),
            send(c.sendz.at[pl.ds(here + 2, 2)], c.nearz2.at[pl.ds(2, 2)], at_z(-2)),
            send(up, c.nearz.at[0], at_z(1)),
            send(down, c.nearz.at[1], at_z(-1)),
        ]

    def to_far(c, got):
        arrived(got)
        total = c.blocks[pl.ds(held, 4)] + c.nearz[0].astype(F32)
        total = total + c.nearz[1].astype(F32) + c.nearz2[...].astype(F32)
        c.sendf[...] = total.astype(BF16)
        out = []
        for n, step in enumerate(FAR):
            there = lax.div(lax.rem(z + step + 16, 16), 4)
            out.append(send(c.sendf.at[there], c.recvf.at[n], at_z(step)))
        return out

    def finish(c, got, n):
        arrived(got)
        total = c.recvf[0].astype(F32) + c.recvf[1].astype(F32)
        total = total + c.recvf[2].astype(F32) + c.recvf[3].astype(F32)
        whole = jnp.concatenate([total[:8], total[8:]], axis=1)
        out_ref[n] = whole[:6].astype(BF16)

    near_h = to_near(h)
    g.acc[...] = grad_in_part(0)
    arrived(spread_g[2:])
    g.acc[...] += grad_in_part(1)
    g.acc[...] += grad_in_part(3)
    arrived(spread_g2)
    g.acc[...] += grad_in_part(2)
    near_g = to_near(g)
    far_h = to_far(h, near_h)
    far_g = to_far(g, near_g)
    late = near_g + far_h + far_g
    for copy in started:
        if not any(copy is other for other in late):
            copy.wait_send()

    @pl.when(x != y)
    def _():
        turn.wait_send()

    finish(h, far_h, 0)
    finish(g, far_g, 1)

    for copy in late:
        copy.wait_send()


def shards(tokens, w_in, w_out, grad_out):
    rows, width = tokens.shape
    half = width // 2
    out = jax.ShapeDtypeStruct((2, rows, width), BF16)
    vmem = pl.BlockSpec(memory_space=pltpu.VMEM)
    hbm = pl.BlockSpec(memory_space=pl.ANY)
    both = pl.pallas_call(
        kernel,
        out_shape=out,
        in_specs=[hbm, hbm, hbm, hbm],
        out_specs=vmem,
        scratch_shapes=[
            pltpu.VMEM((4, width, width), BF16),
            pltpu.VMEM((4, width, width), BF16),
            pltpu.VMEM((2,) + tokens.shape, BF16),
            pltpu.VMEM((2, 16, half), BF16),
            pltpu.VMEM((2, 16, 16, half), BF16),
            pltpu.VMEM((48, half), F32),
            pltpu.VMEM((48, half), F32),
        ]
        + chain_scratch(half, width)
        + chain_scratch(half, width)
        + [
            pltpu.SemaphoreType.DMA((6,)),
            pltpu.SemaphoreType.DMA((COPIES,)),
            pltpu.SemaphoreType.DMA((COPIES,)),
        ],
        compiler_params=pltpu.CompilerParams(
            collective_id=0, has_side_effects=True, vmem_limit_bytes=62 * 1024 * 1024
        ),
        cost_estimate=pl.CostEstimate(
            flops=8 * 192 * width * w_in.shape[1], bytes_accessed=4 * w_in.size, transcendentals=0
        ),
    )(tokens, w_in, w_out, grad_out)
    return both[0], both[1]


def solution(mesh):
    placed = (P("col", "row"), P("row", "col"), P("col", "row"), P("col", "row"))
    return jax.shard_map(
        shards,
        mesh=mesh,
        in_specs=placed,
        out_specs=(P("col", "row"), P("col", "row")),
        check_vma=False,
    )
```

```python
import jax
import jax.numpy as jnp
from jax import lax
from jax.experimental import pallas as pl
from jax.experimental.pallas import tpu as pltpu
from jax.sharding import PartitionSpec as P

gelu_scale = 0.7978845608028654
cubic_coef = 0.044715

F32, BF16 = jnp.float32, jnp.bfloat16
MESH = pl.DeviceIdType.MESH
FAR = (6, -6, 2, -2)


def gelu_and_slope(values):
    squared = values * values
    bent = jnp.tanh(gelu_scale * (values + cubic_coef * squared * values))
    act = 0.5 * values * (1.0 + bent)
    slope = 0.5 * (1.0 + bent) + 0.5 * values * (1.0 - bent * bent) * gelu_scale * (
        1.0 + 3.0 * cubic_coef * squared
    )
    return act, slope


def against(left, right):
    return lax.dot_general(left, right, (((1,), (1,)), ((), ())), preferred_element_type=F32)


class Chain:
    def __init__(self, refs):
        (self.x, self.part, self.send1, self.relay, self.near1,
         self.total, self.send2, self.recv2, self.all, self.acc, self.blocks, self.sendz,
         self.nearz, self.nearz2, self.sendf, self.recvf) = refs


def chain_scratch(half, width):
    block = (48, half)
    return [
        pltpu.VMEM((96, width), BF16),
        pltpu.VMEM((4, 4) + block, F32),
        pltpu.VMEM((4, 4) + block, BF16),
        pltpu.VMEM((2, 2) + block, BF16),
        pltpu.VMEM((2, 4) + block, BF16),
        pltpu.VMEM((4,) + block, F32),
        pltpu.VMEM((4,) + block, BF16),
        pltpu.VMEM((3,) + block, BF16),
        pltpu.VMEM((4, 4) + block, BF16),
        pltpu.VMEM((128, width), F32),
        pltpu.VMEM((16, 16, half), F32),
        pltpu.VMEM((16, 16, half), BF16),
        pltpu.VMEM((2, 4, 16, half), BF16),
        pltpu.VMEM((4, 16, half), BF16),
        pltpu.VMEM((4, 16, half), BF16),
        pltpu.VMEM((4, 16, half), BF16),
    ]


CHAIN_REFS = 16
COPIES = 96


def kernel(tok_ref, win_ref, wout_ref, gout_ref, out_ref, *scratch):
    win, wout, raw, own, gathered, slope_out, slope_in = scratch[:7]
    h = Chain(scratch[7:7 + CHAIN_REFS])
    g = Chain(scratch[7 + CHAIN_REFS:7 + 2 * CHAIN_REFS])
    local_sem, send_sem, recv_sem = scratch[7 + 2 * CHAIN_REFS:]
    width = tok_ref.shape[1]
    half = width // 2

    row, col = lax.axis_index("row"), lax.axis_index("col")
    y, x = lax.div(row, 4), lax.rem(row, 4)
    z, core = lax.div(col, 2), lax.rem(col, 2)

    def at_x(step):
        return (y * 4 + lax.rem(x + step + 4, 4), col)

    def at_y(step):
        return (lax.rem(y + step + 4, 4) * 4 + x, col)

    def at_z(step):
        return (row, lax.rem(z + step + 16, 16) * 2 + core)

    other_core = (row, z * 2 + 1 - core)
    turned = (x * 4 + y, col)
    same = lax.div(3 - lax.max(x - y, y - x), 3)

    moves = [(tok_ref, raw.at[0]), (gout_ref, raw.at[1])]
    for part in range(2):
        cut = pl.ds(part * width, width)
        moves.append((win_ref.at[:, cut], win.at[2 * core + part]))
    for part in range(2):
        cut = pl.ds(part * width, width)
        moves.append((wout_ref.at[cut, :], wout.at[2 * core + part]))
    local = [pltpu.make_async_copy(src, dst, local_sem.at[n]) for n, (src, dst) in enumerate(moves)]
    for copy in local:
        copy.start()

    partners = [at_z(step) for step in (6, -6, 2, -2, 1, -1)]
    partners += [other_core, (x * 4 + y, z * 2 + core + same * (1 - 2 * core))]
    partners += [at_x(step) for step in (2, 1, -1)]
    partners += [at_y(step) for step in (2, 1, -1)]
    barrier = pltpu.get_barrier_semaphore()
    for partner in partners:
        pl.semaphore_signal(barrier, inc=1, device_id=partner, device_id_type=MESH)

    empty = jnp.zeros((2, width), F32)
    for n in range(2):
        local[n].wait()
        whole = jnp.concatenate([raw[n].astype(F32), empty], axis=0)
        folded = jnp.concatenate([whole[:, :half], whole[:, half:]], axis=0)
        own[n] = folded.astype(BF16)

    pl.semaphore_wait(barrier, len(partners))

    started = []

    def send(src, dst, device):
        n = len(started)
        copy = pltpu.make_async_remote_copy(
            src_ref=src, dst_ref=dst, send_sem=send_sem.at[n], recv_sem=recv_sem.at[n],
            device_id=device, device_id_type=MESH,
        )
        copy.start()
        started.append(copy)
        return copy

    def arrived(copies):
        for copy in copies:
            copy.wait_recv()

    slot = lax.rem(z, 4) * 4 + lax.div(z, 4)
    held = lax.rem(z + 2, 4) * 4

    def gather_far(n):
        return [send(own.at[n], gathered.at[n, slot], at_z(step)) for step in FAR]

    def gather_near(n):
        out = []
        for step, first, count in ((2, 0, 2), (-2, 2, 2), (1, 0, 4), (-1, 0, 4)):
            piece = gathered.at[n, pl.ds(held + first, count)]
            out.append(send(piece, piece, at_z(step)))
        return out

    far_in = [gather_far(0), gather_far(1)]
    pushed = []
    for part in range(2):
        for lot in range(2):
            rows = pl.ds(lot * half, half)
            src = win_ref.at[rows, pl.ds(part * width, width)]
            pushed.append(send(src, win.at[2 * core + part, rows], other_core))
    near_in = []
    for n in range(2):
        arrived(far_in[n])
        near_in.append(gather_near(n))
    for part in range(2):
        for lot in range(2):
            src = wout_ref.at[pl.ds(part * width + lot * half, half)]
            pushed.append(send(src, wout.at[2 * core + part, pl.ds(lot * half, half)], other_core))

    def squeeze(c, n):
        blocks = gathered[n].astype(F32)
        left = blocks[:, :8, :].reshape(128, half)
        right = blocks[:, 8:, :].reshape(128, half)
        spread = jnp.concatenate([left, right], axis=1).astype(BF16)
        at = lax.broadcasted_iota(jnp.int32, (96, 128), 0)
        come = lax.broadcasted_iota(jnp.int32, (96, 128), 1)
        within = come & 7
        pick = jnp.where((within < 6) & (at == 6 * (come >> 3) + within), 1.0, 0.0).astype(BF16)
        c.x[...] = jnp.dot(pick, spread, preferred_element_type=F32).astype(BF16)

    def expander():
        at = lax.broadcasted_iota(jnp.int32, (128, 96), 0)
        come = lax.broadcasted_iota(jnp.int32, (128, 96), 1)
        within = at & 7
        return jnp.where((within < 6) & (come == 6 * (at >> 3) + within), 1.0, 0.0).astype(BF16)

    def quarters(value):
        return [
            value[48 * up:48 * up + 48, half * side:half * side + half]
            for up in range(2) for side in range(2)
        ]

    def relays(c, got, ahead):
        for v in range(4):
            c.send1[2, v] = got[v].astype(BF16)
        return [
            send(c.send1.at[2, pl.ds(0, 2)], c.relay.at[0], ahead(1)),
            send(c.send1.at[2, pl.ds(2, 2)], c.relay.at[1], ahead(-1)),
        ]

    def direct_up(c, got, ahead):
        for v in (2, 3):
            c.send1[1, v] = got[v].astype(BF16)
        out = [send(c.send1.at[1, pl.ds(2, 2)], c.near1.at[0, pl.ds(2, 2)], ahead(1))]
        for v in (0, 1):
            c.part[1, v] = got[v]
        return out

    def direct_down(c, got, ahead):
        for v in (0, 1):
            c.send1[3, v] = got[v].astype(BF16)
        out = [send(c.send1.at[3, pl.ds(0, 2)], c.near1.at[1, pl.ds(0, 2)], ahead(-1))]
        for v in (2, 3):
            c.part[3, v] = got[v]
        return out

    def stay(c, got):
        for v in range(4):
            c.part[0, v] = got[v]

    def passed_on(c, got, ahead):
        arrived(got[:1])
        c.send1[1, 0:2] = (c.part[1, 0:2] + c.relay[0].astype(F32)).astype(BF16)
        out = [send(c.send1.at[1, pl.ds(0, 2)], c.near1.at[0, pl.ds(0, 2)], ahead(1))]
        arrived(got[1:])
        c.send1[3, 2:4] = (c.part[3, 2:4] + c.relay[1].astype(F32)).astype(BF16)
        out.append(send(c.send1.at[3, pl.ds(2, 2)], c.near1.at[1, pl.ds(2, 2)], ahead(-1)))
        return out

    def second_sum(c, got, ahead, place):
        arrived(got)
        c.total[...] = c.part[0] + c.near1[0].astype(F32) + c.near1[1].astype(F32)
        c.send2[...] = c.total[...].astype(BF16)
        out = []
        for n, step in enumerate((2, 1, -1)):
            there = lax.rem(place + step + 4, 4)
            out.append(send(c.send2.at[there], c.recv2.at[n], ahead(step)))
        return out

    def summed(c, got, place):
        arrived(got)
        return (
            c.total[place] + c.recv2[0].astype(F32) + c.recv2[1].astype(F32) + c.recv2[2].astype(F32)
        )

    arrived(near_in[0])
    squeeze(h, 0)
    for copy in local[2:4]:
        copy.wait()
    arrived(pushed[:4])

    def hidden_part(rel):
        return quarters(jnp.dot(h.x[...], win[lax.rem(x + rel, 4)], preferred_element_type=F32))

    def grad_part(rel):
        return quarters(against(g.x[...], wout[lax.rem(y + rel, 4)]))

    relay_h = relays(h, hidden_part(2), at_x)
    direct_h = direct_up(h, hidden_part(1), at_x)
    direct_h += direct_down(h, hidden_part(3), at_x)
    stay(h, hidden_part(0))

    arrived(near_in[1])
    squeeze(g, 1)
    for copy in local[4:]:
        copy.wait()
    arrived(pushed[4:])

    relay_g = relays(g, grad_part(2), at_y)
    direct_h += passed_on(h, relay_h, at_x)
    direct_g = direct_up(g, grad_part(1), at_y)
    direct_g += direct_down(g, grad_part(3), at_y)
    stay(g, grad_part(0))
    direct_g += passed_on(g, relay_g, at_y)
    second_h = second_sum(h, direct_h, at_y, y)
    hidden = summed(h, second_h, y)
    act, slope = gelu_and_slope(hidden)
    h.all[x, y] = act.astype(BF16)

    def spread_first(c, chunk, place, ahead):
        piece = c.all.at[chunk, place]
        return [send(piece, piece, ahead(step)) for step in (2, 1, -1)]

    def spread_second(c, got, chunk, ahead):
        arrived(got)
        low, high = c.all.at[chunk, pl.ds(0, 2)], c.all.at[chunk, pl.ds(2, 2)]
        return [
            send(low, low, ahead(1)),
            send(high, high, ahead(-1)),
            send(high, high, ahead(1)),
            send(low, low, ahead(-1)),
        ]

    def spread_third(c, got, place, ahead):
        arrived(got[:1])
        piece = c.all.at[lax.rem(place + 3, 4), pl.ds(0, 2)]
        out = [send(piece, piece, ahead(1))]
        arrived(got[1:2])
        piece = c.all.at[lax.rem(place + 1, 4), pl.ds(2, 2)]
        out.append(send(piece, piece, ahead(-1)))
        return out

    first_h = spread_first(h, x, y, at_y)
    slope_out[...] = slope
    turn = pltpu.make_async_remote_copy(
        src_ref=slope_out, dst_ref=slope_in, send_sem=send_sem.at[COPIES - 1],
        recv_sem=recv_sem.at[COPIES - 1], device_id=turned, device_id_type=MESH,
    )

    @pl.when(x != y)
    def _():
        turn.start()

    @pl.when(x == y)
    def _():
        slope_in[...] = slope_out[...]

    second_g = second_sum(g, direct_g, at_x, x)
    spread_h = spread_second(h, first_h, x, at_x)
    grad_act = summed(g, second_g, x)

    @pl.when(x != y)
    def _():
        turn.wait_recv()

    g.all[y, x] = (grad_act * slope_in[...]).astype(BF16)
    first_g = spread_first(g, y, x, at_x)

    expand = expander()

    def widened(blocks):
        rows = [jnp.concatenate([blocks[2 * up], blocks[2 * up + 1]], axis=1) for up in range(2)]
        return jnp.dot(
            expand, jnp.concatenate(rows, axis=0), preferred_element_type=F32
        ).astype(BF16)

    def mixed_part(rel):
        u = lax.rem(x + rel, 4)
        return jnp.dot(widened(h.all[u]), wout[u], preferred_element_type=F32)

    def grad_in_part(rel):
        u = lax.rem(y + rel, 4)
        return against(widened(g.all[u]), win[u])

    h.acc[...] = mixed_part(0)
    spread_h2 = spread_third(h, spread_h, x, at_x)
    spread_g = spread_second(g, first_g, y, at_y)
    arrived(spread_h[2:])
    h.acc[...] += mixed_part(1)
    h.acc[...] += mixed_part(3)
    spread_g2 = spread_third(g, spread_g, y, at_y)
    arrived(spread_h2)
    h.acc[...] += mixed_part(2)

    def to_near(c):
        acc = c.acc[...]
        left = acc[:, :half].reshape(16, 8, half)
        right = acc[:, half:].reshape(16, 8, half)
        blocks = jnp.concatenate([left, right], axis=1)
        c.blocks[...] = blocks
        c.sendz[...] = blocks.astype(BF16)
        up = c.sendz.at[pl.ds(lax.rem(z + 3, 4) * 4, 4)]
        down = c.sendz.at[pl.ds(lax.rem(z + 1, 4) * 4, 4)]
        here = lax.rem(z, 4) * 4
        return [
            send(c.sendz.at[pl.ds(here, 2)], c.nearz2.at[pl.ds(0, 2)], at_z(2)),
            send(c.sendz.at[pl.ds(here + 2, 2)], c.nearz2.at[pl.ds(2, 2)], at_z(-2)),
            send(up, c.nearz.at[0], at_z(1)),
            send(down, c.nearz.at[1], at_z(-1)),
        ]

    def to_far(c, got):
        arrived(got)
        total = c.blocks[pl.ds(held, 4)] + c.nearz[0].astype(F32)
        total = total + c.nearz[1].astype(F32) + c.nearz2[...].astype(F32)
        c.sendf[...] = total.astype(BF16)
        out = []
        for n, step in enumerate(FAR):
            there = lax.div(lax.rem(z + step + 16, 16), 4)
            out.append(send(c.sendf.at[there], c.recvf.at[n], at_z(step)))
        return out

    def finish(c, got, n):
        arrived(got)
        total = c.recvf[0].astype(F32) + c.recvf[1].astype(F32)
        total = total + c.recvf[2].astype(F32) + c.recvf[3].astype(F32)
        whole = jnp.concatenate([total[:8], total[8:]], axis=1)
        out_ref[n] = whole[:6].astype(BF16)

    near_h = to_near(h)
    g.acc[...] = grad_in_part(0)
    arrived(spread_g[2:])
    g.acc[...] += grad_in_part(1)
    g.acc[...] += grad_in_part(3)
    arrived(spread_g2)
    g.acc[...] += grad_in_part(2)
    near_g = to_near(g)
    far_h = to_far(h, near_h)
    far_g = to_far(g, near_g)
    late = near_g + far_h + far_g
    for copy in started:
        if not any(copy is other for other in late):
            copy.wait_send()

    @pl.when(x != y)
    def _():
        turn.wait_send()

    finish(h, far_h, 0)
    finish(g, far_g, 1)

    for copy in late:
        copy.wait_send()


def shards(tokens, w_in, w_out, grad_out):
    rows, width = tokens.shape
    half = width // 2
    out = jax.ShapeDtypeStruct((2, rows, width), BF16)
    vmem = pl.BlockSpec(memory_space=pltpu.VMEM)
    hbm = pl.BlockSpec(memory_space=pl.ANY)
    both = pl.pallas_call(
        kernel,
        out_shape=out,
        in_specs=[hbm, hbm, hbm, hbm],
        out_specs=vmem,
        scratch_shapes=[
            pltpu.VMEM((4, width, width), BF16),
            pltpu.VMEM((4, width, width), BF16),
            pltpu.VMEM((2,) + tokens.shape, BF16),
            pltpu.VMEM((2, 16, half), BF16),
            pltpu.VMEM((2, 16, 16, half), BF16),
            pltpu.VMEM((48, half), F32),
            pltpu.VMEM((48, half), F32),
        ]
        + chain_scratch(half, width)
        + chain_scratch(half, width)
        + [
            pltpu.SemaphoreType.DMA((6,)),
            pltpu.SemaphoreType.DMA((COPIES,)),
            pltpu.SemaphoreType.DMA((COPIES,)),
        ],
        compiler_params=pltpu.CompilerParams(
            collective_id=0, has_side_effects=True, vmem_limit_bytes=62 * 1024 * 1024
        ),
        cost_estimate=pl.CostEstimate(
            flops=8 * 192 * width * w_in.shape[1], bytes_accessed=4 * w_in.size, transcendentals=0
        ),
    )(tokens, w_in, w_out, grad_out)
    return both[0], both[1]


def solution(mesh):
    placed = (P("col", "row"), P("row", "col"), P("col", "row"), P("col", "row"))
    return jax.shard_map(
        shards,
        mesh=mesh,
        in_specs=placed,
        out_specs=(P("col", "row"), P("col", "row")),
        check_vma=False,
    )
```

```python
import jax
import jax.numpy as jnp
from jax import lax
from jax.experimental import pallas as pl
from jax.experimental.pallas import tpu as pltpu
from jax.sharding import PartitionSpec as P

gelu_scale = 0.7978845608028654
cubic_coef = 0.044715

F32, BF16 = jnp.float32, jnp.bfloat16
MESH = pl.DeviceIdType.MESH
FAR = (6, -6, 2, -2)


def gelu_and_slope(values):
    squared = values * values
    bent = jnp.tanh(gelu_scale * (values + cubic_coef * squared * values))
    act = 0.5 * values * (1.0 + bent)
    slope = 0.5 * (1.0 + bent) + 0.5 * values * (1.0 - bent * bent) * gelu_scale * (
        1.0 + 3.0 * cubic_coef * squared
    )
    return act, slope


def against(left, right):
    return lax.dot_general(left, right, (((1,), (1,)), ((), ())), preferred_element_type=F32)


class Chain:
    def __init__(self, refs):
        (self.x, self.part, self.send1, self.relay, self.near1,
         self.total, self.send2, self.recv2, self.all, self.acc, self.blocks, self.sendz,
         self.nearz, self.nearz2, self.sendf, self.recvf) = refs


def chain_scratch(half, width):
    block = (48, half)
    return [
        pltpu.VMEM((96, width), BF16),
        pltpu.VMEM((4, 4) + block, F32),
        pltpu.VMEM((4, 4) + block, BF16),
        pltpu.VMEM((2, 2) + block, BF16),
        pltpu.VMEM((2, 4) + block, BF16),
        pltpu.VMEM((4,) + block, F32),
        pltpu.VMEM((4,) + block, BF16),
        pltpu.VMEM((3,) + block, BF16),
        pltpu.VMEM((4, 4) + block, BF16),
        pltpu.VMEM((128, width), F32),
        pltpu.VMEM((16, 16, half), F32),
        pltpu.VMEM((16, 16, half), BF16),
        pltpu.VMEM((2, 4, 16, half), BF16),
        pltpu.VMEM((4, 16, half), BF16),
        pltpu.VMEM((4, 16, half), BF16),
        pltpu.VMEM((4, 16, half), BF16),
    ]


CHAIN_REFS = 16
COPIES = 96


def kernel(tok_ref, win_ref, wout_ref, gout_ref, out_ref, *scratch):
    win, wout, raw, own, gathered, slope_out, slope_in = scratch[:7]
    h = Chain(scratch[7:7 + CHAIN_REFS])
    g = Chain(scratch[7 + CHAIN_REFS:7 + 2 * CHAIN_REFS])
    local_sem, send_sem, recv_sem = scratch[7 + 2 * CHAIN_REFS:]
    width = tok_ref.shape[1]
    half = width // 2

    row, col = lax.axis_index("row"), lax.axis_index("col")
    y, x = lax.div(row, 4), lax.rem(row, 4)
    z, core = lax.div(col, 2), lax.rem(col, 2)

    def at_x(step):
        return (y * 4 + lax.rem(x + step + 4, 4), col)

    def at_y(step):
        return (lax.rem(y + step + 4, 4) * 4 + x, col)

    def at_z(step):
        return (row, lax.rem(z + step + 16, 16) * 2 + core)

    other_core = (row, z * 2 + 1 - core)
    turned = (x * 4 + y, col)
    same = lax.div(3 - lax.max(x - y, y - x), 3)

    moves = [(tok_ref, raw.at[0]), (gout_ref, raw.at[1])]
    for part in range(2):
        cut = pl.ds(part * width, width)
        moves.append((win_ref.at[:, cut], win.at[2 * core + part]))
    for part in range(2):
        cut = pl.ds(part * width, width)
        moves.append((wout_ref.at[cut, :], wout.at[2 * core + part]))
    local = [pltpu.make_async_copy(src, dst, local_sem.at[n]) for n, (src, dst) in enumerate(moves)]
    for copy in local:
        copy.start()

    partners = [at_z(step) for step in (6, -6, 2, -2, 1, -1)]
    partners += [other_core, (x * 4 + y, z * 2 + core + same * (1 - 2 * core))]
    partners += [at_x(step) for step in (2, 1, -1)]
    partners += [at_y(step) for step in (2, 1, -1)]
    barrier = pltpu.get_barrier_semaphore()
    for partner in partners:
        pl.semaphore_signal(barrier, inc=1, device_id=partner, device_id_type=MESH)

    empty = jnp.zeros((2, width), F32)
    for n in range(2):
        local[n].wait()
        whole = jnp.concatenate([raw[n].astype(F32), empty], axis=0)
        folded = jnp.concatenate([whole[:, :half], whole[:, half:]], axis=0)
        own[n] = folded.astype(BF16)

    pl.semaphore_wait(barrier, len(partners))

    started = []

    def send(src, dst, device):
        n = len(started)
        copy = pltpu.make_async_remote_copy(
            src_ref=src, dst_ref=dst, send_sem=send_sem.at[n], recv_sem=recv_sem.at[n],
            device_id=device, device_id_type=MESH,
        )
        copy.start()
        started.append(copy)
        return copy

    def arrived(copies):
        for copy in copies:
            copy.wait_recv()

    slot = lax.rem(z, 4) * 4 + lax.div(z, 4)
    held = lax.rem(z + 2, 4) * 4

    def gather_far(n):
        return [send(own.at[n], gathered.at[n, slot], at_z(step)) for step in FAR]

    def gather_near(n):
        out = []
        for step, first, count in ((2, 0, 2), (-2, 2, 2), (1, 0, 4), (-1, 0, 4)):
            piece = gathered.at[n, pl.ds(held + first, count)]
            out.append(send(piece, piece, at_z(step)))
        return out

    far_in = [gather_far(0), gather_far(1)]
    pushed = []
    for part in range(2):
        src = win_ref.at[:, pl.ds(part * width, width)]
        pushed.append(send(src, win.at[2 * core + part], other_core))
    for part in range(2):
        src = wout_ref.at[pl.ds(part * width, width)]
        pushed.append(send(src, wout.at[2 * core + part], other_core))
    near_in = []
    for n in range(2):
        arrived(far_in[n])
        near_in.append(gather_near(n))

    def squeeze(c, n):
        blocks = gathered[n].astype(F32)
        left = blocks[:, :8, :].reshape(128, half)
        right = blocks[:, 8:, :].reshape(128, half)
        spread = jnp.concatenate([left, right], axis=1).astype(BF16)
        at = lax.broadcasted_iota(jnp.int32, (96, 128), 0)
        come = lax.broadcasted_iota(jnp.int32, (96, 128), 1)
        within = come & 7
        pick = jnp.where((within < 6) & (at == 6 * (come >> 3) + within), 1.0, 0.0).astype(BF16)
        c.x[...] = jnp.dot(pick, spread, preferred_element_type=F32).astype(BF16)

    def expander():
        at = lax.broadcasted_iota(jnp.int32, (128, 96), 0)
        come = lax.broadcasted_iota(jnp.int32, (128, 96), 1)
        within = at & 7
        return jnp.where((within < 6) & (come == 6 * (at >> 3) + within), 1.0, 0.0).astype(BF16)

    def quarters(value):
        return [
            value[48 * up:48 * up + 48, half * side:half * side + half]
            for up in range(2) for side in range(2)
        ]

    def relays(c, got, ahead):
        for v in range(4):
            c.send1[2, v] = got[v].astype(BF16)
        return [
            send(c.send1.at[2, pl.ds(0, 2)], c.relay.at[0], ahead(1)),
            send(c.send1.at[2, pl.ds(2, 2)], c.relay.at[1], ahead(-1)),
        ]

    def direct_up(c, got, ahead):
        for v in (2, 3):
            c.send1[1, v] = got[v].astype(BF16)
        out = [send(c.send1.at[1, pl.ds(2, 2)], c.near1.at[0, pl.ds(2, 2)], ahead(1))]
        for v in (0, 1):
            c.part[1, v] = got[v]
        return out

    def direct_down(c, got, ahead):
        for v in (0, 1):
            c.send1[3, v] = got[v].astype(BF16)
        out = [send(c.send1.at[3, pl.ds(0, 2)], c.near1.at[1, pl.ds(0, 2)], ahead(-1))]
        for v in (2, 3):
            c.part[3, v] = got[v]
        return out

    def stay(c, got):
        for v in range(4):
            c.part[0, v] = got[v]

    def passed_on(c, got, ahead):
        arrived(got[:1])
        c.send1[1, 0:2] = (c.part[1, 0:2] + c.relay[0].astype(F32)).astype(BF16)
        out = [send(c.send1.at[1, pl.ds(0, 2)], c.near1.at[0, pl.ds(0, 2)], ahead(1))]
        arrived(got[1:])
        c.send1[3, 2:4] = (c.part[3, 2:4] + c.relay[1].astype(F32)).astype(BF16)
        out.append(send(c.send1.at[3, pl.ds(2, 2)], c.near1.at[1, pl.ds(2, 2)], ahead(-1)))
        return out

    def second_sum(c, got, ahead, place):
        arrived(got)
        c.total[...] = c.part[0] + c.near1[0].astype(F32) + c.near1[1].astype(F32)
        c.send2[...] = c.total[...].astype(BF16)
        out = []
        for n, step in enumerate((2, 1, -1)):
            there = lax.rem(place + step + 4, 4)
            out.append(send(c.send2.at[there], c.recv2.at[n], ahead(step)))
        return out

    def summed(c, got, place):
        arrived(got)
        return (
            c.total[place] + c.recv2[0].astype(F32) + c.recv2[1].astype(F32) + c.recv2[2].astype(F32)
        )

    arrived(near_in[0])
    squeeze(h, 0)
    for copy in local[2:4]:
        copy.wait()
    arrived(pushed[:2])

    def hidden_part(rel):
        return quarters(jnp.dot(h.x[...], win[lax.rem(x + rel, 4)], preferred_element_type=F32))

    def grad_part(rel):
        return quarters(against(g.x[...], wout[lax.rem(y + rel, 4)]))

    relay_h = relays(h, hidden_part(2), at_x)
    direct_h = direct_up(h, hidden_part(1), at_x)
    direct_h += direct_down(h, hidden_part(3), at_x)
    stay(h, hidden_part(0))

    arrived(near_in[1])
    squeeze(g, 1)
    direct_h += passed_on(h, relay_h, at_x)
    for copy in local[4:]:
        copy.wait()
    arrived(pushed[2:])

    relay_g = relays(g, grad_part(2), at_y)
    direct_g = direct_up(g, grad_part(1), at_y)
    direct_g += direct_down(g, grad_part(3), at_y)
    second_h = second_sum(h, direct_h, at_y, y)
    stay(g, grad_part(0))
    direct_g += passed_on(g, relay_g, at_y)
    hidden = summed(h, second_h, y)
    act, slope = gelu_and_slope(hidden)
    h.all[x, y] = act.astype(BF16)

    def spread_first(c, chunk, place, ahead):
        piece = c.all.at[chunk, place]
        return [send(piece, piece, ahead(step)) for step in (2, 1, -1)]

    def spread_second(c, got, chunk, ahead):
        arrived(got)
        low, high = c.all.at[chunk, pl.ds(0, 2)], c.all.at[chunk, pl.ds(2, 2)]
        return [
            send(low, low, ahead(1)),
            send(high, high, ahead(-1)),
            send(high, high, ahead(1)),
            send(low, low, ahead(-1)),
        ]

    def spread_third(c, got, place, ahead):
        arrived(got[:1])
        piece = c.all.at[lax.rem(place + 3, 4), pl.ds(0, 2)]
        out = [send(piece, piece, ahead(1))]
        arrived(got[1:2])
        piece = c.all.at[lax.rem(place + 1, 4), pl.ds(2, 2)]
        out.append(send(piece, piece, ahead(-1)))
        return out

    first_h = spread_first(h, x, y, at_y)
    slope_out[...] = slope
    turn = pltpu.make_async_remote_copy(
        src_ref=slope_out, dst_ref=slope_in, send_sem=send_sem.at[COPIES - 1],
        recv_sem=recv_sem.at[COPIES - 1], device_id=turned, device_id_type=MESH,
    )

    @pl.when(x != y)
    def _():
        turn.start()

    @pl.when(x == y)
    def _():
        slope_in[...] = slope_out[...]

    second_g = second_sum(g, direct_g, at_x, x)
    spread_h = spread_second(h, first_h, x, at_x)
    grad_act = summed(g, second_g, x)

    @pl.when(x != y)
    def _():
        turn.wait_recv()

    g.all[y, x] = (grad_act * slope_in[...]).astype(BF16)
    first_g = spread_first(g, y, x, at_x)

    expand = expander()

    def widened(blocks):
        rows = [jnp.concatenate([blocks[2 * up], blocks[2 * up + 1]], axis=1) for up in range(2)]
        return jnp.dot(
            expand, jnp.concatenate(rows, axis=0), preferred_element_type=F32
        ).astype(BF16)

    def mixed_part(rel):
        u = lax.rem(x + rel, 4)
        return jnp.dot(widened(h.all[u]), wout[u], preferred_element_type=F32)

    def grad_in_part(rel):
        u = lax.rem(y + rel, 4)
        return against(widened(g.all[u]), win[u])

    h.acc[...] = mixed_part(0)
    spread_h2 = spread_third(h, spread_h, x, at_x)
    spread_g = spread_second(g, first_g, y, at_y)
    arrived(spread_h[2:])
    h.acc[...] += mixed_part(1)
    h.acc[...] += mixed_part(3)
    spread_g2 = spread_third(g, spread_g, y, at_y)
    arrived(spread_h2)
    h.acc[...] += mixed_part(2)

    def to_near(c):
        acc = c.acc[...]
        left = acc[:, :half].reshape(16, 8, half)
        right = acc[:, half:].reshape(16, 8, half)
        blocks = jnp.concatenate([left, right], axis=1)
        c.blocks[...] = blocks
        c.sendz[...] = blocks.astype(BF16)
        up = c.sendz.at[pl.ds(lax.rem(z + 3, 4) * 4, 4)]
        down = c.sendz.at[pl.ds(lax.rem(z + 1, 4) * 4, 4)]
        here = lax.rem(z, 4) * 4
        return [
            send(c.sendz.at[pl.ds(here, 2)], c.nearz2.at[pl.ds(0, 2)], at_z(2)),
            send(c.sendz.at[pl.ds(here + 2, 2)], c.nearz2.at[pl.ds(2, 2)], at_z(-2)),
            send(up, c.nearz.at[0], at_z(1)),
            send(down, c.nearz.at[1], at_z(-1)),
        ]

    def to_far(c, got):
        arrived(got)
        total = c.blocks[pl.ds(held, 4)] + c.nearz[0].astype(F32)
        total = total + c.nearz[1].astype(F32) + c.nearz2[...].astype(F32)
        c.sendf[...] = total.astype(BF16)
        out = []
        for n, step in enumerate(FAR):
            there = lax.div(lax.rem(z + step + 16, 16), 4)
            out.append(send(c.sendf.at[there], c.recvf.at[n], at_z(step)))
        return out

    def finish(c, got, n):
        arrived(got)
        total = c.recvf[0].astype(F32) + c.recvf[1].astype(F32)
        total = total + c.recvf[2].astype(F32) + c.recvf[3].astype(F32)
        whole = jnp.concatenate([total[:8], total[8:]], axis=1)
        out_ref[n] = whole[:6].astype(BF16)

    near_h = to_near(h)
    g.acc[...] = grad_in_part(0)
    arrived(spread_g[2:])
    g.acc[...] += grad_in_part(1)
    g.acc[...] += grad_in_part(3)
    arrived(spread_g2)
    g.acc[...] += grad_in_part(2)
    near_g = to_near(g)
    far_h = to_far(h, near_h)
    far_g = to_far(g, near_g)
    late = near_g + far_h + far_g
    for copy in started:
        if not any(copy is other for other in late):
            copy.wait_send()

    @pl.when(x != y)
    def _():
        turn.wait_send()

    finish(h, far_h, 0)
    finish(g, far_g, 1)

    for copy in late:
        copy.wait_send()


def shards(tokens, w_in, w_out, grad_out):
    rows, width = tokens.shape
    half = width // 2
    out = jax.ShapeDtypeStruct((2, rows, width), BF16)
    vmem = pl.BlockSpec(memory_space=pltpu.VMEM)
    hbm = pl.BlockSpec(memory_space=pl.ANY)
    both = pl.pallas_call(
        kernel,
        out_shape=out,
        in_specs=[hbm, hbm, hbm, hbm],
        out_specs=vmem,
        scratch_shapes=[
            pltpu.VMEM((4, width, width), BF16),
            pltpu.VMEM((4, width, width), BF16),
            pltpu.VMEM((2,) + tokens.shape, BF16),
            pltpu.VMEM((2, 16, half), BF16),
            pltpu.VMEM((2, 16, 16, half), BF16),
            pltpu.VMEM((48, half), F32),
            pltpu.VMEM((48, half), F32),
        ]
        + chain_scratch(half, width)
        + chain_scratch(half, width)
        + [
            pltpu.SemaphoreType.DMA((6,)),
            pltpu.SemaphoreType.DMA((COPIES,)),
            pltpu.SemaphoreType.DMA((COPIES,)),
        ],
        compiler_params=pltpu.CompilerParams(
            collective_id=0, has_side_effects=True, vmem_limit_bytes=62 * 1024 * 1024
        ),
        cost_estimate=pl.CostEstimate(
            flops=8 * 192 * width * w_in.shape[1], bytes_accessed=4 * w_in.size, transcendentals=0
        ),
    )(tokens, w_in, w_out, grad_out)
    return both[0], both[1]


def solution(mesh):
    placed = (P("col", "row"), P("row", "col"), P("col", "row"), P("col", "row"))
    return jax.shard_map(
        shards,
        mesh=mesh,
        in_specs=placed,
        out_specs=(P("col", "row"), P("col", "row")),
        check_vma=False,
    )
```

```python
import jax
import jax.numpy as jnp
from jax import lax
from jax.experimental import pallas as pl
from jax.experimental.pallas import tpu as pltpu
from jax.sharding import PartitionSpec as P

gelu_scale = 0.7978845608028654
cubic_coef = 0.044715

F32, BF16 = jnp.float32, jnp.bfloat16
MESH = pl.DeviceIdType.MESH
FAR = (6, -6, 2, -2)


def gelu_and_slope(values):
    squared = values * values
    bent = jnp.tanh(gelu_scale * (values + cubic_coef * squared * values))
    act = 0.5 * values * (1.0 + bent)
    slope = 0.5 * (1.0 + bent) + 0.5 * values * (1.0 - bent * bent) * gelu_scale * (
        1.0 + 3.0 * cubic_coef * squared
    )
    return act, slope


def against(left, right):
    return lax.dot_general(left, right, (((1,), (1,)), ((), ())), preferred_element_type=F32)


class Chain:
    def __init__(self, refs):
        (self.x, self.part, self.send1, self.relay, self.near1,
         self.total, self.send2, self.recv2, self.all, self.acc, self.blocks, self.sendz,
         self.nearz, self.nearz2, self.sendf, self.recvf) = refs


def chain_scratch(half, width):
    block = (48, half)
    return [
        pltpu.VMEM((96, width), BF16),
        pltpu.VMEM((4, 4) + block, F32),
        pltpu.VMEM((4, 4) + block, BF16),
        pltpu.VMEM((2, 2) + block, BF16),
        pltpu.VMEM((2, 4) + block, BF16),
        pltpu.VMEM((4,) + block, F32),
        pltpu.VMEM((4,) + block, BF16),
        pltpu.VMEM((3,) + block, BF16),
        pltpu.VMEM((4, 4) + block, BF16),
        pltpu.VMEM((128, width), F32),
        pltpu.VMEM((16, 16, half), F32),
        pltpu.VMEM((16, 16, half), BF16),
        pltpu.VMEM((2, 4, 16, half), BF16),
        pltpu.VMEM((4, 16, half), BF16),
        pltpu.VMEM((4, 16, half), BF16),
        pltpu.VMEM((4, 16, half), BF16),
    ]


CHAIN_REFS = 16
COPIES = 96


def kernel(tok_ref, win_ref, wout_ref, gout_ref, out_ref, *scratch):
    win, wout, raw, own, gathered, slope_out, slope_in = scratch[:7]
    h = Chain(scratch[7:7 + CHAIN_REFS])
    g = Chain(scratch[7 + CHAIN_REFS:7 + 2 * CHAIN_REFS])
    local_sem, send_sem, recv_sem = scratch[7 + 2 * CHAIN_REFS:]
    width = tok_ref.shape[1]
    half = width // 2

    row, col = lax.axis_index("row"), lax.axis_index("col")
    y, x = lax.div(row, 4), lax.rem(row, 4)
    z, core = lax.div(col, 2), lax.rem(col, 2)

    def at_x(step):
        return (y * 4 + lax.rem(x + step + 4, 4), col)

    def at_y(step):
        return (lax.rem(y + step + 4, 4) * 4 + x, col)

    def at_z(step):
        return (row, lax.rem(z + step + 16, 16) * 2 + core)

    other_core = (row, z * 2 + 1 - core)
    turned = (x * 4 + y, col)
    same = lax.div(3 - lax.max(x - y, y - x), 3)

    moves = [(tok_ref, raw.at[0]), (gout_ref, raw.at[1])]
    for part in range(2):
        cut = pl.ds(part * width, width)
        moves.append((win_ref.at[:, cut], win.at[2 * core + part]))
    for part in range(2):
        cut = pl.ds(part * width, width)
        moves.append((wout_ref.at[cut, :], wout.at[2 * core + part]))
    local = [pltpu.make_async_copy(src, dst, local_sem.at[n]) for n, (src, dst) in enumerate(moves)]
    for copy in local:
        copy.start()

    partners = [at_z(step) for step in (6, -6, 2, -2, 1, -1)]
    partners += [other_core, (x * 4 + y, z * 2 + core + same * (1 - 2 * core))]
    partners += [at_x(step) for step in (2, 1, -1)]
    partners += [at_y(step) for step in (2, 1, -1)]
    barrier = pltpu.get_barrier_semaphore()
    for partner in partners:
        pl.semaphore_signal(barrier, inc=1, device_id=partner, device_id_type=MESH)

    empty = jnp.zeros((2, width), F32)
    for n in range(2):
        local[n].wait()
        whole = jnp.concatenate([raw[n].astype(F32), empty], axis=0)
        folded = jnp.concatenate([whole[:, :half], whole[:, half:]], axis=0)
        own[n] = folded.astype(BF16)

    pl.semaphore_wait(barrier, len(partners))

    started = []

    def send(src, dst, device):
        n = len(started)
        copy = pltpu.make_async_remote_copy(
            src_ref=src, dst_ref=dst, send_sem=send_sem.at[n], recv_sem=recv_sem.at[n],
            device_id=device, device_id_type=MESH,
        )
        copy.start()
        started.append(copy)
        return copy

    def arrived(copies):
        for copy in copies:
            copy.wait_recv()

    slot = lax.rem(z, 4) * 4 + lax.div(z, 4)
    held = lax.rem(z + 2, 4) * 4

    def gather_far(n):
        return [send(own.at[n], gathered.at[n, slot], at_z(step)) for step in FAR]

    def gather_near(n):
        out = []
        for step, first, count in ((2, 0, 2), (-2, 2, 2), (1, 0, 4), (-1, 0, 4)):
            piece = gathered.at[n, pl.ds(held + first, count)]
            out.append(send(piece, piece, at_z(step)))
        return out

    far_in = [gather_far(0), gather_far(1)]
    pushed = []
    for part in range(2):
        src = win_ref.at[:, pl.ds(part * width, width)]
        pushed.append(send(src, win.at[2 * core + part], other_core))
    for part in range(2):
        src = wout_ref.at[pl.ds(part * width, width)]
        pushed.append(send(src, wout.at[2 * core + part], other_core))
    near_in = []
    for n in range(2):
        arrived(far_in[n])
        near_in.append(gather_near(n))

    def squeeze(c, n):
        blocks = gathered[n].astype(F32)
        left = blocks[:, :8, :].reshape(128, half)
        right = blocks[:, 8:, :].reshape(128, half)
        spread = jnp.concatenate([left, right], axis=1).astype(BF16)
        at = lax.broadcasted_iota(jnp.int32, (96, 128), 0)
        come = lax.broadcasted_iota(jnp.int32, (96, 128), 1)
        within = come & 7
        pick = jnp.where((within < 6) & (at == 6 * (come >> 3) + within), 1.0, 0.0).astype(BF16)
        c.x[...] = jnp.dot(pick, spread, preferred_element_type=F32).astype(BF16)

    def expander():
        at = lax.broadcasted_iota(jnp.int32, (128, 96), 0)
        come = lax.broadcasted_iota(jnp.int32, (128, 96), 1)
        within = at & 7
        return jnp.where((within < 6) & (come == 6 * (at >> 3) + within), 1.0, 0.0).astype(BF16)

    def quarters(value):
        return [
            value[48 * up:48 * up + 48, half * side:half * side + half]
            for up in range(2) for side in range(2)
        ]

    def relays(c, got, ahead):
        for v in range(4):
            c.send1[2, v] = got[v].astype(BF16)
        return [
            send(c.send1.at[2, pl.ds(0, 2)], c.relay.at[0], ahead(1)),
            send(c.send1.at[2, pl.ds(2, 2)], c.relay.at[1], ahead(-1)),
        ]

    def direct_up(c, got, ahead):
        for v in (2, 3):
            c.send1[1, v] = got[v].astype(BF16)
        out = [send(c.send1.at[1, pl.ds(2, 2)], c.near1.at[0, pl.ds(2, 2)], ahead(1))]
        for v in (0, 1):
            c.part[1, v] = got[v]
        return out

    def direct_down(c, got, ahead):
        for v in (0, 1):
            c.send1[3, v] = got[v].astype(BF16)
        out = [send(c.send1.at[3, pl.ds(0, 2)], c.near1.at[1, pl.ds(0, 2)], ahead(-1))]
        for v in (2, 3):
            c.part[3, v] = got[v]
        return out

    def stay(c, got):
        for v in range(4):
            c.part[0, v] = got[v]

    def passed_on(c, got, ahead):
        arrived(got[:1])
        c.send1[1, 0:2] = (c.part[1, 0:2] + c.relay[0].astype(F32)).astype(BF16)
        out = [send(c.send1.at[1, pl.ds(0, 2)], c.near1.at[0, pl.ds(0, 2)], ahead(1))]
        arrived(got[1:])
        c.send1[3, 2:4] = (c.part[3, 2:4] + c.relay[1].astype(F32)).astype(BF16)
        out.append(send(c.send1.at[3, pl.ds(2, 2)], c.near1.at[1, pl.ds(2, 2)], ahead(-1)))
        return out

    def second_sum(c, got, ahead, place):
        arrived(got)
        c.total[...] = c.part[0] + c.near1[0].astype(F32) + c.near1[1].astype(F32)
        c.send2[...] = c.total[...].astype(BF16)
        out = []
        for n, step in enumerate((2, 1, -1)):
            there = lax.rem(place + step + 4, 4)
            out.append(send(c.send2.at[there], c.recv2.at[n], ahead(step)))
        return out

    def summed(c, got, place):
        arrived(got)
        return (
            c.total[place] + c.recv2[0].astype(F32) + c.recv2[1].astype(F32) + c.recv2[2].astype(F32)
        )

    arrived(near_in[0])
    squeeze(h, 0)
    for copy in local[2:4]:
        copy.wait()
    arrived(pushed[:2])

    def hidden_part(rel):
        return quarters(jnp.dot(h.x[...], win[lax.rem(x + rel, 4)], preferred_element_type=F32))

    def grad_part(rel):
        return quarters(against(g.x[...], wout[lax.rem(y + rel, 4)]))

    relay_h = relays(h, hidden_part(2), at_x)
    direct_h = direct_up(h, hidden_part(1), at_x)
    direct_h += direct_down(h, hidden_part(3), at_x)
    stay(h, hidden_part(0))

    arrived(near_in[1])
    squeeze(g, 1)
    for copy in local[4:]:
        copy.wait()
    arrived(pushed[2:])

    relay_g = relays(g, grad_part(2), at_y)
    direct_h += passed_on(h, relay_h, at_x)
    direct_g = direct_up(g, grad_part(1), at_y)
    direct_g += direct_down(g, grad_part(3), at_y)
    stay(g, grad_part(0))
    second_h = second_sum(h, direct_h, at_y, y)
    direct_g += passed_on(g, relay_g, at_y)
    hidden = summed(h, second_h, y)
    act, slope = gelu_and_slope(hidden)
    h.all[x, y] = act.astype(BF16)

    def spread_first(c, chunk, place, ahead):
        piece = c.all.at[chunk, place]
        return [send(piece, piece, ahead(step)) for step in (2, 1, -1)]

    def spread_second(c, got, chunk, ahead):
        arrived(got)
        low, high = c.all.at[chunk, pl.ds(0, 2)], c.all.at[chunk, pl.ds(2, 2)]
        return [
            send(low, low, ahead(1)),
            send(high, high, ahead(-1)),
            send(high, high, ahead(1)),
            send(low, low, ahead(-1)),
        ]

    def spread_third(c, got, place, ahead):
        arrived(got[:1])
        piece = c.all.at[lax.rem(place + 3, 4), pl.ds(0, 2)]
        out = [send(piece, piece, ahead(1))]
        arrived(got[1:2])
        piece = c.all.at[lax.rem(place + 1, 4), pl.ds(2, 2)]
        out.append(send(piece, piece, ahead(-1)))
        return out

    first_h = spread_first(h, x, y, at_y)
    slope_out[...] = slope
    turn = pltpu.make_async_remote_copy(
        src_ref=slope_out, dst_ref=slope_in, send_sem=send_sem.at[COPIES - 1],
        recv_sem=recv_sem.at[COPIES - 1], device_id=turned, device_id_type=MESH,
    )

    @pl.when(x != y)
    def _():
        turn.start()

    @pl.when(x == y)
    def _():
        slope_in[...] = slope_out[...]

    second_g = second_sum(g, direct_g, at_x, x)
    spread_h = spread_second(h, first_h, x, at_x)
    grad_act = summed(g, second_g, x)

    @pl.when(x != y)
    def _():
        turn.wait_recv()

    g.all[y, x] = (grad_act * slope_in[...]).astype(BF16)
    first_g = spread_first(g, y, x, at_x)

    expand = expander()

    def widened(blocks):
        rows = [jnp.concatenate([blocks[2 * up], blocks[2 * up + 1]], axis=1) for up in range(2)]
        return jnp.dot(
            expand, jnp.concatenate(rows, axis=0), preferred_element_type=F32
        ).astype(BF16)

    def mixed_part(rel):
        u = lax.rem(x + rel, 4)
        return jnp.dot(widened(h.all[u]), wout[u], preferred_element_type=F32)

    def grad_in_part(rel):
        u = lax.rem(y + rel, 4)
        return against(widened(g.all[u]), win[u])

    h.acc[...] = mixed_part(0)
    spread_h2 = spread_third(h, spread_h, x, at_x)
    spread_g = spread_second(g, first_g, y, at_y)
    g.acc[...] = grad_in_part(0)
    arrived(spread_h[2:])
    h.acc[...] += mixed_part(1)
    h.acc[...] += mixed_part(3)
    spread_g2 = spread_third(g, spread_g, y, at_y)
    arrived(spread_h2)
    h.acc[...] += mixed_part(2)

    def to_near(c):
        acc = c.acc[...]
        left = acc[:, :half].reshape(16, 8, half)
        right = acc[:, half:].reshape(16, 8, half)
        blocks = jnp.concatenate([left, right], axis=1)
        c.blocks[...] = blocks
        c.sendz[...] = blocks.astype(BF16)
        up = c.sendz.at[pl.ds(lax.rem(z + 3, 4) * 4, 4)]
        down = c.sendz.at[pl.ds(lax.rem(z + 1, 4) * 4, 4)]
        here = lax.rem(z, 4) * 4
        return [
            send(c.sendz.at[pl.ds(here, 2)], c.nearz2.at[pl.ds(0, 2)], at_z(2)),
            send(c.sendz.at[pl.ds(here + 2, 2)], c.nearz2.at[pl.ds(2, 2)], at_z(-2)),
            send(up, c.nearz.at[0], at_z(1)),
            send(down, c.nearz.at[1], at_z(-1)),
        ]

    def to_far(c, got):
        arrived(got)
        total = c.blocks[pl.ds(held, 4)] + c.nearz[0].astype(F32)
        total = total + c.nearz[1].astype(F32) + c.nearz2[...].astype(F32)
        c.sendf[...] = total.astype(BF16)
        out = []
        for n, step in enumerate(FAR):
            there = lax.div(lax.rem(z + step + 16, 16), 4)
            out.append(send(c.sendf.at[there], c.recvf.at[n], at_z(step)))
        return out

    def finish(c, got, n):
        arrived(got)
        total = c.recvf[0].astype(F32) + c.recvf[1].astype(F32)
        total = total + c.recvf[2].astype(F32) + c.recvf[3].astype(F32)
        whole = jnp.concatenate([total[:8], total[8:]], axis=1)
        out_ref[n] = whole[:6].astype(BF16)

    near_h = to_near(h)
    arrived(spread_g[2:])
    g.acc[...] += grad_in_part(1)
    g.acc[...] += grad_in_part(3)
    arrived(spread_g2)
    g.acc[...] += grad_in_part(2)
    near_g = to_near(g)
    far_h = to_far(h, near_h)
    far_g = to_far(g, near_g)
    late = near_g + far_h + far_g
    for copy in started:
        if not any(copy is other for other in late):
            copy.wait_send()

    @pl.when(x != y)
    def _():
        turn.wait_send()

    finish(h, far_h, 0)
    finish(g, far_g, 1)

    for copy in late:
        copy.wait_send()


def shards(tokens, w_in, w_out, grad_out):
    rows, width = tokens.shape
    half = width // 2
    out = jax.ShapeDtypeStruct((2, rows, width), BF16)
    vmem = pl.BlockSpec(memory_space=pltpu.VMEM)
    hbm = pl.BlockSpec(memory_space=pl.ANY)
    both = pl.pallas_call(
        kernel,
        out_shape=out,
        in_specs=[hbm, hbm, hbm, hbm],
        out_specs=vmem,
        scratch_shapes=[
            pltpu.VMEM((4, width, width), BF16),
            pltpu.VMEM((4, width, width), BF16),
            pltpu.VMEM((2,) + tokens.shape, BF16),
            pltpu.VMEM((2, 16, half), BF16),
            pltpu.VMEM((2, 16, 16, half), BF16),
            pltpu.VMEM((48, half), F32),
            pltpu.VMEM((48, half), F32),
        ]
        + chain_scratch(half, width)
        + chain_scratch(half, width)
        + [
            pltpu.SemaphoreType.DMA((6,)),
            pltpu.SemaphoreType.DMA((COPIES,)),
            pltpu.SemaphoreType.DMA((COPIES,)),
        ],
        compiler_params=pltpu.CompilerParams(
            collective_id=0, has_side_effects=True, vmem_limit_bytes=62 * 1024 * 1024
        ),
        cost_estimate=pl.CostEstimate(
            flops=8 * 192 * width * w_in.shape[1], bytes_accessed=4 * w_in.size, transcendentals=0
        ),
    )(tokens, w_in, w_out, grad_out)
    return both[0], both[1]


def solution(mesh):
    placed = (P("col", "row"), P("row", "col"), P("col", "row"), P("col", "row"))
    return jax.shard_map(
        shards,
        mesh=mesh,
        in_specs=placed,
        out_specs=(P("col", "row"), P("col", "row")),
        check_vma=False,
    )
```

```python
import jax
import jax.numpy as jnp
from jax import lax
from jax.experimental import pallas as pl
from jax.experimental.pallas import tpu as pltpu
from jax.sharding import PartitionSpec as P

gelu_scale = 0.7978845608028654
cubic_coef = 0.044715

F32, BF16 = jnp.float32, jnp.bfloat16
MESH = pl.DeviceIdType.MESH
FAR = (6, -6, 2, -2)


def gelu_and_slope(values):
    squared = values * values
    bent = jnp.tanh(gelu_scale * (values + cubic_coef * squared * values))
    act = 0.5 * values * (1.0 + bent)
    slope = 0.5 * (1.0 + bent) + 0.5 * values * (1.0 - bent * bent) * gelu_scale * (
        1.0 + 3.0 * cubic_coef * squared
    )
    return act, slope


def against(left, right):
    return lax.dot_general(left, right, (((1,), (1,)), ((), ())), preferred_element_type=F32)


class Chain:
    def __init__(self, refs):
        (self.x, self.part, self.send1, self.relay, self.near1,
         self.total, self.send2, self.recv2, self.all, self.acc, self.blocks, self.sendz,
         self.nearz, self.nearz2, self.sendf, self.recvf) = refs


def chain_scratch(half, width):
    block = (48, half)
    return [
        pltpu.VMEM((96, width), BF16),
        pltpu.VMEM((4, 4) + block, F32),
        pltpu.VMEM((4, 4) + block, BF16),
        pltpu.VMEM((2, 2) + block, BF16),
        pltpu.VMEM((2, 4) + block, BF16),
        pltpu.VMEM(block, F32),
        pltpu.VMEM((3,) + block, BF16),
        pltpu.VMEM((3,) + block, BF16),
        pltpu.VMEM((4, 4) + block, BF16),
        pltpu.VMEM((128, width), F32),
        pltpu.VMEM((4, 16, half), F32),
        pltpu.VMEM((3, 4, 16, half), BF16),
        pltpu.VMEM((2, 4, 16, half), BF16),
        pltpu.VMEM((4, 16, half), BF16),
        pltpu.VMEM((4, 16, half), BF16),
        pltpu.VMEM((4, 16, half), BF16),
    ]


CHAIN_REFS = 16
COPIES = 96


def kernel(tok_ref, win_ref, wout_ref, gout_ref, out_ref, *scratch):
    win, wout, raw, own, gathered, slope_out, slope_in, picks, expand = scratch[:9]
    h = Chain(scratch[9:9 + CHAIN_REFS])
    g = Chain(scratch[9 + CHAIN_REFS:9 + 2 * CHAIN_REFS])
    local_sem, send_sem, recv_sem = scratch[9 + 2 * CHAIN_REFS:]
    width = tok_ref.shape[1]
    half = width // 2

    row, col = lax.axis_index("row"), lax.axis_index("col")
    y, x = lax.div(row, 4), lax.rem(row, 4)
    z, core = lax.div(col, 2), lax.rem(col, 2)

    def at_x(step):
        return (y * 4 + lax.rem(x + step + 4, 4), col)

    def at_y(step):
        return (lax.rem(y + step + 4, 4) * 4 + x, col)

    def at_z(step):
        return (row, lax.rem(z + step + 16, 16) * 2 + core)

    other_core = (row, z * 2 + 1 - core)
    turned = (x * 4 + y, col)
    same = lax.div(3 - lax.max(x - y, y - x), 3)

    moves = [(tok_ref, raw.at[0]), (gout_ref, raw.at[1])]
    for part in range(2):
        cut = pl.ds(part * width, width)
        moves.append((win_ref.at[:, cut], win.at[2 * core + part]))
    for part in range(2):
        cut = pl.ds(part * width, width)
        moves.append((wout_ref.at[cut, :], wout.at[2 * core + part]))
    local = [pltpu.make_async_copy(src, dst, local_sem.at[n]) for n, (src, dst) in enumerate(moves)]
    for copy in local:
        copy.start()

    partners = [at_z(step) for step in (6, -6, 2, -2, 1, -1)]
    partners += [other_core, (x * 4 + y, z * 2 + core + same * (1 - 2 * core))]
    partners += [at_x(step) for step in (2, 1, -1)]
    partners += [at_y(step) for step in (2, 1, -1)]
    barrier = pltpu.get_barrier_semaphore()
    for partner in partners:
        pl.semaphore_signal(barrier, inc=1, device_id=partner, device_id_type=MESH)

    empty = jnp.zeros((2, width), F32)
    for n in range(2):
        local[n].wait()
        whole = jnp.concatenate([raw[n].astype(F32), empty], axis=0)
        folded = jnp.concatenate([whole[:, :half], whole[:, half:]], axis=0)
        own[n] = folded.astype(BF16)

    at = lax.broadcasted_iota(jnp.int32, (96, 256), 0)
    come = lax.broadcasted_iota(jnp.int32, (96, 256), 1)
    for side in range(2):
        within = (come & 15) - 8 * side
        chosen = (within >= 0) & (within < 6) & (at == 6 * (come >> 4) + within)
        picks[side] = jnp.where(chosen, 1.0, 0.0).astype(BF16)
    at = lax.broadcasted_iota(jnp.int32, (128, 96), 0)
    come = lax.broadcasted_iota(jnp.int32, (128, 96), 1)
    within = at & 7
    chosen = (within < 6) & (come == 6 * (at >> 3) + within)
    expand[...] = jnp.where(chosen, 1.0, 0.0).astype(BF16)

    pl.semaphore_wait(barrier, len(partners))

    started = []

    def send(src, dst, device):
        n = len(started)
        copy = pltpu.make_async_remote_copy(
            src_ref=src, dst_ref=dst, send_sem=send_sem.at[n], recv_sem=recv_sem.at[n],
            device_id=device, device_id_type=MESH,
        )
        copy.start()
        started.append(copy)
        return copy

    def arrived(copies):
        for copy in copies:
            copy.wait_recv()

    slot = lax.rem(z, 4) * 4 + lax.div(z, 4)
    held = lax.rem(z + 2, 4) * 4

    def gather_far(n):
        return [send(own.at[n], gathered.at[n, slot], at_z(step)) for step in FAR]

    def gather_near(n):
        out = []
        for step, first, count in ((2, 0, 2), (-2, 2, 2), (1, 0, 4), (-1, 0, 4)):
            piece = gathered.at[n, pl.ds(held + first, count)]
            out.append(send(piece, piece, at_z(step)))
        return out

    far_in = [gather_far(0), gather_far(1)]
    pushed = []
    for part in range(2):
        src = win_ref.at[:, pl.ds(part * width, width)]
        pushed.append(send(src, win.at[2 * core + part], other_core))
    for part in range(2):
        src = wout_ref.at[pl.ds(part * width, width)]
        pushed.append(send(src, wout.at[2 * core + part], other_core))
    near_in = []
    for n in range(2):
        arrived(far_in[n])
        near_in.append(gather_near(n))

    def squeeze(c, n):
        blocks = gathered[n].reshape(256, half)
        for side in range(2):
            got = jnp.dot(picks[side], blocks, preferred_element_type=F32)
            c.x[:, half * side:half * side + half] = got.astype(BF16)

    def quarters(value):
        return [
            value[48 * up:48 * up + 48, half * side:half * side + half]
            for up in range(2) for side in range(2)
        ]

    def relays(c, got, ahead):
        for v in range(4):
            c.send1[2, v] = got[v].astype(BF16)
        return [
            send(c.send1.at[2, pl.ds(0, 2)], c.relay.at[0], ahead(1)),
            send(c.send1.at[2, pl.ds(2, 2)], c.relay.at[1], ahead(-1)),
        ]

    def direct_up(c, got, ahead):
        for v in (2, 3):
            c.send1[1, v] = got[v].astype(BF16)
        out = [send(c.send1.at[1, pl.ds(2, 2)], c.near1.at[0, pl.ds(2, 2)], ahead(1))]
        for v in (0, 1):
            c.part[1, v] = got[v]
        return out

    def direct_down(c, got, ahead):
        for v in (0, 1):
            c.send1[3, v] = got[v].astype(BF16)
        out = [send(c.send1.at[3, pl.ds(0, 2)], c.near1.at[1, pl.ds(0, 2)], ahead(-1))]
        for v in (2, 3):
            c.part[3, v] = got[v]
        return out

    def stay(c, got):
        for v in range(4):
            c.part[0, v] = got[v]

    def passed_on(c, got, ahead):
        arrived(got[:1])
        c.send1[1, 0:2] = (c.part[1, 0:2] + c.relay[0].astype(F32)).astype(BF16)
        out = [send(c.send1.at[1, pl.ds(0, 2)], c.near1.at[0, pl.ds(0, 2)], ahead(1))]
        arrived(got[1:])
        c.send1[3, 2:4] = (c.part[3, 2:4] + c.relay[1].astype(F32)).astype(BF16)
        out.append(send(c.send1.at[3, pl.ds(2, 2)], c.near1.at[1, pl.ds(2, 2)], ahead(-1)))
        return out

    def second_sum(c, got, ahead, place):
        arrived(got)
        out = []
        for n, step in enumerate((2, 1, -1)):
            c.send2[n] = first_sum(c, lax.rem(place + step + 4, 4)).astype(BF16)
            out.append(send(c.send2.at[n], c.recv2.at[n], ahead(step)))
        c.total[...] = first_sum(c, place)
        return out

    def first_sum(c, there):
        return c.part[0, there] + c.near1[0, there].astype(F32) + c.near1[1, there].astype(F32)

    def summed(c, got):
        arrived(got)
        return (
            c.total[...] + c.recv2[0].astype(F32) + c.recv2[1].astype(F32) + c.recv2[2].astype(F32)
        )

    arrived(near_in[0])
    squeeze(h, 0)
    for copy in local[2:4]:
        copy.wait()
    arrived(pushed[:2])

    def hidden_part(rel):
        return quarters(jnp.dot(h.x[...], win[lax.rem(x + rel, 4)], preferred_element_type=F32))

    def grad_part(rel):
        return quarters(against(g.x[...], wout[lax.rem(y + rel, 4)]))

    relay_h = relays(h, hidden_part(2), at_x)
    direct_h = direct_up(h, hidden_part(1), at_x)
    direct_h += direct_down(h, hidden_part(3), at_x)
    stay(h, hidden_part(0))

    arrived(near_in[1])
    squeeze(g, 1)
    for copy in local[4:]:
        copy.wait()
    arrived(pushed[2:])

    relay_g = relays(g, grad_part(2), at_y)
    direct_h += passed_on(h, relay_h, at_x)
    direct_g = direct_up(g, grad_part(1), at_y)
    direct_g += direct_down(g, grad_part(3), at_y)
    stay(g, grad_part(0))
    second_h = second_sum(h, direct_h, at_y, y)
    direct_g += passed_on(g, relay_g, at_y)
    hidden = summed(h, second_h)
    act, slope = gelu_and_slope(hidden)
    h.all[x, y] = act.astype(BF16)

    def spread_first(c, chunk, place, ahead):
        piece = c.all.at[chunk, place]
        return [send(piece, piece, ahead(step)) for step in (2, 1, -1)]

    def spread_second(c, got, chunk, ahead):
        arrived(got)
        low, high = c.all.at[chunk, pl.ds(0, 2)], c.all.at[chunk, pl.ds(2, 2)]
        return [
            send(low, low, ahead(1)),
            send(high, high, ahead(-1)),
            send(high, high, ahead(1)),
            send(low, low, ahead(-1)),
        ]

    def spread_third(c, got, place, ahead):
        arrived(got[:1])
        piece = c.all.at[lax.rem(place + 3, 4), pl.ds(0, 2)]
        out = [send(piece, piece, ahead(1))]
        arrived(got[1:2])
        piece = c.all.at[lax.rem(place + 1, 4), pl.ds(2, 2)]
        out.append(send(piece, piece, ahead(-1)))
        return out

    first_h = spread_first(h, x, y, at_y)
    slope_out[...] = slope
    turn = pltpu.make_async_remote_copy(
        src_ref=slope_out, dst_ref=slope_in, send_sem=send_sem.at[COPIES - 1],
        recv_sem=recv_sem.at[COPIES - 1], device_id=turned, device_id_type=MESH,
    )

    @pl.when(x != y)
    def _():
        turn.start()

    @pl.when(x == y)
    def _():
        slope_in[...] = slope_out[...]

    second_g = second_sum(g, direct_g, at_x, x)
    spread_h = spread_second(h, first_h, x, at_x)
    grad_act = summed(g, second_g)

    @pl.when(x != y)
    def _():
        turn.wait_recv()

    g.all[y, x] = (grad_act * slope_in[...]).astype(BF16)
    first_g = spread_first(g, y, x, at_x)

    def widened(blocks):
        rows = [jnp.concatenate([blocks[2 * up], blocks[2 * up + 1]], axis=1) for up in range(2)]
        return jnp.dot(
            expand[...], jnp.concatenate(rows, axis=0), preferred_element_type=F32
        ).astype(BF16)

    def mixed_part(rel):
        u = lax.rem(x + rel, 4)
        return jnp.dot(widened(h.all[u]), wout[u], preferred_element_type=F32)

    def grad_in_part(rel):
        u = lax.rem(y + rel, 4)
        return against(widened(g.all[u]), win[u])

    h.acc[...] = mixed_part(0)
    spread_h2 = spread_third(h, spread_h, x, at_x)
    spread_g = spread_second(g, first_g, y, at_y)
    g.acc[...] = grad_in_part(0)
    arrived(spread_h[2:])
    h.acc[...] += mixed_part(1)
    h.acc[...] += mixed_part(3)
    spread_g2 = spread_third(g, spread_g, y, at_y)
    arrived(spread_h2)
    h.acc[...] += mixed_part(2)

    def folded_class(c, step):
        first = pl.multiple_of(lax.rem(z + step, 4) * 32, 32)
        acc = c.acc[pl.ds(first, 32), :]
        left = acc[:, :half].reshape(4, 8, half)
        right = acc[:, half:].reshape(4, 8, half)
        return jnp.concatenate([left, right], axis=1)

    def to_near(c):
        c.sendz[0] = folded_class(c, 0).astype(BF16)
        out = [
            send(c.sendz.at[0, pl.ds(0, 2)], c.nearz2.at[pl.ds(0, 2)], at_z(2)),
            send(c.sendz.at[0, pl.ds(2, 2)], c.nearz2.at[pl.ds(2, 2)], at_z(-2)),
        ]
        c.sendz[1] = folded_class(c, 3).astype(BF16)
        out.append(send(c.sendz.at[1], c.nearz.at[0], at_z(1)))
        c.sendz[2] = folded_class(c, 1).astype(BF16)
        out.append(send(c.sendz.at[2], c.nearz.at[1], at_z(-1)))
        c.blocks[...] = folded_class(c, 2)
        return out

    def to_far(c, got):
        arrived(got)
        total = c.blocks[...] + c.nearz[0].astype(F32)
        total = total + c.nearz[1].astype(F32) + c.nearz2[...].astype(F32)
        c.sendf[...] = total.astype(BF16)
        out = []
        for n, step in enumerate(FAR):
            there = lax.div(lax.rem(z + step + 16, 16), 4)
            out.append(send(c.sendf.at[there], c.recvf.at[n], at_z(step)))
        return out

    def finish(c, got, n):
        arrived(got)
        total = c.recvf[0].astype(F32) + c.recvf[1].astype(F32)
        total = total + c.recvf[2].astype(F32) + c.recvf[3].astype(F32)
        whole = jnp.concatenate([total[:8], total[8:]], axis=1)
        out_ref[n] = whole[:6].astype(BF16)

    near_h = to_near(h)
    arrived(spread_g[2:])
    g.acc[...] += grad_in_part(1)
    g.acc[...] += grad_in_part(3)
    arrived(spread_g2)
    g.acc[...] += grad_in_part(2)
    near_g = to_near(g)
    far_h = to_far(h, near_h)
    far_g = to_far(g, near_g)
    late = near_g + far_h + far_g
    for copy in started:
        if not any(copy is other for other in late):
            copy.wait_send()

    @pl.when(x != y)
    def _():
        turn.wait_send()

    finish(h, far_h, 0)
    finish(g, far_g, 1)

    for copy in late:
        copy.wait_send()


def shards(tokens, w_in, w_out, grad_out):
    rows, width = tokens.shape
    half = width // 2
    out = jax.ShapeDtypeStruct((2, rows, width), BF16)
    vmem = pl.BlockSpec(memory_space=pltpu.VMEM)
    hbm = pl.BlockSpec(memory_space=pl.ANY)
    both = pl.pallas_call(
        kernel,
        out_shape=out,
        in_specs=[hbm, hbm, hbm, hbm],
        out_specs=vmem,
        scratch_shapes=[
            pltpu.VMEM((4, width, width), BF16),
            pltpu.VMEM((4, width, width), BF16),
            pltpu.VMEM((2,) + tokens.shape, BF16),
            pltpu.VMEM((2, 16, half), BF16),
            pltpu.VMEM((2, 16, 16, half), BF16),
            pltpu.VMEM((48, half), F32),
            pltpu.VMEM((48, half), F32),
            pltpu.VMEM((2, 96, 256), BF16),
            pltpu.VMEM((128, 96), BF16),
        ]
        + chain_scratch(half, width)
        + chain_scratch(half, width)
        + [
            pltpu.SemaphoreType.DMA((6,)),
            pltpu.SemaphoreType.DMA((COPIES,)),
            pltpu.SemaphoreType.DMA((COPIES,)),
        ],
        compiler_params=pltpu.CompilerParams(
            collective_id=0, has_side_effects=True, vmem_limit_bytes=62 * 1024 * 1024
        ),
        cost_estimate=pl.CostEstimate(
            flops=8 * 192 * width * w_in.shape[1], bytes_accessed=4 * w_in.size, transcendentals=0
        ),
    )(tokens, w_in, w_out, grad_out)
    return both[0], both[1]


def solution(mesh):
    placed = (P("col", "row"), P("row", "col"), P("col", "row"), P("col", "row"))
    return jax.shard_map(
        shards,
        mesh=mesh,
        in_specs=placed,
        out_specs=(P("col", "row"), P("col", "row")),
        check_vma=False,
    )
```

```python
import jax
import jax.numpy as jnp
from jax import lax
from jax.experimental import pallas as pl
from jax.experimental.pallas import tpu as pltpu
from jax.sharding import PartitionSpec as P

gelu_scale = 0.7978845608028654
cubic_coef = 0.044715

F32, BF16 = jnp.float32, jnp.bfloat16
MESH = pl.DeviceIdType.MESH
FAR = (6, -6, 2, -2)


def gelu_and_slope(values):
    squared = values * values
    bent = jnp.tanh(gelu_scale * (values + cubic_coef * squared * values))
    act = 0.5 * values * (1.0 + bent)
    slope = 0.5 * (1.0 + bent) + 0.5 * values * (1.0 - bent * bent) * gelu_scale * (
        1.0 + 3.0 * cubic_coef * squared
    )
    return act, slope


def against(left, right):
    return lax.dot_general(left, right, (((1,), (1,)), ((), ())), preferred_element_type=F32)


class Chain:
    def __init__(self, refs):
        (self.x, self.part, self.send1, self.relay, self.near1,
         self.total, self.send2, self.recv2, self.all, self.acc, self.blocks, self.sendz,
         self.nearz, self.nearz2, self.sendf, self.recvf) = refs


def chain_scratch(half, width):
    block = (48, half)
    return [
        pltpu.VMEM((96, width), BF16),
        pltpu.VMEM((4, 4) + block, F32),
        pltpu.VMEM((4, 4) + block, BF16),
        pltpu.VMEM((2, 2) + block, BF16),
        pltpu.VMEM((2, 4) + block, BF16),
        pltpu.VMEM(block, F32),
        pltpu.VMEM((3,) + block, BF16),
        pltpu.VMEM((3,) + block, BF16),
        pltpu.VMEM((4, 4) + block, BF16),
        pltpu.VMEM((128, width), F32),
        pltpu.VMEM((4, 16, half), F32),
        pltpu.VMEM((3, 4, 16, half), BF16),
        pltpu.VMEM((2, 4, 16, half), BF16),
        pltpu.VMEM((4, 16, half), BF16),
        pltpu.VMEM((4, 16, half), BF16),
        pltpu.VMEM((4, 16, half), BF16),
    ]


CHAIN_REFS = 16
COPIES = 96


def kernel(tok_ref, win_ref, wout_ref, gout_ref, out_ref, *scratch):
    win, wout, raw, own, gathered, slope_out, slope_in, picks, expand = scratch[:9]
    h = Chain(scratch[9:9 + CHAIN_REFS])
    g = Chain(scratch[9 + CHAIN_REFS:9 + 2 * CHAIN_REFS])
    local_sem, send_sem, recv_sem = scratch[9 + 2 * CHAIN_REFS:]
    width = tok_ref.shape[1]
    half = width // 2

    row, col = lax.axis_index("row"), lax.axis_index("col")
    y, x = lax.div(row, 4), lax.rem(row, 4)
    z, core = lax.div(col, 2), lax.rem(col, 2)

    def at_x(step):
        return (y * 4 + lax.rem(x + step + 4, 4), col)

    def at_y(step):
        return (lax.rem(y + step + 4, 4) * 4 + x, col)

    def at_z(step):
        return (row, lax.rem(z + step + 16, 16) * 2 + core)

    def far_z(step):
        return (row, lax.rem(z + step + 16, 16) * 2 + 1 - core)

    other_core = (row, z * 2 + 1 - core)
    turned = (x * 4 + y, col)
    same = lax.div(3 - lax.max(x - y, y - x), 3)

    moves = [(tok_ref, raw.at[0]), (gout_ref, raw.at[1])]
    for part in range(2):
        cut = pl.ds(part * width, width)
        moves.append((win_ref.at[:, cut], win.at[2 * core + part]))
    for part in range(2):
        cut = pl.ds(part * width, width)
        moves.append((wout_ref.at[cut, :], wout.at[2 * core + part]))
    local = [pltpu.make_async_copy(src, dst, local_sem.at[n]) for n, (src, dst) in enumerate(moves)]
    for copy in local:
        copy.start()

    partners = [far_z(step) for step in FAR] + [at_z(step) for step in (2, -2, 1, -1)]
    partners += [other_core, (x * 4 + y, z * 2 + core + same * (1 - 2 * core))]
    partners += [at_x(step) for step in (2, 1, -1)]
    partners += [at_y(step) for step in (2, 1, -1)]
    barrier = pltpu.get_barrier_semaphore()
    for partner in partners:
        pl.semaphore_signal(barrier, inc=1, device_id=partner, device_id_type=MESH)

    empty = jnp.zeros((2, width), F32)
    for n in range(2):
        local[n].wait()
        whole = jnp.concatenate([raw[n].astype(F32), empty], axis=0)
        folded = jnp.concatenate([whole[:, :half], whole[:, half:]], axis=0)
        own[n] = folded.astype(BF16)

    at = lax.broadcasted_iota(jnp.int32, (96, 256), 0)
    come = lax.broadcasted_iota(jnp.int32, (96, 256), 1)
    for side in range(2):
        within = (come & 15) - 8 * side
        chosen = (within >= 0) & (within < 6) & (at == 6 * (come >> 4) + within)
        picks[side] = jnp.where(chosen, 1.0, 0.0).astype(BF16)
    at = lax.broadcasted_iota(jnp.int32, (128, 96), 0)
    come = lax.broadcasted_iota(jnp.int32, (128, 96), 1)
    within = at & 7
    chosen = (within < 6) & (come == 6 * (at >> 3) + within)
    expand[...] = jnp.where(chosen, 1.0, 0.0).astype(BF16)

    pl.semaphore_wait(barrier, len(partners))

    started = []

    def send(src, dst, device):
        n = len(started)
        copy = pltpu.make_async_remote_copy(
            src_ref=src, dst_ref=dst, send_sem=send_sem.at[n], recv_sem=recv_sem.at[n],
            device_id=device, device_id_type=MESH,
        )
        copy.start()
        started.append(copy)
        return copy

    def arrived(copies):
        for copy in copies:
            copy.wait_recv()

    slot = lax.rem(z, 4) * 4 + lax.div(z, 4)
    held = lax.rem(z + 2, 4) * 4

    def gather_far(n):
        return [send(own.at[n], gathered.at[n, slot], far_z(step)) for step in FAR]

    def gather_near(n):
        out = []
        for step, first, count in ((2, 0, 2), (-2, 2, 2), (1, 0, 4), (-1, 0, 4)):
            piece = gathered.at[n, pl.ds(held + first, count)]
            out.append(send(piece, piece, at_z(step)))
        return out

    far_in = [gather_far(0), gather_far(1)]
    pushed = []
    for part in range(2):
        src = win_ref.at[:, pl.ds(part * width, width)]
        pushed.append(send(src, win.at[2 * core + part], other_core))
    for part in range(2):
        src = wout_ref.at[pl.ds(part * width, width)]
        pushed.append(send(src, wout.at[2 * core + part], other_core))
    near_in = []
    for n in range(2):
        arrived(far_in[n])
        near_in.append(gather_near(n))

    def squeeze(c, n):
        blocks = gathered[n].reshape(256, half)
        for side in range(2):
            got = jnp.dot(picks[side], blocks, preferred_element_type=F32)
            c.x[:, half * side:half * side + half] = got.astype(BF16)

    def quarters(value):
        return [
            value[48 * up:48 * up + 48, half * side:half * side + half]
            for up in range(2) for side in range(2)
        ]

    def relays(c, got, ahead):
        for v in range(4):
            c.send1[2, v] = got[v].astype(BF16)
        return [
            send(c.send1.at[2, pl.ds(0, 2)], c.relay.at[0], ahead(1)),
            send(c.send1.at[2, pl.ds(2, 2)], c.relay.at[1], ahead(-1)),
        ]

    def direct_up(c, got, ahead):
        for v in (2, 3):
            c.send1[1, v] = got[v].astype(BF16)
        out = [send(c.send1.at[1, pl.ds(2, 2)], c.near1.at[0, pl.ds(2, 2)], ahead(1))]
        for v in (0, 1):
            c.part[1, v] = got[v]
        return out

    def direct_down(c, got, ahead):
        for v in (0, 1):
            c.send1[3, v] = got[v].astype(BF16)
        out = [send(c.send1.at[3, pl.ds(0, 2)], c.near1.at[1, pl.ds(0, 2)], ahead(-1))]
        for v in (2, 3):
            c.part[3, v] = got[v]
        return out

    def stay(c, got):
        for v in range(4):
            c.part[0, v] = got[v]

    def passed_on(c, got, ahead):
        arrived(got[:1])
        c.send1[1, 0:2] = (c.part[1, 0:2] + c.relay[0].astype(F32)).astype(BF16)
        out = [send(c.send1.at[1, pl.ds(0, 2)], c.near1.at[0, pl.ds(0, 2)], ahead(1))]
        arrived(got[1:])
        c.send1[3, 2:4] = (c.part[3, 2:4] + c.relay[1].astype(F32)).astype(BF16)
        out.append(send(c.send1.at[3, pl.ds(2, 2)], c.near1.at[1, pl.ds(2, 2)], ahead(-1)))
        return out

    def second_sum(c, got, ahead, place):
        arrived(got)
        out = []
        for n, step in enumerate((2, 1, -1)):
            c.send2[n] = first_sum(c, lax.rem(place + step + 4, 4)).astype(BF16)
            out.append(send(c.send2.at[n], c.recv2.at[n], ahead(step)))
        c.total[...] = first_sum(c, place)
        return out

    def first_sum(c, there):
        return c.part[0, there] + c.near1[0, there].astype(F32) + c.near1[1, there].astype(F32)

    def summed(c, got):
        arrived(got)
        return (
            c.total[...] + c.recv2[0].astype(F32) + c.recv2[1].astype(F32) + c.recv2[2].astype(F32)
        )

    arrived(near_in[0])
    squeeze(h, 0)
    for copy in local[2:4]:
        copy.wait()
    arrived(pushed[:2])

    def hidden_part(rel):
        return quarters(jnp.dot(h.x[...], win[lax.rem(x + rel, 4)], preferred_element_type=F32))

    def grad_part(rel):
        return quarters(against(g.x[...], wout[lax.rem(y + rel, 4)]))

    relay_h = relays(h, hidden_part(2), at_x)
    direct_h = direct_up(h, hidden_part(1), at_x)
    direct_h += direct_down(h, hidden_part(3), at_x)
    stay(h, hidden_part(0))

    arrived(near_in[1])
    squeeze(g, 1)
    for copy in local[4:]:
        copy.wait()
    arrived(pushed[2:])

    relay_g = relays(g, grad_part(2), at_y)
    direct_h += passed_on(h, relay_h, at_x)
    direct_g = direct_up(g, grad_part(1), at_y)
    direct_g += direct_down(g, grad_part(3), at_y)
    stay(g, grad_part(0))
    second_h = second_sum(h, direct_h, at_y, y)
    direct_g += passed_on(g, relay_g, at_y)
    hidden = summed(h, second_h)
    act, slope = gelu_and_slope(hidden)
    h.all[x, y] = act.astype(BF16)

    def spread_first(c, chunk, place, ahead):
        piece = c.all.at[chunk, place]
        return [send(piece, piece, ahead(step)) for step in (2, 1, -1)]

    def spread_second(c, got, chunk, ahead):
        arrived(got)
        low, high = c.all.at[chunk, pl.ds(0, 2)], c.all.at[chunk, pl.ds(2, 2)]
        return [
            send(low, low, ahead(1)),
            send(high, high, ahead(-1)),
            send(high, high, ahead(1)),
            send(low, low, ahead(-1)),
        ]

    def spread_third(c, got, place, ahead):
        arrived(got[:1])
        piece = c.all.at[lax.rem(place + 3, 4), pl.ds(0, 2)]
        out = [send(piece, piece, ahead(1))]
        arrived(got[1:2])
        piece = c.all.at[lax.rem(place + 1, 4), pl.ds(2, 2)]
        out.append(send(piece, piece, ahead(-1)))
        return out

    first_h = spread_first(h, x, y, at_y)
    slope_out[...] = slope
    turn = pltpu.make_async_remote_copy(
        src_ref=slope_out, dst_ref=slope_in, send_sem=send_sem.at[COPIES - 1],
        recv_sem=recv_sem.at[COPIES - 1], device_id=turned, device_id_type=MESH,
    )

    @pl.when(x != y)
    def _():
        turn.start()

    @pl.when(x == y)
    def _():
        slope_in[...] = slope_out[...]

    second_g = second_sum(g, direct_g, at_x, x)
    spread_h = spread_second(h, first_h, x, at_x)
    grad_act = summed(g, second_g)

    @pl.when(x != y)
    def _():
        turn.wait_recv()

    g.all[y, x] = (grad_act * slope_in[...]).astype(BF16)
    first_g = spread_first(g, y, x, at_x)

    def widened(blocks):
        rows = [jnp.concatenate([blocks[2 * up], blocks[2 * up + 1]], axis=1) for up in range(2)]
        return jnp.dot(
            expand[...], jnp.concatenate(rows, axis=0), preferred_element_type=F32
        ).astype(BF16)

    def mixed_part(rel):
        u = lax.rem(x + rel, 4)
        return jnp.dot(widened(h.all[u]), wout[u], preferred_element_type=F32)

    def grad_in_part(rel):
        u = lax.rem(y + rel, 4)
        return against(widened(g.all[u]), win[u])

    h.acc[...] = mixed_part(0)
    spread_h2 = spread_third(h, spread_h, x, at_x)
    spread_g = spread_second(g, first_g, y, at_y)
    g.acc[...] = grad_in_part(0)
    arrived(spread_h[2:])
    h.acc[...] += mixed_part(1)
    h.acc[...] += mixed_part(3)
    spread_g2 = spread_third(g, spread_g, y, at_y)
    arrived(spread_h2)
    h.acc[...] += mixed_part(2)

    def folded_class(c, step):
        first = pl.multiple_of(lax.rem(z + step, 4) * 32, 32)
        acc = c.acc[pl.ds(first, 32), :]
        left = acc[:, :half].reshape(4, 8, half)
        right = acc[:, half:].reshape(4, 8, half)
        return jnp.concatenate([left, right], axis=1)

    def to_near(c):
        c.sendz[0] = folded_class(c, 0).astype(BF16)
        out = [
            send(c.sendz.at[0, pl.ds(0, 2)], c.nearz2.at[pl.ds(0, 2)], at_z(2)),
            send(c.sendz.at[0, pl.ds(2, 2)], c.nearz2.at[pl.ds(2, 2)], at_z(-2)),
        ]
        c.sendz[1] = folded_class(c, 3).astype(BF16)
        out.append(send(c.sendz.at[1], c.nearz.at[0], at_z(1)))
        c.sendz[2] = folded_class(c, 1).astype(BF16)
        out.append(send(c.sendz.at[2], c.nearz.at[1], at_z(-1)))
        c.blocks[...] = folded_class(c, 2)
        return out

    def to_far(c, got):
        arrived(got)
        total = c.blocks[...] + c.nearz[0].astype(F32)
        total = total + c.nearz[1].astype(F32) + c.nearz2[...].astype(F32)
        c.sendf[...] = total.astype(BF16)
        out = []
        for n, step in enumerate(FAR):
            there = lax.div(lax.rem(z + step + 16, 16), 4)
            out.append(send(c.sendf.at[there], c.recvf.at[n], far_z(step)))
        return out

    def finish(c, got, n):
        arrived(got)
        total = c.recvf[0].astype(F32) + c.recvf[1].astype(F32)
        total = total + c.recvf[2].astype(F32) + c.recvf[3].astype(F32)
        whole = jnp.concatenate([total[:8], total[8:]], axis=1)
        out_ref[n] = whole[:6].astype(BF16)

    near_h = to_near(h)
    arrived(spread_g[2:])
    g.acc[...] += grad_in_part(1)
    g.acc[...] += grad_in_part(3)
    arrived(spread_g2)
    g.acc[...] += grad_in_part(2)
    near_g = to_near(g)
    far_h = to_far(h, near_h)
    far_g = to_far(g, near_g)
    late = near_g + far_h + far_g
    for copy in started:
        if not any(copy is other for other in late):
            copy.wait_send()

    @pl.when(x != y)
    def _():
        turn.wait_send()

    finish(h, far_h, 0)
    finish(g, far_g, 1)

    for copy in late:
        copy.wait_send()


def shards(tokens, w_in, w_out, grad_out):
    rows, width = tokens.shape
    half = width // 2
    out = jax.ShapeDtypeStruct((2, rows, width), BF16)
    vmem = pl.BlockSpec(memory_space=pltpu.VMEM)
    hbm = pl.BlockSpec(memory_space=pl.ANY)
    both = pl.pallas_call(
        kernel,
        out_shape=out,
        in_specs=[hbm, hbm, hbm, hbm],
        out_specs=vmem,
        scratch_shapes=[
            pltpu.VMEM((4, width, width), BF16),
            pltpu.VMEM((4, width, width), BF16),
            pltpu.VMEM((2,) + tokens.shape, BF16),
            pltpu.VMEM((2, 16, half), BF16),
            pltpu.VMEM((2, 16, 16, half), BF16),
            pltpu.VMEM((48, half), F32),
            pltpu.VMEM((48, half), F32),
            pltpu.VMEM((2, 96, 256), BF16),
            pltpu.VMEM((128, 96), BF16),
        ]
        + chain_scratch(half, width)
        + chain_scratch(half, width)
        + [
            pltpu.SemaphoreType.DMA((6,)),
            pltpu.SemaphoreType.DMA((COPIES,)),
            pltpu.SemaphoreType.DMA((COPIES,)),
        ],
        compiler_params=pltpu.CompilerParams(
            collective_id=0, has_side_effects=True, vmem_limit_bytes=62 * 1024 * 1024
        ),
        cost_estimate=pl.CostEstimate(
            flops=8 * 192 * width * w_in.shape[1], bytes_accessed=4 * w_in.size, transcendentals=0
        ),
    )(tokens, w_in, w_out, grad_out)
    return both[0], both[1]


def solution(mesh):
    placed = (P("col", "row"), P("row", "col"), P("col", "row"), P("col", "row"))
    return jax.shard_map(
        shards,
        mesh=mesh,
        in_specs=placed,
        out_specs=(P("col", "row"), P("col", "row")),
        check_vma=False,
    )
```

```python
import jax
import jax.numpy as jnp
from jax import lax
from jax.experimental import pallas as pl
from jax.experimental.pallas import tpu as pltpu
from jax.sharding import PartitionSpec as P

gelu_scale = 0.7978845608028654
cubic_coef = 0.044715

F32, BF16 = jnp.float32, jnp.bfloat16
MESH = pl.DeviceIdType.MESH
FAR = (6, -6, 2, -2)


def gelu_and_slope(values):
    squared = values * values
    bent = jnp.tanh(gelu_scale * (values + cubic_coef * squared * values))
    act = 0.5 * values * (1.0 + bent)
    slope = 0.5 * (1.0 + bent) + 0.5 * values * (1.0 - bent * bent) * gelu_scale * (
        1.0 + 3.0 * cubic_coef * squared
    )
    return act, slope


def against(left, right):
    return lax.dot_general(left, right, (((1,), (1,)), ((), ())), preferred_element_type=F32)


class Chain:
    def __init__(self, refs):
        (self.x, self.part, self.send1, self.relay, self.near1,
         self.total, self.send2, self.recv2, self.all, self.acc, self.blocks, self.sendz,
         self.nearz, self.nearz2, self.sendf, self.recvf) = refs


def chain_scratch(half, width):
    block = (48, half)
    return [
        pltpu.VMEM((96, width), BF16),
        pltpu.VMEM((4, 4) + block, F32),
        pltpu.VMEM((4, 4) + block, BF16),
        pltpu.VMEM((2, 2) + block, BF16),
        pltpu.VMEM((2, 4) + block, BF16),
        pltpu.VMEM(block, F32),
        pltpu.VMEM((3,) + block, BF16),
        pltpu.VMEM((3,) + block, BF16),
        pltpu.VMEM((4, 4) + block, BF16),
        pltpu.VMEM((128, width), F32),
        pltpu.VMEM((4, 16, half), F32),
        pltpu.VMEM((3, 4, 16, half), BF16),
        pltpu.VMEM((2, 4, 16, half), BF16),
        pltpu.VMEM((4, 16, half), BF16),
        pltpu.VMEM((4, 16, half), BF16),
        pltpu.VMEM((4, 16, half), BF16),
    ]


CHAIN_REFS = 16
COPIES = 96


def kernel(tok_ref, win_ref, wout_ref, gout_ref, out_ref, *scratch):
    win, wout, raw, own, gathered, slope_out, slope_in, picks, expand = scratch[:9]
    h = Chain(scratch[9:9 + CHAIN_REFS])
    g = Chain(scratch[9 + CHAIN_REFS:9 + 2 * CHAIN_REFS])
    local_sem, send_sem, recv_sem = scratch[9 + 2 * CHAIN_REFS:]
    width = tok_ref.shape[1]
    half = width // 2

    row, col = lax.axis_index("row"), lax.axis_index("col")
    y, x = lax.div(row, 4), lax.rem(row, 4)
    z, core = lax.div(col, 2), lax.rem(col, 2)

    a = core * x + (1 - core) * y
    b = core * y + (1 - core) * x

    def at_a(step):
        there = lax.rem(a + step + 4, 4)
        return (core * (y * 4 + there) + (1 - core) * (there * 4 + x), col)

    def at_b(step):
        there = lax.rem(b + step + 4, 4)
        return (core * (there * 4 + x) + (1 - core) * (y * 4 + there), col)

    def at_z(step):
        return (row, lax.rem(z + step + 16, 16) * 2 + core)

    other_core = (row, z * 2 + 1 - core)
    turned = (x * 4 + y, col)
    same = lax.div(3 - lax.max(x - y, y - x), 3)

    moves = [(tok_ref, raw.at[0]), (gout_ref, raw.at[1])]
    for part in range(2):
        cut = pl.ds(part * width, width)
        moves.append((win_ref.at[:, cut], win.at[2 * core + part]))
    for part in range(2):
        cut = pl.ds(part * width, width)
        moves.append((wout_ref.at[cut, :], wout.at[2 * core + part]))
    local = [pltpu.make_async_copy(src, dst, local_sem.at[n]) for n, (src, dst) in enumerate(moves)]
    for copy in local:
        copy.start()

    partners = [at_z(step) for step in (6, -6, 2, -2, 1, -1)]
    partners += [other_core, (x * 4 + y, z * 2 + core + same * (1 - 2 * core))]
    partners += [at_a(step) for step in (2, 1, -1)]
    partners += [at_b(step) for step in (2, 1, -1)]
    barrier = pltpu.get_barrier_semaphore()
    for partner in partners:
        pl.semaphore_signal(barrier, inc=1, device_id=partner, device_id_type=MESH)

    empty = jnp.zeros((2, width), F32)
    for n in range(2):
        local[n].wait()
        whole = jnp.concatenate([raw[n].astype(F32), empty], axis=0)
        folded = jnp.concatenate([whole[:, :half], whole[:, half:]], axis=0)
        own[n] = folded.astype(BF16)

    at = lax.broadcasted_iota(jnp.int32, (96, 256), 0)
    come = lax.broadcasted_iota(jnp.int32, (96, 256), 1)
    for side in range(2):
        within = (come & 15) - 8 * side
        chosen = (within >= 0) & (within < 6) & (at == 6 * (come >> 4) + within)
        picks[side] = jnp.where(chosen, 1.0, 0.0).astype(BF16)
    at = lax.broadcasted_iota(jnp.int32, (128, 96), 0)
    come = lax.broadcasted_iota(jnp.int32, (128, 96), 1)
    within = at & 7
    chosen = (within < 6) & (come == 6 * (at >> 3) + within)
    expand[...] = jnp.where(chosen, 1.0, 0.0).astype(BF16)

    pl.semaphore_wait(barrier, len(partners))

    started = []

    def send(src, dst, device):
        n = len(started)
        copy = pltpu.make_async_remote_copy(
            src_ref=src, dst_ref=dst, send_sem=send_sem.at[n], recv_sem=recv_sem.at[n],
            device_id=device, device_id_type=MESH,
        )
        copy.start()
        started.append(copy)
        return copy

    def arrived(copies):
        for copy in copies:
            copy.wait_recv()

    slot = lax.rem(z, 4) * 4 + lax.div(z, 4)
    held = lax.rem(z + 2, 4) * 4

    def gather_far(n):
        return [send(own.at[n], gathered.at[n, slot], at_z(step)) for step in FAR]

    def gather_near(n):
        out = []
        for step, first, count in ((2, 0, 2), (-2, 2, 2), (1, 0, 4), (-1, 0, 4)):
            piece = gathered.at[n, pl.ds(held + first, count)]
            out.append(send(piece, piece, at_z(step)))
        return out

    far_in = [gather_far(0), gather_far(1)]
    pushed = []
    for part in range(2):
        src = win_ref.at[:, pl.ds(part * width, width)]
        pushed.append(send(src, win.at[2 * core + part], other_core))
    for part in range(2):
        src = wout_ref.at[pl.ds(part * width, width)]
        pushed.append(send(src, wout.at[2 * core + part], other_core))
    near_in = []
    for n in range(2):
        arrived(far_in[n])
        near_in.append(gather_near(n))

    def squeeze(c, n):
        blocks = gathered[n].reshape(256, half)
        for side in range(2):
            got = jnp.dot(picks[side], blocks, preferred_element_type=F32)
            c.x[:, half * side:half * side + half] = got.astype(BF16)

    def quarters(value):
        return [
            value[48 * up:48 * up + 48, half * side:half * side + half]
            for up in range(2) for side in range(2)
        ]

    def relays(c, got, ahead):
        for v in range(4):
            c.send1[2, v] = got[v].astype(BF16)
        return [
            send(c.send1.at[2, pl.ds(0, 2)], c.relay.at[0], ahead(1)),
            send(c.send1.at[2, pl.ds(2, 2)], c.relay.at[1], ahead(-1)),
        ]

    def direct_up(c, got, ahead):
        for v in (2, 3):
            c.send1[1, v] = got[v].astype(BF16)
        out = [send(c.send1.at[1, pl.ds(2, 2)], c.near1.at[0, pl.ds(2, 2)], ahead(1))]
        for v in (0, 1):
            c.part[1, v] = got[v]
        return out

    def direct_down(c, got, ahead):
        for v in (0, 1):
            c.send1[3, v] = got[v].astype(BF16)
        out = [send(c.send1.at[3, pl.ds(0, 2)], c.near1.at[1, pl.ds(0, 2)], ahead(-1))]
        for v in (2, 3):
            c.part[3, v] = got[v]
        return out

    def stay(c, got):
        for v in range(4):
            c.part[0, v] = got[v]

    def passed_on(c, got, ahead):
        arrived(got[:1])
        c.send1[1, 0:2] = (c.part[1, 0:2] + c.relay[0].astype(F32)).astype(BF16)
        out = [send(c.send1.at[1, pl.ds(0, 2)], c.near1.at[0, pl.ds(0, 2)], ahead(1))]
        arrived(got[1:])
        c.send1[3, 2:4] = (c.part[3, 2:4] + c.relay[1].astype(F32)).astype(BF16)
        out.append(send(c.send1.at[3, pl.ds(2, 2)], c.near1.at[1, pl.ds(2, 2)], ahead(-1)))
        return out

    def second_sum(c, got, ahead, place):
        arrived(got)
        out = []
        for n, step in enumerate((2, 1, -1)):
            c.send2[n] = first_sum(c, lax.rem(place + step + 4, 4)).astype(BF16)
            out.append(send(c.send2.at[n], c.recv2.at[n], ahead(step)))
        c.total[...] = first_sum(c, place)
        return out

    def first_sum(c, there):
        return c.part[0, there] + c.near1[0, there].astype(F32) + c.near1[1, there].astype(F32)

    def summed(c, got):
        arrived(got)
        return (
            c.total[...] + c.recv2[0].astype(F32) + c.recv2[1].astype(F32) + c.recv2[2].astype(F32)
        )

    arrived(near_in[0])
    squeeze(h, 0)
    for copy in local[2:4]:
        copy.wait()
    arrived(pushed[:2])

    def hidden_part(rel):
        return quarters(jnp.dot(h.x[...], win[lax.rem(a + rel, 4)], preferred_element_type=F32))

    def grad_part(rel):
        return quarters(against(g.x[...], wout[lax.rem(b + rel, 4)]))

    relay_h = relays(h, hidden_part(2), at_a)
    direct_h = direct_up(h, hidden_part(1), at_a)
    direct_h += direct_down(h, hidden_part(3), at_a)
    stay(h, hidden_part(0))

    arrived(near_in[1])
    squeeze(g, 1)
    for copy in local[4:]:
        copy.wait()
    arrived(pushed[2:])

    relay_g = relays(g, grad_part(2), at_b)
    direct_h += passed_on(h, relay_h, at_a)
    direct_g = direct_up(g, grad_part(1), at_b)
    direct_g += direct_down(g, grad_part(3), at_b)
    stay(g, grad_part(0))
    second_h = second_sum(h, direct_h, at_b, b)
    direct_g += passed_on(g, relay_g, at_b)
    hidden = summed(h, second_h)
    act, slope = gelu_and_slope(hidden)
    h.all[a, b] = act.astype(BF16)

    def spread_first(c, chunk, place, ahead):
        piece = c.all.at[chunk, place]
        return [send(piece, piece, ahead(step)) for step in (2, 1, -1)]

    def spread_second(c, got, chunk, ahead):
        arrived(got)
        low, high = c.all.at[chunk, pl.ds(0, 2)], c.all.at[chunk, pl.ds(2, 2)]
        return [
            send(low, low, ahead(1)),
            send(high, high, ahead(-1)),
            send(high, high, ahead(1)),
            send(low, low, ahead(-1)),
        ]

    def spread_third(c, got, place, ahead):
        arrived(got[:1])
        piece = c.all.at[lax.rem(place + 3, 4), pl.ds(0, 2)]
        out = [send(piece, piece, ahead(1))]
        arrived(got[1:2])
        piece = c.all.at[lax.rem(place + 1, 4), pl.ds(2, 2)]
        out.append(send(piece, piece, ahead(-1)))
        return out

    first_h = spread_first(h, a, b, at_b)
    slope_out[...] = slope
    turn = pltpu.make_async_remote_copy(
        src_ref=slope_out, dst_ref=slope_in, send_sem=send_sem.at[COPIES - 1],
        recv_sem=recv_sem.at[COPIES - 1], device_id=turned, device_id_type=MESH,
    )

    @pl.when(x != y)
    def _():
        turn.start()

    @pl.when(x == y)
    def _():
        slope_in[...] = slope_out[...]

    second_g = second_sum(g, direct_g, at_a, a)
    spread_h = spread_second(h, first_h, a, at_a)
    grad_act = summed(g, second_g)

    @pl.when(x != y)
    def _():
        turn.wait_recv()

    g.all[b, a] = (grad_act * slope_in[...]).astype(BF16)
    first_g = spread_first(g, b, a, at_a)

    def widened(blocks):
        rows = [jnp.concatenate([blocks[2 * up], blocks[2 * up + 1]], axis=1) for up in range(2)]
        return jnp.dot(
            expand[...], jnp.concatenate(rows, axis=0), preferred_element_type=F32
        ).astype(BF16)

    def mixed_part(rel):
        u = lax.rem(a + rel, 4)
        return jnp.dot(widened(h.all[u]), wout[u], preferred_element_type=F32)

    def grad_in_part(rel):
        u = lax.rem(b + rel, 4)
        return against(widened(g.all[u]), win[u])

    h.acc[...] = mixed_part(0)
    spread_h2 = spread_third(h, spread_h, a, at_a)
    spread_g = spread_second(g, first_g, b, at_b)
    g.acc[...] = grad_in_part(0)
    arrived(spread_h[2:])
    h.acc[...] += mixed_part(1)
    h.acc[...] += mixed_part(3)
    spread_g2 = spread_third(g, spread_g, b, at_b)
    arrived(spread_h2)
    h.acc[...] += mixed_part(2)

    def folded_class(c, step):
        first = pl.multiple_of(lax.rem(z + step, 4) * 32, 32)
        acc = c.acc[pl.ds(first, 32), :]
        left = acc[:, :half].reshape(4, 8, half)
        right = acc[:, half:].reshape(4, 8, half)
        return jnp.concatenate([left, right], axis=1)

    def to_near(c):
        c.sendz[0] = folded_class(c, 0).astype(BF16)
        out = [
            send(c.sendz.at[0, pl.ds(0, 2)], c.nearz2.at[pl.ds(0, 2)], at_z(2)),
            send(c.sendz.at[0, pl.ds(2, 2)], c.nearz2.at[pl.ds(2, 2)], at_z(-2)),
        ]
        c.sendz[1] = folded_class(c, 3).astype(BF16)
        out.append(send(c.sendz.at[1], c.nearz.at[0], at_z(1)))
        c.sendz[2] = folded_class(c, 1).astype(BF16)
        out.append(send(c.sendz.at[2], c.nearz.at[1], at_z(-1)))
        c.blocks[...] = folded_class(c, 2)
        return out

    def to_far(c, got):
        arrived(got)
        total = c.blocks[...] + c.nearz[0].astype(F32)
        total = total + c.nearz[1].astype(F32) + c.nearz2[...].astype(F32)
        c.sendf[...] = total.astype(BF16)
        out = []
        for n, step in enumerate(FAR):
            there = lax.div(lax.rem(z + step + 16, 16), 4)
            out.append(send(c.sendf.at[there], c.recvf.at[n], at_z(step)))
        return out

    def finish(c, got, n):
        arrived(got)
        total = c.recvf[0].astype(F32) + c.recvf[1].astype(F32)
        total = total + c.recvf[2].astype(F32) + c.recvf[3].astype(F32)
        whole = jnp.concatenate([total[:8], total[8:]], axis=1)
        out_ref[n] = whole[:6].astype(BF16)

    near_h = to_near(h)
    arrived(spread_g[2:])
    g.acc[...] += grad_in_part(1)
    g.acc[...] += grad_in_part(3)
    arrived(spread_g2)
    g.acc[...] += grad_in_part(2)
    near_g = to_near(g)
    far_h = to_far(h, near_h)
    far_g = to_far(g, near_g)
    late = near_g + far_h + far_g
    for copy in started:
        if not any(copy is other for other in late):
            copy.wait_send()

    @pl.when(x != y)
    def _():
        turn.wait_send()

    finish(h, far_h, 0)
    finish(g, far_g, 1)

    for copy in late:
        copy.wait_send()


def shards(tokens, w_in, w_out, grad_out):
    rows, width = tokens.shape
    half = width // 2
    out = jax.ShapeDtypeStruct((2, rows, width), BF16)
    vmem = pl.BlockSpec(memory_space=pltpu.VMEM)
    hbm = pl.BlockSpec(memory_space=pl.ANY)
    both = pl.pallas_call(
        kernel,
        out_shape=out,
        in_specs=[hbm, hbm, hbm, hbm],
        out_specs=vmem,
        scratch_shapes=[
            pltpu.VMEM((4, width, width), BF16),
            pltpu.VMEM((4, width, width), BF16),
            pltpu.VMEM((2,) + tokens.shape, BF16),
            pltpu.VMEM((2, 16, half), BF16),
            pltpu.VMEM((2, 16, 16, half), BF16),
            pltpu.VMEM((48, half), F32),
            pltpu.VMEM((48, half), F32),
            pltpu.VMEM((2, 96, 256), BF16),
            pltpu.VMEM((128, 96), BF16),
        ]
        + chain_scratch(half, width)
        + chain_scratch(half, width)
        + [
            pltpu.SemaphoreType.DMA((6,)),
            pltpu.SemaphoreType.DMA((COPIES,)),
            pltpu.SemaphoreType.DMA((COPIES,)),
        ],
        compiler_params=pltpu.CompilerParams(
            collective_id=0, has_side_effects=True, vmem_limit_bytes=62 * 1024 * 1024
        ),
        cost_estimate=pl.CostEstimate(
            flops=8 * 192 * width * w_in.shape[1], bytes_accessed=4 * w_in.size, transcendentals=0
        ),
    )(tokens, w_in, w_out, grad_out)
    return both[0], both[1]


def solution(mesh):
    placed = (P("col", "row"), P("row", "col"), P("col", "row"), P("col", "row"))
    return jax.shard_map(
        shards,
        mesh=mesh,
        in_specs=placed,
        out_specs=(P("col", "row"), P("col", "row")),
        check_vma=False,
    )
```

```python
import jax
import jax.numpy as jnp
from jax import lax
from jax.experimental import pallas as pl
from jax.experimental.pallas import tpu as pltpu
from jax.sharding import PartitionSpec as P

gelu_scale = 0.7978845608028654
cubic_coef = 0.044715

F32, BF16 = jnp.float32, jnp.bfloat16
MESH = pl.DeviceIdType.MESH
FAR = (6, -6, 2, -2)


def gelu_and_slope(values):
    squared = values * values
    bent = jnp.tanh(gelu_scale * (values + cubic_coef * squared * values))
    act = 0.5 * values * (1.0 + bent)
    slope = 0.5 * (1.0 + bent) + 0.5 * values * (1.0 - bent * bent) * gelu_scale * (
        1.0 + 3.0 * cubic_coef * squared
    )
    return act, slope


def against(left, right):
    return lax.dot_general(left, right, (((1,), (1,)), ((), ())), preferred_element_type=F32)


class Chain:
    def __init__(self, refs):
        (self.x, self.part, self.send1, self.relay, self.near1,
         self.total, self.send2, self.recv2, self.all, self.acc, self.blocks, self.sendz,
         self.nearz, self.nearz2, self.sendf, self.recvf) = refs


def chain_scratch(half, width):
    block = (48, half)
    return [
        pltpu.VMEM((96, width), BF16),
        pltpu.VMEM((4, 4) + block, F32),
        pltpu.VMEM((4, 4) + block, BF16),
        pltpu.VMEM((2, 2) + block, BF16),
        pltpu.VMEM((2, 4) + block, BF16),
        pltpu.VMEM((4,) + block, F32),
        pltpu.VMEM((4,) + block, BF16),
        pltpu.VMEM((3,) + block, BF16),
        pltpu.VMEM((4, 4) + block, BF16),
        pltpu.VMEM((128, width), F32),
        pltpu.VMEM((16, 16, half), F32),
        pltpu.VMEM((16, 16, half), BF16),
        pltpu.VMEM((2, 4, 16, half), BF16),
        pltpu.VMEM((4, 16, half), BF16),
        pltpu.VMEM((4, 16, half), BF16),
        pltpu.VMEM((4, 16, half), BF16),
    ]


CHAIN_REFS = 16
COPIES = 96


def kernel(tok_ref, win_ref, wout_ref, gout_ref, out_ref, *scratch):
    win, wout, raw, own, gathered, slope_out, slope_in = scratch[:7]
    h = Chain(scratch[7:7 + CHAIN_REFS])
    g = Chain(scratch[7 + CHAIN_REFS:7 + 2 * CHAIN_REFS])
    local_sem, send_sem, recv_sem = scratch[7 + 2 * CHAIN_REFS:]
    width = tok_ref.shape[1]
    half = width // 2

    row, col = lax.axis_index("row"), lax.axis_index("col")
    y, x = lax.div(row, 4), lax.rem(row, 4)
    z, core = lax.div(col, 2), lax.rem(col, 2)

    def at_x(step):
        return (y * 4 + lax.rem(x + step + 4, 4), col)

    def at_y(step):
        return (lax.rem(y + step + 4, 4) * 4 + x, col)

    def at_z(step):
        return (row, lax.rem(z + step + 16, 16) * 2 + core)

    other_core = (row, z * 2 + 1 - core)
    turned = (x * 4 + y, col)
    same = lax.div(3 - lax.max(x - y, y - x), 3)

    moves = [(tok_ref, raw.at[0]), (gout_ref, raw.at[1])]
    for part in range(2):
        cut = pl.ds(part * width, width)
        moves.append((win_ref.at[:, cut], win.at[2 * core + part]))
    for part in range(2):
        cut = pl.ds(part * width, width)
        moves.append((wout_ref.at[cut, :], wout.at[2 * core + part]))
    local = [pltpu.make_async_copy(src, dst, local_sem.at[n]) for n, (src, dst) in enumerate(moves)]
    for copy in local:
        copy.start()

    partners = [at_z(step) for step in (6, -6, 2, -2, 1, -1)]
    partners += [other_core, (x * 4 + y, z * 2 + core + same * (1 - 2 * core))]
    partners += [at_x(step) for step in (2, 1, -1)]
    partners += [at_y(step) for step in (2, 1, -1)]
    barrier = pltpu.get_barrier_semaphore()
    for partner in partners:
        pl.semaphore_signal(barrier, inc=1, device_id=partner, device_id_type=MESH)

    empty = jnp.zeros((2, width), F32)
    for n in range(2):
        local[n].wait()
        whole = jnp.concatenate([raw[n].astype(F32), empty], axis=0)
        folded = jnp.concatenate([whole[:, :half], whole[:, half:]], axis=0)
        own[n] = folded.astype(BF16)

    pl.semaphore_wait(barrier, len(partners))

    started = []

    def send(src, dst, device):
        n = len(started)
        copy = pltpu.make_async_remote_copy(
            src_ref=src, dst_ref=dst, send_sem=send_sem.at[n], recv_sem=recv_sem.at[n],
            device_id=device, device_id_type=MESH,
        )
        copy.start()
        started.append(copy)
        return copy

    def arrived(copies):
        for copy in copies:
            copy.wait_recv()

    slot = lax.rem(z, 4) * 4 + lax.div(z, 4)
    held = lax.rem(z + 2, 4) * 4

    def gather_far(n):
        return [send(own.at[n], gathered.at[n, slot], at_z(step)) for step in FAR]

    def gather_near(n):
        out = []
        for step, first, count in ((2, 0, 2), (-2, 2, 2), (1, 0, 4), (-1, 0, 4)):
            piece = gathered.at[n, pl.ds(held + first, count)]
            out.append(send(piece, piece, at_z(step)))
        return out

    far_in = [gather_far(0), gather_far(1)]
    pushed = []
    for part in range(2):
        src = win_ref.at[:, pl.ds(part * width, width)]
        pushed.append(send(src, win.at[2 * core + part], other_core))
    for part in range(2):
        src = wout_ref.at[pl.ds(part * width, width)]
        pushed.append(send(src, wout.at[2 * core + part], other_core))
    near_in = []
    for n in range(2):
        arrived(far_in[n])
        near_in.append(gather_near(n))

    def squeeze(c, n):
        blocks = gathered[n].astype(F32)
        left = blocks[:, :8, :].reshape(128, half)
        right = blocks[:, 8:, :].reshape(128, half)
        spread = jnp.concatenate([left, right], axis=1).astype(BF16)
        at = lax.broadcasted_iota(jnp.int32, (96, 128), 0)
        come = lax.broadcasted_iota(jnp.int32, (96, 128), 1)
        within = come & 7
        pick = jnp.where((within < 6) & (at == 6 * (come >> 3) + within), 1.0, 0.0).astype(BF16)
        c.x[...] = jnp.dot(pick, spread, preferred_element_type=F32).astype(BF16)

    def expander():
        at = lax.broadcasted_iota(jnp.int32, (128, 96), 0)
        come = lax.broadcasted_iota(jnp.int32, (128, 96), 1)
        within = at & 7
        return jnp.where((within < 6) & (come == 6 * (at >> 3) + within), 1.0, 0.0).astype(BF16)

    def quarters(value):
        return [
            value[48 * up:48 * up + 48, half * side:half * side + half]
            for up in range(2) for side in range(2)
        ]

    def relays(c, got, ahead):
        for v in range(4):
            c.send1[2, v] = got[v].astype(BF16)
        return [
            send(c.send1.at[2, pl.ds(0, 2)], c.relay.at[0], ahead(1)),
            send(c.send1.at[2, pl.ds(2, 2)], c.relay.at[1], ahead(-1)),
        ]

    def direct_up(c, got, ahead):
        for v in (2, 3):
            c.send1[1, v] = got[v].astype(BF16)
        out = [send(c.send1.at[1, pl.ds(2, 2)], c.near1.at[0, pl.ds(2, 2)], ahead(1))]
        for v in (0, 1):
            c.part[1, v] = got[v]
        return out

    def direct_down(c, got, ahead):
        for v in (0, 1):
            c.send1[3, v] = got[v].astype(BF16)
        out = [send(c.send1.at[3, pl.ds(0, 2)], c.near1.at[1, pl.ds(0, 2)], ahead(-1))]
        for v in (2, 3):
            c.part[3, v] = got[v]
        return out

    def stay(c, got):
        for v in range(4):
            c.part[0, v] = got[v]

    def passed_on(c, got, ahead):
        arrived(got[:1])
        c.send1[1, 0:2] = (c.part[1, 0:2] + c.relay[0].astype(F32)).astype(BF16)
        out = [send(c.send1.at[1, pl.ds(0, 2)], c.near1.at[0, pl.ds(0, 2)], ahead(1))]
        arrived(got[1:])
        c.send1[3, 2:4] = (c.part[3, 2:4] + c.relay[1].astype(F32)).astype(BF16)
        out.append(send(c.send1.at[3, pl.ds(2, 2)], c.near1.at[1, pl.ds(2, 2)], ahead(-1)))
        return out

    def second_sum(c, got, ahead, place):
        arrived(got)
        c.total[...] = c.part[0] + c.near1[0].astype(F32) + c.near1[1].astype(F32)
        c.send2[...] = c.total[...].astype(BF16)
        out = []
        for n, step in enumerate((2, 1, -1)):
            there = lax.rem(place + step + 4, 4)
            out.append(send(c.send2.at[there], c.recv2.at[n], ahead(step)))
        return out

    def summed(c, got, place):
        arrived(got)
        return (
            c.total[place] + c.recv2[0].astype(F32) + c.recv2[1].astype(F32) + c.recv2[2].astype(F32)
        )

    arrived(near_in[0])
    squeeze(h, 0)
    for copy in local[2:4]:
        copy.wait()
    arrived(pushed[:2])

    def hidden_part(rel):
        return quarters(jnp.dot(h.x[...], win[lax.rem(x + rel, 4)], preferred_element_type=F32))

    def grad_part(rel):
        return quarters(against(g.x[...], wout[lax.rem(y + rel, 4)]))

    relay_h = relays(h, hidden_part(2), at_x)
    direct_h = direct_up(h, hidden_part(1), at_x)
    direct_h += direct_down(h, hidden_part(3), at_x)
    stay(h, hidden_part(0))

    arrived(near_in[1])
    squeeze(g, 1)
    for copy in local[4:]:
        copy.wait()
    arrived(pushed[2:])

    relay_g = relays(g, grad_part(2), at_y)
    direct_h += passed_on(h, relay_h, at_x)
    direct_g = direct_up(g, grad_part(1), at_y)
    direct_g += direct_down(g, grad_part(3), at_y)
    stay(g, grad_part(0))
    second_h = second_sum(h, direct_h, at_y, y)
    direct_g += passed_on(g, relay_g, at_y)
    hidden = summed(h, second_h, y)
    act, slope = gelu_and_slope(hidden)
    h.all[x, y] = act.astype(BF16)

    def spread_first(c, chunk, place, ahead):
        piece = c.all.at[chunk, place]
        return [send(piece, piece, ahead(step)) for step in (2, 1, -1)]

    def spread_second(c, got, chunk, ahead):
        arrived(got)
        low, high = c.all.at[chunk, pl.ds(0, 2)], c.all.at[chunk, pl.ds(2, 2)]
        return [
            send(low, low, ahead(1)),
            send(high, high, ahead(-1)),
            send(high, high, ahead(1)),
            send(low, low, ahead(-1)),
        ]

    def spread_third(c, got, place, ahead):
        arrived(got[:1])
        piece = c.all.at[lax.rem(place + 3, 4), pl.ds(0, 2)]
        out = [send(piece, piece, ahead(1))]
        arrived(got[1:2])
        piece = c.all.at[lax.rem(place + 1, 4), pl.ds(2, 2)]
        out.append(send(piece, piece, ahead(-1)))
        return out

    first_h = spread_first(h, x, y, at_y)
    slope_out[...] = slope
    turn = pltpu.make_async_remote_copy(
        src_ref=slope_out, dst_ref=slope_in, send_sem=send_sem.at[COPIES - 1],
        recv_sem=recv_sem.at[COPIES - 1], device_id=turned, device_id_type=MESH,
    )

    @pl.when(x != y)
    def _():
        turn.start()

    @pl.when(x == y)
    def _():
        slope_in[...] = slope_out[...]

    second_g = second_sum(g, direct_g, at_x, x)
    spread_h = spread_second(h, first_h, x, at_x)
    grad_act = summed(g, second_g, x)

    @pl.when(x != y)
    def _():
        turn.wait_recv()

    g.all[y, x] = (grad_act * slope_in[...]).astype(BF16)
    first_g = spread_first(g, y, x, at_x)

    expand = expander()

    def widened(blocks):
        rows = [jnp.concatenate([blocks[2 * up], blocks[2 * up + 1]], axis=1) for up in range(2)]
        return jnp.dot(
            expand, jnp.concatenate(rows, axis=0), preferred_element_type=F32
        ).astype(BF16)

    def mixed_part(rel):
        u = lax.rem(x + rel, 4)
        return jnp.dot(widened(h.all[u]), wout[u], preferred_element_type=F32)

    def grad_in_part(rel):
        u = lax.rem(y + rel, 4)
        return against(widened(g.all[u]), win[u])

    h.acc[...] = mixed_part(0)
    spread_h2 = spread_third(h, spread_h, x, at_x)
    spread_g = spread_second(g, first_g, y, at_y)
    g.acc[...] = grad_in_part(0)
    arrived(spread_h[2:])
    h.acc[...] += mixed_part(1)
    h.acc[...] += mixed_part(3)
    arrived(spread_h2)
    h.acc[...] += mixed_part(2)

    def to_near(c):
        acc = c.acc[...]
        left = acc[:, :half].reshape(16, 8, half)
        right = acc[:, half:].reshape(16, 8, half)
        blocks = jnp.concatenate([left, right], axis=1)
        c.blocks[...] = blocks
        c.sendz[...] = blocks.astype(BF16)
        up = c.sendz.at[pl.ds(lax.rem(z + 3, 4) * 4, 4)]
        down = c.sendz.at[pl.ds(lax.rem(z + 1, 4) * 4, 4)]
        here = lax.rem(z, 4) * 4
        return [
            send(c.sendz.at[pl.ds(here, 2)], c.nearz2.at[pl.ds(0, 2)], at_z(2)),
            send(c.sendz.at[pl.ds(here + 2, 2)], c.nearz2.at[pl.ds(2, 2)], at_z(-2)),
            send(up, c.nearz.at[0], at_z(1)),
            send(down, c.nearz.at[1], at_z(-1)),
        ]

    def to_far(c, got):
        arrived(got)
        total = c.blocks[pl.ds(held, 4)] + c.nearz[0].astype(F32)
        total = total + c.nearz[1].astype(F32) + c.nearz2[...].astype(F32)
        c.sendf[...] = total.astype(BF16)
        out = []
        for n, step in enumerate(FAR):
            there = lax.div(lax.rem(z + step + 16, 16), 4)
            out.append(send(c.sendf.at[there], c.recvf.at[n], at_z(step)))
        return out

    def finish(c, got, n):
        arrived(got)
        total = c.recvf[0].astype(F32) + c.recvf[1].astype(F32)
        total = total + c.recvf[2].astype(F32) + c.recvf[3].astype(F32)
        whole = jnp.concatenate([total[:8], total[8:]], axis=1)
        out_ref[n] = whole[:6].astype(BF16)

    near_h = to_near(h)
    spread_g2 = spread_third(g, spread_g, y, at_y)
    arrived(spread_g[2:])
    g.acc[...] += grad_in_part(1)
    g.acc[...] += grad_in_part(3)
    arrived(spread_g2)
    g.acc[...] += grad_in_part(2)
    near_g = to_near(g)
    far_h = to_far(h, near_h)
    far_g = to_far(g, near_g)
    late = near_g + far_h + far_g
    for copy in started:
        if not any(copy is other for other in late):
            copy.wait_send()

    @pl.when(x != y)
    def _():
        turn.wait_send()

    finish(h, far_h, 0)
    finish(g, far_g, 1)

    for copy in late:
        copy.wait_send()


def shards(tokens, w_in, w_out, grad_out):
    rows, width = tokens.shape
    half = width // 2
    out = jax.ShapeDtypeStruct((2, rows, width), BF16)
    vmem = pl.BlockSpec(memory_space=pltpu.VMEM)
    hbm = pl.BlockSpec(memory_space=pl.ANY)
    both = pl.pallas_call(
        kernel,
        out_shape=out,
        in_specs=[hbm, hbm, hbm, hbm],
        out_specs=vmem,
        scratch_shapes=[
            pltpu.VMEM((4, width, width), BF16),
            pltpu.VMEM((4, width, width), BF16),
            pltpu.VMEM((2,) + tokens.shape, BF16),
            pltpu.VMEM((2, 16, half), BF16),
            pltpu.VMEM((2, 16, 16, half), BF16),
            pltpu.VMEM((48, half), F32),
            pltpu.VMEM((48, half), F32),
        ]
        + chain_scratch(half, width)
        + chain_scratch(half, width)
        + [
            pltpu.SemaphoreType.DMA((6,)),
            pltpu.SemaphoreType.DMA((COPIES,)),
            pltpu.SemaphoreType.DMA((COPIES,)),
        ],
        compiler_params=pltpu.CompilerParams(
            collective_id=0, has_side_effects=True, vmem_limit_bytes=62 * 1024 * 1024
        ),
        cost_estimate=pl.CostEstimate(
            flops=8 * 192 * width * w_in.shape[1], bytes_accessed=4 * w_in.size, transcendentals=0
        ),
    )(tokens, w_in, w_out, grad_out)
    return both[0], both[1]


def solution(mesh):
    placed = (P("col", "row"), P("row", "col"), P("col", "row"), P("col", "row"))
    return jax.shard_map(
        shards,
        mesh=mesh,
        in_specs=placed,
        out_specs=(P("col", "row"), P("col", "row")),
        check_vma=False,
    )
```
